32 devices in a mesh: member: 2 (over y), lat: 4 (over z), lon: 2 (over x), lev: 2 (over core).
Axes of the slice: x: 2, y: 2, z: 4, core: 2. Of those that a mesh axis runs over, the one named last changes fastest.
Arguments:
- control: float32 [4, 448, 1024], P('lev', ('member', 'lat'), 'lon'), parts along dimension 1, may hold values from -6 to 6
- vertical: float32 [4, 4], replicated, may hold values from -3 to 3
- spread: float32 [4, 224, 1024], P('lev', 'lat', 'lon'), may hold values from 0.4 to 1
- error_scale: float32 [4, 224, 1024], P('lev', 'lat', 'lon'), may hold values from 0.3 to 6
- wind_lon: float32 [4, 448, 1024], P('lev', ('member', 'lat'), 'lon'), parts along dimension 1, may hold values from -0.6 to 0.6
- wind_lat: float32 [4, 448, 1024], P('lev', ('member', 'lat'), 'lon'), parts along dimension 1, may hold values from -0.6 to 0.6
- obs_block: int32 [2, 4, 2, 8, 2], P('lev', 'lat', 'lon'), may hold values from 0 to 447
- obs_platform: int32 [2, 4, 2, 8, 2], P('lev', 'lat', 'lon'), may hold values from 0 to 7
- obs_count: int32 [2, 4, 2, 8], P('lev', 'lat', 'lon'), may hold values from 1 to 2, as said below
- interp: float32 [2, 4, 2, 8, 2, 128, 128], P('lev', 'lat', 'lon'), may hold values from -0.5 to 0.5
- innovation: float32 [2, 8, 2, 8, 2, 128], P('lev', ('member', 'lat'), 'lon'), parts along dimension 1, may hold values from -6 to 6
- error_inverse: float32 [4, 2, 8, 128, 128], P('lat', 'lon'), may hold values from -0.8 to 4.8
- previous_direction: float32 [4, 448, 1024], P('lev', ('member', 'lat'), 'lon'), parts along dimension 1, may hold values from -6 to 6
- previous_square: float32 [2], P('member'), parts along dimension 0, may hold values from 0.5 to 2
Outputs:
- gradient: float32 [4, 448, 1024], P('lev', ('member', 'lat'), 'lon'), parts along dimension 1
- direction: float32 [4, 448, 1024], P('lev', ('member', 'lat'), 'lon'), parts along dimension 1
The draws below stay inside these ranges and needn't reach their ends.
There are 2 independent parts, one for each index of `member`. The reference program is written for one: setup_inputs(seed, part) draws one part's arguments, and reference() takes and returns one part's arrays. A program takes and returns all parts, laid end to end along the dimension named above; an argument that names none is the same for every part. Nothing has to cross between parts.
Inputs may be any that keep to these rules, and one draw needn't show every extreme that they name: The first obs_count slots toward an owner are used; at most 2 go from one tile to one owner.
All inputs are finite; a program needn't handle non-finite values.
Results may differ from the reference program's by a relative error of at most 0.00013.
Values sent between devices are 32-bit elements; how exact they have to be, the bound alone decides.
No kernel may reach another device: no remote copies, remote signals or barrier semaphores. Data moves between devices by JAX's collectives and lax.ppermute only.
A program may use at most 64 MiB of HBM per device.

```python
import math
import jax
import jax.numpy as jnp
from jax import lax

LEV_DEV = 2
CLAT = 56
CLON = 512
FILTER = 2
OBS_W = 128
SLOTS = 2
PLAT_DEV = 8
LEV = 4
NLAT = 224
NLON = 1024
OWNERS = 8
NBLK = 448
N_LAT = 4
N_LON = 2
N_LEV = 2


def draw_error_scale(key, part):
    key = jax.random.fold_in(key, 11)
    array_shape = (LEV, NLAT, NLON)
    roughness = jnp.exp(jax.random.uniform(key, array_shape, jnp.float32, math.log(0.5), math.log(1.5)))
    trend = 3.0 ** (jnp.arange(NLAT, dtype=jnp.float32) / max(NLAT - 1, 1))
    return roughness * trend[None, :, None]


def draw_obs_count(key, part):
    key = jax.random.fold_in(key, 12)
    counts = jax.random.randint(key, (N_LEV, N_LAT, N_LON, OWNERS), 1, SLOTS + 1, dtype=jnp.int32)
    full_owner = jax.random.randint(jax.random.fold_in(key, 1), (), 0, OWNERS, dtype=jnp.int32)
    return jnp.where(jnp.arange(OWNERS, dtype=jnp.int32) == full_owner, jnp.int32(SLOTS), counts)


def draw_error_inverse(key, part):
    key = jax.random.fold_in(key, 13)
    key_noise, key_scale = jax.random.split(key)
    array_shape = (N_LAT, N_LON, PLAT_DEV, OBS_W, OBS_W)
    gaussian = jax.random.normal(key_noise, array_shape, jnp.float32)
    symmetric = jnp.clip((gaussian + jnp.swapaxes(gaussian, -1, -2)) * (0.4 / math.sqrt(2.0 * OBS_W)), -0.2, 0.2)
    lower, upper = (0.5, 2.0)
    precision_scale = jnp.exp(jax.random.uniform(key_scale, (N_LAT, N_LON, PLAT_DEV, 1, 1), jnp.float32, math.log(lower), math.log(upper)))
    identity = jnp.eye(OBS_W, dtype=jnp.float32)
    return precision_scale * (identity + symmetric)


def place_ends(drawn, stream_key, smallest, largest):
    spot = [jax.random.randint(jax.random.fold_in(stream_key, axis), (), 0, length) for axis, length in enumerate(drawn.shape)]
    widest = drawn.shape.index(max(drawn.shape))
    neighbour = spot[:widest] + [(spot[widest] + 1) % drawn.shape[widest]] + spot[widest + 1:]
    return drawn.at[tuple(spot)].set(smallest).at[tuple(neighbour)].set(largest)


def steps_of(stream_key, extent, cuts, smallest, high):
    gain = 1.0
    for dim, parts in cuts:
        draws = jax.random.uniform(jax.random.fold_in(jax.random.fold_in(stream_key, 6), dim), (parts,), jnp.float32, smallest / len(cuts), high / len(cuts))
        gain = gain * jnp.repeat(jnp.exp(draws), extent[dim] // parts).reshape((-1,) + (1,) * (len(extent) - 1 - dim))
    return gain


def bell_draw(own_key, dims, deviation, limit, cuts=(), kind=jnp.bfloat16):
    array = deviation * jax.random.normal(own_key, dims, jnp.float32)
    if cuts:
        array = array * steps_of(own_key, dims, cuts, -0.22, 0.18)
    return jnp.clip(array, -limit, limit).astype(kind)


def setup_inputs(seed: int = 0, part: int = 0) -> dict:
    keys = jax.random.split(jax.random.key(seed), 15)
    own_keys = jax.random.split(jax.random.fold_in(keys[14], part), 15)
    control = bell_draw(own_keys[0], (LEV, NLAT, NLON), 1.0, 6.0, ((0, 2), (1, 4), (2, 2)), jnp.float32)
    vertical = bell_draw(keys[1], (LEV, LEV), LEV ** -0.5, 3.0, (), jnp.float32)
    spread = jnp.clip(jnp.exp(math.log(1.0) - 0.9162907 * jax.random.uniform(keys[2], (LEV, NLAT, NLON), jnp.float32) ** steps_of(keys[2], (LEV, NLAT, NLON), ((0, 2), (1, 4), (2, 2)), -0.2, 0.2)), 0.4, 1.0)
    error_scale = draw_error_scale(jax.random.fold_in(keys[14], 71), part)
    wind_lon = jnp.clip(jax.random.uniform(own_keys[4], (LEV, NLAT, NLON), jnp.float32, -0.6, 0.6) * steps_of(own_keys[4], (LEV, NLAT, NLON), ((0, 2), (1, 4), (2, 2)), -0.4, 0.0), -0.6, 0.6)
    wind_lat = jnp.clip(jax.random.uniform(own_keys[5], (LEV, NLAT, NLON), jnp.float32, -0.6, 0.6) * steps_of(own_keys[5], (LEV, NLAT, NLON), ((0, 2), (1, 4), (2, 2)), -0.4, 0.0), -0.6, 0.6)
    obs_block = place_ends(jax.random.randint(keys[6], (N_LEV, N_LAT, N_LON, OWNERS, SLOTS), 0, NBLK), jax.random.fold_in(keys[6], 1), 0, NBLK - 1).astype(jnp.int32)
    obs_platform = place_ends(jax.random.randint(keys[7], (N_LEV, N_LAT, N_LON, OWNERS, SLOTS), 0, PLAT_DEV), jax.random.fold_in(keys[7], 1), 0, PLAT_DEV - 1).astype(jnp.int32)
    obs_count = draw_obs_count(jax.random.fold_in(keys[14], 71), part)
    interp = bell_draw(keys[9], (N_LEV, N_LAT, N_LON, OWNERS, SLOTS, OBS_W, OBS_W), OBS_W ** -0.5, 0.5, ((0, 2), (1, 4), (2, 2)), jnp.float32)
    innovation = bell_draw(own_keys[10], (N_LEV, N_LAT, N_LON, OWNERS, SLOTS, OBS_W), 1.0, 6.0, ((0, 2), (1, 4), (2, 2)), jnp.float32)
    error_inverse = draw_error_inverse(jax.random.fold_in(keys[14], 71), part)
    previous_direction = bell_draw(own_keys[12], (LEV, NLAT, NLON), 1.0, 6.0, ((0, 2), (1, 4), (2, 2)), jnp.float32)
    previous_square = jnp.clip(jnp.exp(jax.random.uniform(own_keys[13], (1,), jnp.float32, math.log(0.5), math.log(2.0))), 0.5, 2.0)
    return dict(control=control, vertical=vertical, spread=spread, error_scale=error_scale, wind_lon=wind_lon, wind_lat=wind_lat, obs_block=obs_block, obs_platform=obs_platform, obs_count=obs_count, interp=interp, innovation=innovation, error_inverse=error_inverse, previous_direction=previous_direction, previous_square=previous_square)


highest = lax.Precision.HIGHEST
smoothing = 0.1
diffusion = 0.15


def neighbours(field):
    padded = jnp.pad(field, ((0, 0), (1, 1), (0, 0)))
    to_north = padded[:, 2:, :]
    to_south = padded[:, :-2, :]
    to_east = jnp.roll(field, -1, axis=2)
    to_west = jnp.roll(field, 1, axis=2)
    return to_north, to_south, to_east, to_west


def laplace(field):
    to_north, to_south, to_east, to_west = neighbours(field)
    return to_north + to_south + to_east + to_west - 4.0 * field


def smooth(field, spread):
    for repeat in range(FILTER):
        field = field + smoothing * spread * laplace(spread * field)
    return field


def advance(field, wind_lon, wind_lat):
    to_north, to_south, to_east, to_west = neighbours(field)
    return field - 0.5 * wind_lon * (to_east - to_west) - 0.5 * wind_lat * (to_north - to_south) + diffusion * laplace(field)


def retreat(field, wind_lon, wind_lat):
    east_flux = neighbours(wind_lon * field)
    north_flux = neighbours(wind_lat * field)
    return field + 0.5 * (east_flux[2] - east_flux[3]) + 0.5 * (north_flux[0] - north_flux[1]) + diffusion * laplace(field)


def to_tiles(field):
    shaped = field.reshape(N_LEV, LEV_DEV, N_LAT, CLAT, N_LON, CLON).transpose(0, 2, 4, 1, 3, 5)
    return shaped.reshape(N_LEV, N_LAT, N_LON, NBLK, OBS_W)


def from_tiles(tile_rows):
    shaped = tile_rows.reshape(N_LEV, N_LAT, N_LON, LEV_DEV, CLAT, CLON).transpose(0, 3, 1, 4, 2, 5)
    return shaped.reshape(LEV, NLAT, NLON)


def reference(control, vertical, spread, error_scale, wind_lon, wind_lat, obs_block, obs_platform, obs_count, interp, innovation, error_inverse, previous_direction, previous_square):
    blended = jnp.einsum("lm,mij->lij", vertical, control, precision=highest)
    field_now = error_scale * smooth(blended, spread)
    for repeat in range(2):
        field_now = advance(field_now, wind_lon, wind_lat)
    tile_rows = to_tiles(field_now)
    block_index = obs_block.reshape(N_LEV, N_LAT, N_LON, OWNERS * SLOTS)
    cell_rows = jnp.take_along_axis(tile_rows, block_index[..., None], axis=3)
    cell_rows = cell_rows.reshape(N_LEV, N_LAT, N_LON, OWNERS, SLOTS, OBS_W)
    evolved = jnp.einsum("dabosij,dabosj->dabosi", interp, cell_rows, precision=highest)
    is_live = jnp.arange(SLOTS, dtype=jnp.int32) < obs_count[..., None]
    departure = jnp.where(is_live[..., None], evolved - innovation, jnp.float32(0.0))
    matrices = error_inverse.reshape(OWNERS, PLAT_DEV, OBS_W, OBS_W)
    products = jnp.einsum("opij,dabosj->pdabosi", matrices, departure, precision=highest)
    selector = (obs_platform[None] == jnp.arange(PLAT_DEV, dtype=jnp.int32)[:, None, None, None, None, None]).astype(jnp.float32)
    weighted = jnp.sum(selector[..., None] * products, axis=0)
    adjoint_obs = jnp.einsum("dabosij,dabosi->dabosj", interp, weighted, precision=highest)
    devices = N_LEV * N_LAT * N_LON
    flat_index = (jnp.arange(devices, dtype=jnp.int32)[:, None] * NBLK + block_index.reshape(devices, OWNERS * SLOTS)).reshape(-1)
    forcing = jnp.zeros((devices * NBLK, OBS_W), jnp.float32).at[flat_index].add(adjoint_obs.reshape(-1, OBS_W))
    adjoint = from_tiles(forcing.reshape(N_LEV, N_LAT, N_LON, NBLK, OBS_W))
    for repeat in range(2):
        adjoint = retreat(adjoint, wind_lon, wind_lat)
    filtered = smooth(error_scale * adjoint, spread)
    gradient = control + jnp.einsum("lm,lij->mij", vertical, filtered, precision=highest)
    square = jnp.sum(gradient * gradient) / (LEV * NLAT * NLON)
    direction = -gradient + (square / previous_square[0]) * previous_direction
    return gradient, direction
```

```python
import functools
import jax
import jax.numpy as jnp
from jax import lax
from jax.experimental import pallas as pl
from jax.experimental.pallas import tpu as pltpu
from jax.sharding import PartitionSpec as P

FILTER = 2
STEPS = 2
HALO = 4
WIDTHS = (4, 4, 4, 4, 2)
LANES = 128
smoothing = 0.1
diffusion = 0.15
f32 = jnp.float32
bf16 = jnp.bfloat16
VMEM = pl.BlockSpec(memory_space=pltpu.VMEM)
SMEM = pl.BlockSpec(memory_space=pltpu.SMEM)
NT = (((1,), (1,)), ((), ()))
NN = (((1,), (0,)), ((), ()))


def call(kernel, out_shape, in_specs, scratch=(), limit=16 << 20, flops=1 << 20):
    many = isinstance(out_shape, (list, tuple))
    return pl.pallas_call(
        kernel,
        out_shape=out_shape,
        in_specs=in_specs,
        out_specs=[VMEM] * len(out_shape) if many else VMEM,
        scratch_shapes=list(scratch),
        compiler_params=pltpu.CompilerParams(vmem_limit_bytes=limit),
        cost_estimate=pl.CostEstimate(flops=flops, bytes_accessed=1 << 20, transcendentals=0),
    )


def shape(*dims):
    return jax.ShapeDtypeStruct(dims, f32)


def split(value):
    high = value.astype(bf16)
    return high, (value - high.astype(f32)).astype(bf16)


def dot(left, right, dims):
    lh, ll = split(left)
    rh, rl = split(right)
    part = lambda a, b: lax.dot_general(a, b, dims, preferred_element_type=f32)
    return part(lh, rh) + (part(ll, rh) + part(lh, rl))


def for_each(count, body, start):
    if count <= 32:
        for i in range(count):
            start = body(i, start)
        return start
    return lax.fori_loop(0, count, body, start)


def north(x):
    return pltpu.roll(x, x.shape[0] - 1, 0)


def south(x):
    return pltpu.roll(x, 1, 0)


def east(x):
    return pltpu.roll(x, x.shape[1] - 1, 1)


def west(x):
    return pltpu.roll(x, 1, 1)


def smooth(s, spread):
    for repeat in range(FILTER):
        q = spread * s
        s = s + smoothing * spread * (north(q) + south(q) + east(q) + west(q) - 4.0 * q)
    return s


def edge_block(rows):
    lane = lax.broadcasted_iota(jnp.int32, (rows.shape[0], LANES), 1)
    return jnp.where(lane < LANES // 2, rows[:, :LANES], rows[:, rows.shape[1] - LANES :])


def blend(flags, vertical, control, others, layer, transposed):
    layers = control.shape[0]
    levs = 1 + len(others)
    total = None
    for shift, source in enumerate([control] + list(others)):
        lev = lax.rem(flags[3] + levs - shift, levs)
        for m in range(layers):
            a, b = flags[3] * layers + layer, lev * layers + m
            weight = vertical[b, a] if transposed else vertical[a, b]
            term = weight * source[m]
            total = term if total is None else total + term
    return total


def pack_kernel(n_other, *refs):
    flags, vertical, control = refs[:3]
    others = refs[3 : 3 + n_other]
    spread, scale, wind_e, wind_n, blocks = refs[3 + n_other : 8 + n_other]
    blended, lon_out, lat_1, lat_2, diag_1, diag_2, first, last = refs[8 + n_other :]
    layers, rows, cols = control.shape
    for l in range(layers):
        blended[l] = blend(flags, vertical, control, others, l, False)
    fields = (blended, spread, wind_e, wind_n, scale)
    lane = lax.broadcasted_iota(jnp.int32, (rows, LANES), 1)
    packed = jnp.zeros((rows, LANES), f32)
    item = 0
    for field in fields:
        for l in range(layers):
            tile = jnp.where(lane < LANES // 2, field[l, :, :LANES], field[l, :, cols - LANES :])
            if item:
                tile = pltpu.roll(tile, 8 * item, 1)
            packed = jnp.where((lane + HALO - 8 * item) % LANES < 8, tile, packed)
            item += 1
    lon_out[:rows, :] = packed
    lon_out[rows:, :] = jnp.zeros((lon_out.shape[0] - rows, LANES), f32)
    lon_out[rows : rows + blocks.shape[0], :] = blocks[...]
    for out, low in ((first, True), (last, False)):
        at = 0
        for field, width in zip(fields, WIDTHS):
            for l in range(layers):
                begin = 0 if low else rows - width
                out[at : at + width, :] = field[l, begin : begin + width, :]
                at += width
        out[at:, :] = jnp.zeros((out.shape[0] - at, cols), f32)
        out[at : at + blocks.shape[0], :LANES] = blocks[...]
        out[at : at + blocks.shape[0], cols - LANES :] = blocks[...]
    a, b = first[...], last[...]
    even = jnp.full(a.shape, flags[0], jnp.int32) == 0
    one = jnp.where(even, b, a)
    two = jnp.where(even, a, b)
    lat_1[...] = one
    lat_2[...] = two
    diag_1[...] = edge_block(one)
    diag_2[...] = edge_block(two)


def unpack(flags, own, lon_in, lat_1, lat_2, diag_1, diag_2, ext):
    layers, rows, cols = own[0].shape
    lane = lax.broadcasted_iota(jnp.int32, (rows, LANES), 1)
    keep = (lane < HALO) | (lane >= LANES - HALO)
    packed = lon_in[:rows, :]
    item = 0
    for field, out in zip(own, ext):
        for l in range(layers):
            out[l, :rows, :cols] = field[l]
            tile = pltpu.roll(packed, LANES - 8 * item, 1) if item else packed
            out[l, :rows, cols:] = jnp.where(keep, tile, 0.0)
            item += 1
    count = sum(WIDTHS) * layers
    for one, two, begin in ((lat_1, lat_2, 0), (diag_1, diag_2, cols)):
        width = one.shape[1]
        a, b = one[:count, :], two[:count, :]
        even = jnp.full(a.shape, flags[0], jnp.int32) == 0
        top = jnp.full(a.shape, flags[2], jnp.int32) == 0
        bottom = jnp.full(a.shape, flags[1], jnp.int32) == 0
        if begin:
            lane_d = lax.broadcasted_iota(jnp.int32, a.shape, 1)
            inside = (lane_d < HALO) | (lane_d >= LANES - HALO)
            top = top & inside
            bottom = bottom & inside
        from_north = jnp.where(top, jnp.where(even, a, b), 0.0)
        from_south = jnp.where(bottom, jnp.where(even, b, a), 0.0)
        at = 0
        for out, l, w in [(e, l, w) for e, w in zip(ext, WIDTHS) for l in range(layers)]:
            if w < HALO:
                out[l, rows : rows + 8, begin : begin + width] = jnp.zeros((8, width), f32)
            out[l, rows : rows + w, begin : begin + width] = from_north[at : at + w, :]
            out[l, rows + 8 - w : rows + 8, begin : begin + width] = from_south[at : at + w, :]
            at += w


def inside_mask(flags, ext_shape):
    row = lax.broadcasted_iota(jnp.int32, ext_shape, 0)
    rows = ext_shape[0] - 8
    north_cut = jnp.where(flags[2] != 0, rows, rows + 8)
    south_cut = jnp.where(flags[1] != 0, rows + 4, rows + 8)
    cut = ((row >= north_cut) & (row < rows + 4)) | (row >= south_cut)
    return jnp.where(cut, 0.0, 1.0).astype(f32)


def forward_kernel(*refs):
    flags, at = refs[:2]
    own = refs[2:7]
    lon_in, lat_1, lat_2, diag_1, diag_2, interp, innovation, live, platform = refs[7:16]
    sent, spread, scale, wind_e, wind_n, mixed, field = refs[16:]
    ext = (mixed, spread, wind_e, wind_n, scale)
    unpack(flags, own, lon_in, lat_1, lat_2, diag_1, diag_2, ext)
    layers, ext_rows, ext_cols = mixed.shape
    mask = inside_mask(flags, (ext_rows, ext_cols))
    for l in range(layers):
        x = scale[l] * smooth(mixed[l], spread[l])
        u, v = 0.5 * wind_e[l], 0.5 * wind_n[l]
        for step in range(STEPS):
            if step:
                x = x * mask
            x = (
                (1.0 - 4.0 * diffusion) * x
                + (diffusion - u) * east(x)
                + (diffusion + u) * west(x)
                + (diffusion - v) * north(x)
                + (diffusion + v) * south(x)
            )
        per = ext_cols // LANES - 1
        for c in range(per):
            begin = (l * per + c) * ext_rows
            field[begin : begin + ext_rows, :] = x[:, c * LANES : (c + 1) * LANES]
    count, width = innovation.shape
    row = lax.broadcasted_iota(jnp.int32, (count, width), 0)

    def body(b, total):
        cells = field[pl.ds(at[b], 1), :]
        left = jnp.where(row == b, jnp.broadcast_to(cells, (count, width)), 0.0)
        return total + dot(left, interp[b], NT)

    evolved = for_each(count, body, jnp.zeros((count, width), f32))
    departure = jnp.where(live[...] > 0.5, evolved - innovation[...], 0.0)
    owners, height = sent.shape[:2]
    slots = count // owners
    half = height // 2
    sent[...] = platform[...]
    for o in range(owners):
        sent[o, :slots, :] = departure[o * slots : (o + 1) * slots, :]


def weigh_kernel(arrived, matrices, out):
    tiles, height, width = arrived.shape
    rows = arrived[...].reshape(tiles * height, width)
    platform = pltpu.roll(rows, rows.shape[0] - height // 2, 0)
    total = jnp.zeros(rows.shape, f32)
    for p in range(matrices.shape[0]):
        left = jnp.where(platform == float(p), rows, 0.0)
        total = total + dot(left, matrices[p], NT)
    out[...] = total.reshape(tiles, height, width)


def transpose_kernel(slots, returned, interp, out):
    count, width = out.shape
    row = lax.broadcasted_iota(jnp.int32, (count, width), 0)

    def body(b, total):
        weighted = returned[b // slots, pl.ds(b % slots, 1), :]
        left = jnp.where(row == b, jnp.broadcast_to(weighted, (count, width)), 0.0)
        return total + dot(left, interp[b], NN)

    out[...] = for_each(count, body, jnp.zeros((count, width), f32))


def adjoint_kernel(n_source, *refs):
    flags, target, lane_mask = refs[:3]
    sources = refs[3 : 3 + n_source]
    spread, scale, wind_e, wind_n = refs[3 + n_source : 7 + n_source]
    filtered, = refs[7 + n_source :]
    layers, ext_rows, ext_cols = spread.shape
    rows, cols = filtered.shape[1:]
    values = jnp.concatenate([s[...] for s in sources], axis=0) * lane_mask[...]
    high, low = split(values)
    places = layers * ext_rows * (ext_cols // LANES)
    place = lax.broadcasted_iota(jnp.int32, (places, values.shape[0]), 0)
    chosen = jnp.where(place == target[...], 1.0, 0.0).astype(bf16)
    forcing = lax.dot_general(chosen, high, NN, preferred_element_type=f32)
    forcing = forcing + lax.dot_general(chosen, low, NN, preferred_element_type=f32)
    mask = inside_mask(flags, (ext_rows, ext_cols))
    per = ext_cols // LANES
    for l in range(layers):
        y = jnp.concatenate(
            [forcing[(l * per + c) * ext_rows : (l * per + c + 1) * ext_rows, :] for c in range(per)], axis=1
        )
        u, v = 0.5 * wind_e[l], 0.5 * wind_n[l]
        for step in range(STEPS):
            if step:
                y = y * mask
            y = (
                (1.0 - 4.0 * diffusion) * y
                + east((diffusion + u) * y)
                + west((diffusion - u) * y)
                + north((diffusion + v) * y)
                + south((diffusion - v) * y)
            )
        s = smooth(scale[l] * y, spread[l])
        filtered[l] = s[:rows, :cols]


def gradient_kernel(n_other, *refs):
    flags, vertical, control, filtered = refs[:4]
    others = refs[4 : 4 + n_other]
    gradient, partial = refs[4 + n_other :]
    layers, rows, cols = control.shape
    total = jnp.zeros((8, LANES), f32)
    for m in range(layers):
        g = control[m] + blend(flags, vertical, filtered, others, m, True)
        gradient[m] = g
        square = g * g
        for r in range(0, rows, 8):
            for c in range(0, cols, LANES):
                total = total + square[r : r + 8, c : c + LANES]
    total = jnp.sum(total, axis=0, keepdims=True)
    partial[...] = jnp.broadcast_to(total[None], partial.shape)


def direction_kernel(cell_count, gradient, sums, previous, previous_square, direction):
    square = jnp.sum(sums[...]) / cell_count
    factor = square / previous_square[0]
    direction[...] = factor * previous[...] - gradient[...]


def local(
    control,
    vertical,
    spread,
    error_scale,
    wind_lon,
    wind_lat,
    obs_block,
    obs_platform,
    obs_count,
    interp,
    innovation,
    error_inverse,
    previous_direction,
    previous_square,
):
    n_lat, n_lon, n_lev = (lax.axis_size(a) for a in ("lat", "lon", "lev"))
    lat, lev = lax.axis_index("lat"), lax.axis_index("lev")
    layers, rows, cols = control.shape
    ext_rows, ext_cols = rows + 8, cols + LANES
    owners = obs_count.shape[-1]
    slots = obs_block.shape[-1]
    width = interp.shape[-1]
    count = owners * slots
    blocks = obs_block.reshape(count)
    weights = interp.reshape(count, width, width)
    flags = jnp.stack([lat % 2, lat == 0, lat == n_lat - 1, lev]).astype(jnp.int32)
    limit = (16 << 20) + 3 * weights.size * 4

    def from_levs(field):
        return [
            lax.ppermute(field, "lev", [(i, (i + k) % n_lev) for i in range(n_lev)]) for k in range(1, n_lev)
        ]

    def partner(a, phase):
        step = 1 if (a % 2 == 0) == (phase == 1) else -1
        return (a + step) % n_lat

    def exchange(field, phase, lon_step):
        pairs = []
        for a in range(n_lat):
            for b in range(n_lon):
                to = partner(a, phase) if phase else a
                pairs.append((a * n_lon + b, to * n_lon + (b + lon_step) % n_lon))
        return lax.ppermute(field, ("lat", "lon"), pairs)

    lon_steps = (1,) if n_lon == 2 else (1, -1)

    def from_sides(field, phase, first_lanes):
        if n_lon == 2:
            return exchange(field, phase, 1)
        return jnp.where(first_lanes, exchange(field, phase, -1), exchange(field, phase, 1))

    block_rows = -(-count // LANES)
    lat_fields = sum(WIDTHS) * layers
    lat_rows = -(-(lat_fields + block_rows) // 8) * 8
    lon_rows = rows + -(-block_rows // 8) * 8
    block_tile = jnp.zeros((block_rows * LANES,), f32).at[:count].set(blocks.astype(f32))
    block_tile = block_tile.reshape(block_rows, LANES)

    others = from_levs(control)
    blended, lon_out, lat_1, lat_2, diag_1, diag_2 = call(
        functools.partial(pack_kernel, len(others)),
        [
            shape(layers, rows, cols),
            shape(lon_rows, LANES),
            shape(lat_rows, cols),
            shape(lat_rows, cols),
            shape(lat_rows, LANES),
            shape(lat_rows, LANES),
        ],
        [SMEM, SMEM] + [VMEM] * (6 + len(others)),
        [pltpu.VMEM((lat_rows, cols), f32)] * 2,
    )(flags, vertical, control, *others, spread, error_scale, wind_lon, wind_lat, block_tile)

    lane = jnp.arange(LANES, dtype=jnp.int32)
    lat_in = {phase: exchange(phase_out, phase, 0) for phase, phase_out in ((1, lat_1), (2, lat_2))}
    lon_raw = {step: exchange(lon_out, 0, -step) for step in lon_steps}
    diag_raw = {
        (phase, step): exchange(phase_out, phase, -step)
        for phase, phase_out in ((1, diag_1), (2, diag_2))
        for step in lon_steps
    }
    if n_lon == 2:
        lon_in = lon_raw[1]
        diag_in = {phase: diag_raw[phase, 1] for phase in (1, 2)}
    else:
        lon_in = jnp.where(lane % 8 < HALO, lon_raw[1], lon_raw[-1])
        diag_in = {
            phase: jnp.where(lane < LANES // 2, diag_raw[phase, 1], diag_raw[phase, -1]) for phase in (1, 2)
        }

    per = cols // LANES
    at = (blocks // (rows * per) * per + blocks % per) * ext_rows + (blocks // per) % rows
    live = jnp.arange(slots, dtype=jnp.int32)[None, :] < obs_count.reshape(owners)[:, None]
    live = jnp.broadcast_to(live.reshape(count, 1), (count, width)).astype(f32)
    half = -(-slots // 4) * 4
    platform = jnp.zeros((owners, 2 * half, width), f32)
    platform = platform.at[:, half : half + slots, :].set(
        jnp.broadcast_to(obs_platform.reshape(owners, slots, 1).astype(f32), (owners, slots, width))
    )
    ext = shape(layers, ext_rows, ext_cols)
    sent, ext_spread, ext_scale, ext_e, ext_n = call(
        forward_kernel,
        [shape(owners, 2 * half, width), ext, ext, ext, ext],
        [SMEM] * 2 + [VMEM] * 14,
        [pltpu.VMEM((layers, ext_rows, ext_cols), f32), pltpu.VMEM((layers * ext_rows * per, LANES), f32)],
        limit,
    )(
        flags, at, blended, spread, wind_lon, wind_lat, error_scale,
        lon_in, lat_in[1], lat_in[2], diag_in[1], diag_in[2],
        weights, innovation.reshape(count, width), live, platform,
    )

    arrived = lax.all_to_all(sent, ("lat", "lon"), split_axis=0, concat_axis=0, tiled=True)
    matrices = error_inverse.reshape(error_inverse.shape[-3:])
    result = call(weigh_kernel, shape(owners, 2 * half, width), [VMEM] * 2)(arrived, matrices)
    returned = lax.all_to_all(result, ("lat", "lon"), split_axis=0, concat_axis=0, tiled=True)
    adjoint_obs = call(
        functools.partial(transpose_kernel, slots), shape(count, width), [VMEM] * 2, (), limit
    )(returned, weights)

    odd = lat % 2
    wide = lane[None, :] < LANES // 2
    sources, targets, masks = [], [], []

    def numbers(tile, begin):
        return tile[begin : begin + block_rows, :LANES].reshape(-1)[:count].astype(jnp.int32)

    def add_source(values, block, is_north, is_south, lon_step):
        block_layer, row, block_col = block // (rows * per), (block // per) % rows, block % per
        place_row = jnp.where(is_north, rows + row, jnp.where(is_south, row + 8, row))
        valid = jnp.where(is_north, row < HALO, jnp.where(is_south, row >= rows - HALO, True))
        valid = valid & ~(is_north & (lat == n_lat - 1)) & ~(is_south & (lat == 0))
        keep = jnp.ones((count, LANES), f32)
        if lon_step:
            at_first, at_last = block_col == 0, block_col == per - 1
            if n_lon > 2:
                at_first, at_last = at_first & (lon_step == 1), at_last & (lon_step == -1)
            valid = valid & (at_first | at_last)
            keep = jnp.where(at_first[:, None], wide, ~wide).astype(f32)
            block_col = jnp.full_like(block_col, per)
        place = (block_layer * (per + 1) + block_col) * ext_rows + place_row
        sources.append(values)
        targets.append(jnp.where(valid, place, -1))
        masks.append(keep)

    no = jnp.zeros((), bool)
    add_source(adjoint_obs, blocks, no, no, 0)
    for step in lon_steps:
        add_source(exchange(adjoint_obs, 0, -step), numbers(lon_raw[step], rows), no, no, step)
    for phase in (1, 2):
        is_north = (odd == 0) == (phase == 1)
        add_source(exchange(adjoint_obs, phase, 0), numbers(lat_in[phase], lat_fields), is_north, ~is_north, 0)
        for step in lon_steps:
            add_source(
                exchange(adjoint_obs, phase, -step), numbers(diag_raw[phase, step], lat_fields), is_north, ~is_north, step
            )
    target = jnp.concatenate(targets)[None, :]
    lane_mask = jnp.concatenate(masks, axis=0)

    filtered = call(
        functools.partial(adjoint_kernel, len(sources)),
        shape(layers, rows, cols),
        [SMEM] + [VMEM] * (6 + len(sources)),
        (),
        limit,
    )(flags, target, lane_mask, *sources, ext_spread, ext_scale, ext_e, ext_n)

    others = from_levs(filtered)
    group = n_lat * n_lon * n_lev
    gradient, partial = call(
        functools.partial(gradient_kernel, len(others)),
        [shape(layers, rows, cols), shape(group, 1, LANES)],
        [SMEM] * 2 + [VMEM] * (2 + len(others)),
    )(flags, vertical, control, filtered, *others)
    sums = lax.all_to_all(partial, ("lat", "lon", "lev"), split_axis=0, concat_axis=0, tiled=True)
    direction = call(
        functools.partial(direction_kernel, float(control.size * group)),
        shape(layers, rows, cols),
        [VMEM] * 3 + [SMEM],
    )(gradient, sums, previous_direction, previous_square)
    return (gradient, direction)


def solution(mesh):
    field = P("lev", ("member", "lat"), "lon")
    shared = P("lev", "lat", "lon")
    placed = (
        field,
        P(),
        shared,
        shared,
        field,
        field,
        P("lev", "lat", "lon", None, None),
        P("lev", "lat", "lon", None, None),
        P("lev", "lat", "lon", None),
        P("lev", "lat", "lon", None, None, None, None),
        P("lev", ("member", "lat"), "lon", None, None, None),
        P("lat", "lon", None, None, None),
        field,
        P("member"),
    )
    return jax.shard_map(local, mesh=mesh, in_specs=placed, out_specs=(field, field), check_vma=False)
```

```python
import functools
import jax
import jax.numpy as jnp
from jax import lax
from jax.experimental import pallas as pl
from jax.experimental.pallas import tpu as pltpu
from jax.sharding import PartitionSpec as P

FILTER = 2
STEPS = 2
HALO = 4
WIDTHS = (4, 4, 4, 4, 2)
LANES = 128
smoothing = 0.1
diffusion = 0.15
f32 = jnp.float32
bf16 = jnp.bfloat16
VMEM = pl.BlockSpec(memory_space=pltpu.VMEM)
SMEM = pl.BlockSpec(memory_space=pltpu.SMEM)
HBM = pl.BlockSpec(memory_space=pltpu.HBM)
NN = (((1,), (0,)), ((), ()))


def call(kernel, out_shape, in_specs, scratch=(), limit=8 << 20, flops=1 << 20):
    many = isinstance(out_shape, (list, tuple))
    return pl.pallas_call(
        kernel,
        out_shape=out_shape,
        in_specs=in_specs,
        out_specs=[VMEM] * len(out_shape) if many else VMEM,
        scratch_shapes=list(scratch),
        compiler_params=pltpu.CompilerParams(vmem_limit_bytes=limit),
        cost_estimate=pl.CostEstimate(flops=flops, bytes_accessed=1 << 20, transcendentals=0),
    )


def held(*dims, dtype=f32):
    return pltpu.VMEM(dims, dtype)


def shape(*dims):
    return jax.ShapeDtypeStruct(dims, f32)


def split(value):
    high = value.astype(bf16)
    return high, (value - high.astype(f32)).astype(bf16)


def halves(value):
    high, low = split(value)
    return jnp.concatenate(
        [jnp.concatenate([high, high], axis=1), jnp.concatenate([low, jnp.zeros_like(low)], axis=1)], axis=0
    )


def dot(left, right, axis):
    pair = jnp.concatenate(split(right), axis=axis)
    result = lax.dot_general(halves(left), pair, (((1,), (axis,)), ((), ())), preferred_element_type=f32)
    return result[: left.shape[0]] + result[left.shape[0] :]


def for_each(count, body, start):
    if count <= 32:
        for i in range(count):
            start = body(i, start)
        return start
    return lax.fori_loop(0, count, body, start)


def north(x):
    return pltpu.roll(x, x.shape[0] - 1, 0)


def south(x):
    return pltpu.roll(x, 1, 0)


def east(x):
    return pltpu.roll(x, x.shape[1] - 1, 1)


def west(x):
    return pltpu.roll(x, 1, 1)


def smooth(s, spread):
    for repeat in range(FILTER):
        q = spread * s
        s = s + smoothing * spread * (north(q) + south(q) + east(q) + west(q) - 4.0 * q)
    return s


def edge_block(rows):
    lane = lax.broadcasted_iota(jnp.int32, (rows.shape[0], LANES), 1)
    return jnp.where(lane < LANES // 2, rows[:, :LANES], rows[:, rows.shape[1] - LANES :])


def blend(weights, own, others, layer):
    layers = own.shape[0]
    total = None
    for i, source in enumerate([own] + list(others)):
        for m in range(layers):
            at = layer * layers * (1 + len(others)) + i * layers + m
            term = weights[at : at + 1, 0:1] * source[m]
            total = term if total is None else total + term
    return total


def load_kernel(
    vertical, blocks, previous_square, control, spread, wind_e, wind_n, scale, previous, innovation,
    forth, back, square_v, control_v, spread_v, wind_e_v, wind_n_v, scale_v, previous_v, innovation_v,
    lon_out, first, last, vertical_s, blocks_s, square_s, sems,
):
    pairs = (
        (spread, spread_v), (wind_e, wind_e_v), (wind_n, wind_n_v), (scale, scale_v), (blocks, blocks_s),
        (vertical, vertical_s), (previous_square, square_s), (control, control_v),
        (innovation, innovation_v), (previous, previous_v),
    )
    copies = [pltpu.make_async_copy(a, b, sems.at[i]) for i, (a, b) in enumerate(pairs)]
    for copy in copies:
        copy.start()
    layers, rows, cols = control.shape
    slots, owners = blocks.shape
    for copy in copies[:5]:
        copy.wait()
    line = lax.broadcasted_iota(jnp.int32, (1, LANES), 1)
    numbers = jnp.full((1, LANES), -1.0, f32)
    for s in range(slots):
        for o in range(owners):
            numbers = jnp.where(line == s * owners + o, blocks_s[s, o].astype(f32), numbers)
    lane = lax.broadcasted_iota(jnp.int32, (rows, LANES), 1)
    packed = jnp.zeros((rows, LANES), f32)
    fields = (spread_v, wind_e_v, wind_n_v, scale_v)
    for i, field in enumerate(fields):
        for l in range(layers):
            packed = lon_item(packed, field[l], (1 + i) * layers + l, lane)
    lon_out[:rows, :] = packed
    lon_out[rows:, :] = jnp.broadcast_to(numbers, (8, LANES))
    for out, low in ((first, True), (last, False)):
        at = WIDTHS[0] * layers
        for field, width in zip(fields, WIDTHS[1:]):
            for l in range(layers):
                begin = 0 if low else rows - width
                out[at : at + width, :] = field[l, begin : begin + width, :]
                at += width
        for c in range(0, cols, LANES):
            out[at:, c : c + LANES] = jnp.broadcast_to(numbers, (out.shape[0] - at, LANES))
    for copy in copies[5:]:
        copy.wait()
    lev, levs = lax.axis_index("lev"), lax.axis_size("lev")
    for l in range(layers):
        for shift in range(levs):
            other = lax.rem(lev + levs - shift, levs)
            for m in range(layers):
                at = (l * levs + shift) * layers + m
                a, b = lev * layers + l, other * layers + m
                forth[at : at + 1, :] = jnp.full((1, LANES), vertical_s[a, b], f32)
                back[at : at + 1, :] = jnp.full((1, LANES), vertical_s[b, a], f32)
    square_v[...] = jnp.full((1, LANES), square_s[0], f32)


def lon_item(packed, field, item, lane):
    cols = field.shape[1]
    tile = jnp.where(lane < LANES // 2, field[:, :LANES], field[:, cols - LANES :])
    if item:
        tile = pltpu.roll(tile, 8 * item, 1)
    return jnp.where((lane + HALO - 8 * item) % LANES < 8, tile, packed)


def pack_kernel(n_other, *refs):
    forth, control, lon_part, first, last = refs[:5]
    others = refs[5 : 5 + n_other]
    blended, lon_out, lat_1, lat_2, diag_1, diag_2 = refs[5 + n_other :]
    layers, rows, cols = control.shape
    packed = lon_part[:rows, :]
    lane = lax.broadcasted_iota(jnp.int32, (rows, LANES), 1)
    firsts, lasts = [], []
    for l in range(layers):
        value = blend(forth, control, others, l)
        blended[l] = value
        packed = lon_item(packed, value, l, lane)
        firsts.append(value[:HALO, :])
        lasts.append(value[rows - HALO :, :])
    lon_out[:rows, :] = packed
    lon_out[rows:, :] = lon_part[rows:, :]
    even = lax.axis_index("lat") % 2 == 0
    for out, diag, use_last in ((lat_1, diag_1, even), (lat_2, diag_2, jnp.logical_not(even))):
        begin = HALO * layers
        flag = jnp.where(use_last, 1, 0)
        for l in range(layers):
            chosen = jnp.full((HALO, cols), flag, jnp.int32) == 1
            out[HALO * l : HALO * (l + 1), :] = jnp.where(chosen, lasts[l], firsts[l])
        chosen = jnp.full((first.shape[0] - begin, cols), flag, jnp.int32) == 1
        out[begin:, :] = jnp.where(chosen, last[begin:, :], first[begin:, :])
        diag[...] = edge_block(out[...])


def at_ends():
    lat = lax.axis_index("lat")
    return lat == 0, lat == lax.axis_size("lat") - 1


def unpack(own, lon_in, lat_1, lat_2, diag_1, diag_2, ext):
    layers, rows, cols = own[0].shape
    lane = lax.broadcasted_iota(jnp.int32, (rows, LANES), 1)
    keep = (lane < HALO) | (lane >= LANES - HALO)
    packed = lon_in[:rows, :]
    item = 0
    for field, out in zip(own, ext):
        for l in range(layers):
            out[l, :rows, :cols] = field[l]
            tile = pltpu.roll(packed, LANES - 8 * item, 1) if item else packed
            out[l, :rows, cols:] = jnp.where(keep, tile, 0.0)
            item += 1
    count = sum(WIDTHS) * layers
    for one, two, begin in ((lat_1, lat_2, 0), (diag_1, diag_2, cols)):
        width = one.shape[1]
        a, b = one[:count, :], two[:count, :]
        even = jnp.full(a.shape, lax.axis_index("lat") % 2, jnp.int32) == 0
        south_end, north_end = at_ends()
        top = jnp.full(a.shape, jnp.where(north_end, 1, 0), jnp.int32) == 0
        bottom = jnp.full(a.shape, jnp.where(south_end, 1, 0), jnp.int32) == 0
        if begin:
            lane_d = lax.broadcasted_iota(jnp.int32, a.shape, 1)
            inside = (lane_d < HALO) | (lane_d >= LANES - HALO)
            top = top & inside
            bottom = bottom & inside
        from_north = jnp.where(top, jnp.where(even, a, b), 0.0)
        from_south = jnp.where(bottom, jnp.where(even, b, a), 0.0)
        at = 0
        for out, l, w in [(e, l, w) for e, w in zip(ext, WIDTHS) for l in range(layers)]:
            if w < HALO:
                out[l, rows : rows + 8, begin : begin + width] = jnp.zeros((8, width), f32)
            out[l, rows : rows + w, begin : begin + width] = from_north[at : at + w, :]
            out[l, rows + 8 - w : rows + 8, begin : begin + width] = from_south[at : at + w, :]
            at += w


def inside_mask(ext_shape):
    south_end, north_end = at_ends()
    row = lax.broadcasted_iota(jnp.int32, ext_shape, 0)
    rows = ext_shape[0] - 8
    north_cut = jnp.where(north_end, rows, rows + 8)
    south_cut = jnp.where(south_end, rows + 4, rows + 8)
    cut = ((row >= north_cut) & (row < rows + 4)) | (row >= south_cut)
    return jnp.where(cut, 0.0, 1.0).astype(f32)


def forward_kernel(
    blocks, platforms, counts, mixed_in, spread_in, wind_e_in, wind_n_in, scale_in,
    lon_in, lat_1, lat_2, diag_1, diag_2, interp, innovation,
    sent, spread, scale, wind_e, wind_n,
    mixed, field, blocks_s, platforms_s, counts_s, sems,
):
    pairs = ((blocks, blocks_s), (platforms, platforms_s), (counts, counts_s))
    copies = [pltpu.make_async_copy(a, b, sems.at[i]) for i, (a, b) in enumerate(pairs)]
    for copy in copies:
        copy.start()
    own = (mixed_in, spread_in, wind_e_in, wind_n_in, scale_in)
    unpack(own, lon_in, lat_1, lat_2, diag_1, diag_2, (mixed, spread, wind_e, wind_n, scale))
    layers, ext_rows, ext_cols = mixed.shape
    rows, per = ext_rows - 8, ext_cols // LANES - 1
    mask = inside_mask((ext_rows, ext_cols))
    for l in range(layers):
        x = scale[l] * smooth(mixed[l], spread[l])
        u, v = 0.5 * wind_e[l], 0.5 * wind_n[l]
        for step in range(STEPS):
            if step:
                x = x * mask
            x = (
                (1.0 - 4.0 * diffusion) * x
                + (diffusion - u) * east(x)
                + (diffusion + u) * west(x)
                + (diffusion - v) * north(x)
                + (diffusion + v) * south(x)
            )
        for c in range(per):
            begin = (l * per + c) * ext_rows
            field[begin : begin + ext_rows, :] = x[:, c * LANES : (c + 1) * LANES]
    for copy in copies:
        copy.wait()
    count, width = innovation.shape
    slots, owners = blocks.shape
    row = lax.broadcasted_iota(jnp.int32, (count, width), 0)

    def body(b, total):
        block = blocks_s[b % slots, b // slots]
        at = (block // (rows * per) * per + block % per) * ext_rows + (block // per) % rows
        left = jnp.where(row == b, jnp.broadcast_to(field[pl.ds(at, 1), :], (count, width)), 0.0)
        return total + dot(left, interp[b], 1)

    departure = for_each(count, body, jnp.zeros((count, width), f32)) - innovation[...]
    half = sent.shape[1] // 2
    sent[...] = jnp.zeros(sent.shape, f32)
    for o in range(owners):
        for s in range(slots):
            live = jnp.full((1, width), counts_s[0, o], jnp.int32) > s
            b = o * slots + s
            sent[o, s : s + 1, :] = jnp.where(live, departure[b : b + 1, :], 0.0)
            sent[o, half + s : half + s + 1, :] = jnp.full((1, width), platforms_s[s, o].astype(f32), f32)


def weigh_kernel(slots, arrived, matrices, out, values, platform):
    tiles, height, width = arrived.shape
    for t in range(tiles):
        for s in range(slots):
            at = s * tiles + t
            values[at : at + 1, :] = arrived[t, s : s + 1, :]
            platform[at : at + 1, :] = arrived[t, height // 2 + s : height // 2 + s + 1, :]
    x, where = values[...], platform[...]
    total = jnp.zeros(x.shape, f32)
    for p in range(matrices.shape[0]):
        total = total + dot(jnp.where(where == float(p), x, 0.0), matrices[p], 1)
    out[...] = jnp.zeros(out.shape, f32)
    for t in range(tiles):
        for s in range(slots):
            at = s * tiles + t
            out[t, s : s + 1, :] = total[at : at + 1, :]


def transpose_kernel(slots, returned, interp, out):
    count, width = out.shape
    row = lax.broadcasted_iota(jnp.int32, (count, width), 0)

    def body(b, total):
        owner, slot = b // slots, b % slots
        weighted = returned[owner, pl.ds(slot, 1), :]
        left = jnp.where(
            row == slot * (count // slots) + owner, jnp.broadcast_to(weighted, (count, width)), 0.0
        )
        return total + dot(left, interp[b], 0)

    out[...] = for_each(count, body, jnp.zeros((count, width), f32))


def place_kernel(count, kinds, rows, layers, per, *refs):
    tiles, out = refs[:-1], refs[-1]
    line = lax.broadcasted_iota(jnp.int32, (1, LANES), 1)
    south_end, north_end = at_ends()
    odd = lax.axis_index("lat") % 2
    packs = -(-len(kinds) * count // LANES)
    targets = [jnp.full((1, LANES), -1.0, f32) for _ in range(packs)]
    for i, (tile, (phase, lon_step, begin)) in enumerate(zip(tiles, kinds)):
        block = tile[begin : begin + 1, :LANES]
        block_row = jnp.floor((block + 0.5) / per)
        col = block - block_row * per
        layer = jnp.floor((block_row + 0.5) / rows)
        row = block_row - layer * rows
        valid = block >= 0.0
        if phase:
            is_north = jnp.where(odd == phase - 1, 1, 0)
            usable = jnp.where(is_north == 1, jnp.where(north_end, 0, 1), jnp.where(south_end, 0, 1))
            is_north = jnp.full((1, LANES), is_north, jnp.int32) == 1
            usable = jnp.full((1, LANES), usable, jnp.int32) == 1
            valid = valid & usable
            valid = valid & ((is_north & (row < HALO)) | (jnp.logical_not(is_north) & (row >= rows - HALO)))
            row = jnp.where(is_north, row + rows, row + 8)
        if lon_step:
            at_first, at_last = col == 0.0, col == per - 1.0
            both = at_first | at_last
            if lon_step == 1:
                both = at_first
            if lon_step == -1:
                both = at_last
            valid = valid & both
            col = jnp.where(at_first, float(per), float(per + 1))
        place = jnp.where(valid, (layer * (per + 2) + col) * (rows + 8) + row, -1.0)
        pack, shift = divmod(i * count, LANES)
        if shift:
            place = pltpu.roll(place, shift, 1)
        mine = (line >= shift) & (line < shift + count)
        targets[pack] = jnp.where(mine, place, targets[pack])
    places = out.shape[0]
    index = lax.broadcasted_iota(jnp.int32, (places, LANES), 0)
    for pack, target in enumerate(targets):
        chosen = jnp.where(index == target.astype(jnp.int32), 1.0, 0.0).astype(bf16)
        out[:, pack * LANES : (pack + 1) * LANES] = chosen
        out[:, (packs + pack) * LANES : (packs + pack + 1) * LANES] = chosen


def adjoint_kernel(n_source, *refs):
    chosen = refs[0]
    sources = refs[1 : 1 + n_source]
    spread, scale, wind_e, wind_n = refs[1 + n_source : 5 + n_source]
    filtered, = refs[5 + n_source :]
    layers, ext_rows, ext_cols = spread.shape
    rows, cols = filtered.shape[1:]
    values = [s[...] for s in sources]
    spare = chosen.shape[1] // 2 - sum(v.shape[0] for v in values)
    if spare:
        values.append(jnp.zeros((spare, LANES), f32))
    parts = jnp.concatenate(split(jnp.concatenate(values, axis=0)), axis=0)
    forcing = lax.dot_general(chosen[...], parts, NN, preferred_element_type=f32)
    mask = inside_mask((ext_rows, ext_cols))
    lane = lax.broadcasted_iota(jnp.int32, (ext_rows, LANES), 1)
    per = cols // LANES
    for l in range(layers):
        begin = l * (per + 2) * ext_rows
        tiles = [forcing[begin + c * ext_rows : begin + (c + 1) * ext_rows, :] for c in range(per + 2)]
        y = jnp.concatenate(tiles[:per] + [jnp.where(lane < LANES // 2, tiles[per], tiles[per + 1])], axis=1)
        u, v = 0.5 * wind_e[l], 0.5 * wind_n[l]
        for step in range(STEPS):
            if step:
                y = y * mask
            y = (
                (1.0 - 4.0 * diffusion) * y
                + east((diffusion + u) * y)
                + west((diffusion - u) * y)
                + north((diffusion + v) * y)
                + south((diffusion - v) * y)
            )
        s = smooth(scale[l] * y, spread[l])
        filtered[l] = s[:rows, :cols]


def gradient_kernel(n_other, *refs):
    back, control, filtered = refs[:3]
    others = refs[3 : 3 + n_other]
    gradient, partial = refs[3 + n_other :]
    layers, rows, cols = control.shape
    total = jnp.zeros((8, LANES), f32)
    for m in range(layers):
        g = control[m] + blend(back, filtered, others, m)
        gradient[m] = g
        square = g * g
        for r in range(0, rows, 8):
            for c in range(0, cols, LANES):
                total = total + square[r : r + 8, c : c + LANES]
    total = jnp.sum(total, axis=0, keepdims=True)
    partial[...] = jnp.broadcast_to(total[None], partial.shape)


def direction_kernel(cell_count, gradient, sums, previous, previous_square, direction):
    total = jnp.sum(jnp.sum(sums[...], axis=0), axis=1, keepdims=True)
    factor = total / cell_count / previous_square[:, 0:1]
    for l in range(gradient.shape[0]):
        direction[l] = factor * previous[l] - gradient[l]


def local(
    control,
    vertical,
    spread,
    error_scale,
    wind_lon,
    wind_lat,
    obs_block,
    obs_platform,
    obs_count,
    interp,
    innovation,
    error_inverse,
    previous_direction,
    previous_square,
):
    n_lat, n_lon, n_lev = (lax.axis_size(a) for a in ("lat", "lon", "lev"))
    layers, rows, cols = control.shape
    ext_rows, ext_cols = rows + 8, cols + LANES
    owners = obs_count.shape[-1]
    slots = obs_block.shape[-1]
    width = interp.shape[-1]
    count = owners * slots
    blocks = obs_block.reshape(owners, slots).T
    platforms = obs_platform.reshape(owners, slots).T
    counts = obs_count.reshape(1, owners)
    weights = interp.reshape(count, width, width)
    limit = (8 << 20) + 3 * weights.size * 4
    per = cols // LANES
    lat_fields = sum(WIDTHS) * layers
    lat_rows = lat_fields // 8 * 8 + 8

    def from_levs(field):
        return [
            lax.ppermute(field, "lev", [(i, (i + k) % n_lev) for i in range(n_lev)]) for k in range(1, n_lev)
        ]

    def partner(a, phase):
        step = 1 if (a % 2 == 0) == (phase == 1) else -1
        return (a + step) % n_lat

    def exchange(field, phase, lon_step):
        pairs = []
        for a in range(n_lat):
            for b in range(n_lon):
                to = partner(a, phase) if phase else a
                pairs.append((a * n_lon + b, to * n_lon + (b + lon_step) % n_lon))
        return lax.ppermute(field, ("lat", "lon"), pairs)

    lon_steps = (2,) if n_lon == 2 else (1, -1)

    def from_lon(field, phase, step):
        return exchange(field, phase, 1 if step == 2 else -step)

    others = from_levs(control)
    field = held(layers, rows, cols)
    mix = held(layers * layers * n_lev, LANES)
    innovations = innovation.reshape(count, width)
    (
        forth, back, square_v, control_v, spread_v, wind_e_v, wind_n_v, scale_v, previous_v, innovation_v,
        lon_part, first, last,
    ) = call(
        load_kernel,
        [mix, mix, held(1, LANES)] + [field] * 6 + [held(count, width)]
        + [held(rows + 8, LANES), held(lat_rows, cols), held(lat_rows, cols)],
        [HBM] * 10,
        [
            pltpu.SMEM(vertical.shape, f32),
            pltpu.SMEM(blocks.shape, jnp.int32),
            pltpu.SMEM((1,), f32),
            pltpu.SemaphoreType.DMA((10,)),
        ],
    )(
        vertical, blocks, previous_square, control, spread, wind_lon, wind_lat, error_scale, previous_direction,
        innovations,
    )
    blended, lon_out, lat_1, lat_2, diag_1, diag_2 = call(
        functools.partial(pack_kernel, len(others)),
        [field, held(rows + 8, LANES)] + [held(lat_rows, cols)] * 2 + [held(lat_rows, LANES)] * 2,
        [VMEM] * (5 + len(others)),
    )(forth, control_v, lon_part, first, last, *others)

    lane = jnp.arange(LANES, dtype=jnp.int32)
    lat_in = {phase: exchange(out, phase, 0) for phase, out in ((1, lat_1), (2, lat_2))}
    lon_raw = {step: from_lon(lon_out, 0, step) for step in lon_steps}
    diag_raw = {
        (phase, step): from_lon(out, phase, step)
        for phase, out in ((1, diag_1), (2, diag_2))
        for step in lon_steps
    }
    if n_lon == 2:
        lon_in = lon_raw[2]
        diag_in = {phase: diag_raw[phase, 2] for phase in (1, 2)}
    else:
        lon_in = jnp.where(lane % 8 < HALO, lon_raw[1], lon_raw[-1])
        diag_in = {
            phase: jnp.where(lane < LANES // 2, diag_raw[phase, 1], diag_raw[phase, -1]) for phase in (1, 2)
        }

    half = -(-slots // 4) * 4
    ext = held(layers, ext_rows, ext_cols)
    sent, ext_spread, ext_scale, ext_e, ext_n = call(
        forward_kernel,
        [shape(owners, 2 * half, width), ext, ext, ext, ext],
        [HBM] * 3 + [VMEM] * 12,
        [
            pltpu.VMEM((layers, ext_rows, ext_cols), f32),
            pltpu.VMEM((layers * ext_rows * per, LANES), f32),
            pltpu.SMEM(blocks.shape, jnp.int32),
            pltpu.SMEM(blocks.shape, jnp.int32),
            pltpu.SMEM(counts.shape, jnp.int32),
            pltpu.SemaphoreType.DMA((3,)),
        ],
        limit,
    )(
        blocks, platforms, counts, blended, spread_v, wind_e_v, wind_n_v, scale_v,
        lon_in, lat_in[1], lat_in[2], diag_in[1], diag_in[2], weights, innovation_v,
    )

    arrived = lax.all_to_all(sent, ("lat", "lon"), split_axis=0, concat_axis=0, tiled=True)
    matrices = error_inverse.reshape(error_inverse.shape[-3:])
    result = call(
        functools.partial(weigh_kernel, slots),
        shape(owners, 2 * half, width),
        [VMEM] * 2,
        [pltpu.VMEM((count, width), f32)] * 2,
    )(arrived, matrices)
    returned = lax.all_to_all(result, ("lat", "lon"), split_axis=0, concat_axis=0, tiled=True)
    adjoint_obs = call(
        functools.partial(transpose_kernel, slots), shape(count, width), [VMEM] * 2, (), limit
    )(returned, weights)

    sources, tiles, kinds = [adjoint_obs], [lon_out], [(0, 0, rows)]
    for step in lon_steps:
        sources.append(from_lon(adjoint_obs, 0, step))
        tiles.append(lon_raw[step])
        kinds.append((0, step, rows))
    for phase in (1, 2):
        sources.append(exchange(adjoint_obs, phase, 0))
        tiles.append(lat_in[phase])
        kinds.append((phase, 0, lat_fields))
        for step in lon_steps:
            sources.append(from_lon(adjoint_obs, phase, step))
            tiles.append(diag_raw[phase, step])
            kinds.append((phase, step, lat_fields))
    depth = -(-len(kinds) * count // LANES) * LANES
    chosen = call(
        functools.partial(place_kernel, count, kinds, rows, layers, per),
        held(layers * (per + 2) * ext_rows, 2 * depth, dtype=bf16),
        [VMEM] * len(tiles),
        (),
        limit,
    )(*tiles)
    filtered = call(
        functools.partial(adjoint_kernel, len(sources)),
        shape(layers, rows, cols),
        [VMEM] * (5 + len(sources)),
        (),
        limit,
    )(chosen, *sources, ext_spread, ext_scale, ext_e, ext_n)

    others = from_levs(filtered)
    group = n_lat * n_lon * n_lev
    gradient, partial = call(
        functools.partial(gradient_kernel, len(others)),
        [field, shape(group, 1, LANES)],
        [VMEM] * (3 + len(others)),
    )(back, control_v, filtered, *others)
    sums = lax.all_to_all(partial, ("lat", "lon", "lev"), split_axis=0, concat_axis=0, tiled=True)
    direction = call(
        functools.partial(direction_kernel, float(control.size * group)),
        shape(layers, rows, cols),
        [VMEM] * 4,
    )(gradient, sums, previous_v, square_v)
    return (gradient, direction)


def solution(mesh):
    field = P("lev", ("member", "lat"), "lon")
    shared = P("lev", "lat", "lon")
    placed = (
        field,
        P(),
        shared,
        shared,
        field,
        field,
        P("lev", "lat", "lon", None, None),
        P("lev", "lat", "lon", None, None),
        P("lev", "lat", "lon", None),
        P("lev", "lat", "lon", None, None, None, None),
        P("lev", ("member", "lat"), "lon", None, None, None),
        P("lat", "lon", None, None, None),
        field,
        P("member"),
    )
    return jax.shard_map(local, mesh=mesh, in_specs=placed, out_specs=(field, field), check_vma=False)
```

```python
import functools
import jax
import jax.numpy as jnp
from jax import lax
from jax.experimental import pallas as pl
from jax.experimental.pallas import tpu as pltpu
from jax.sharding import PartitionSpec as P

FILTER = 2
STEPS = 2
HALO = 4
WIDTHS = (4, 4, 4, 4, 2)
LANES = 128
smoothing = 0.1
diffusion = 0.15
f32 = jnp.float32
bf16 = jnp.bfloat16
VMEM = pl.BlockSpec(memory_space=pltpu.VMEM)
SMEM = pl.BlockSpec(memory_space=pltpu.SMEM)
HBM = pl.BlockSpec(memory_space=pltpu.HBM)
NN = (((1,), (0,)), ((), ()))


def call(kernel, out_shape, in_specs, scratch=(), limit=8 << 20, flops=1 << 20):
    many = isinstance(out_shape, (list, tuple))
    return pl.pallas_call(
        kernel,
        out_shape=out_shape,
        in_specs=in_specs,
        out_specs=[VMEM] * len(out_shape) if many else VMEM,
        scratch_shapes=list(scratch),
        compiler_params=pltpu.CompilerParams(vmem_limit_bytes=limit),
        cost_estimate=pl.CostEstimate(flops=flops, bytes_accessed=1 << 20, transcendentals=0),
    )


def held(*dims, dtype=f32):
    return pltpu.VMEM(dims, dtype)


def shape(*dims):
    return jax.ShapeDtypeStruct(dims, f32)


def split(value):
    high = value.astype(bf16)
    return high, (value - high.astype(f32)).astype(bf16)


def halves(value):
    high, low = split(value)
    return jnp.concatenate(
        [jnp.concatenate([high, high], axis=1), jnp.concatenate([low, jnp.zeros_like(low)], axis=1)], axis=0
    )


def dot(left, right, axis):
    pair = jnp.concatenate(split(right), axis=axis)
    result = lax.dot_general(halves(left), pair, (((1,), (axis,)), ((), ())), preferred_element_type=f32)
    return result[: left.shape[0]] + result[left.shape[0] :]


def for_each(count, body, start):
    if count <= 32:
        for i in range(count):
            start = body(i, start)
        return start
    return lax.fori_loop(0, count, body, start)


def north(x):
    return pltpu.roll(x, x.shape[0] - 1, 0)


def south(x):
    return pltpu.roll(x, 1, 0)


def east(x):
    return pltpu.roll(x, x.shape[1] - 1, 1)


def west(x):
    return pltpu.roll(x, 1, 1)


def smooth(s, spread):
    for repeat in range(FILTER):
        q = spread * s
        s = s + smoothing * spread * (north(q) + south(q) + east(q) + west(q) - 4.0 * q)
    return s


def edge_block(rows):
    lane = lax.broadcasted_iota(jnp.int32, (rows.shape[0], LANES), 1)
    return jnp.where(lane < LANES // 2, rows[:, :LANES], rows[:, rows.shape[1] - LANES :])


def blend(weights, own, others, layer):
    layers = own.shape[0]
    total = None
    for i, source in enumerate([own] + list(others)):
        for m in range(layers):
            at = layer * layers * (1 + len(others)) + i * layers + m
            term = weights[at : at + 1, 0:1] * source[m]
            total = term if total is None else total + term
    return total


def load_kernel(
    vertical, blocks, previous_square, control, spread, wind_e, wind_n, scale, previous, innovation,
    platforms, counts,
    forth, back, square_v, control_v, spread_v, wind_e_v, wind_n_v, scale_v, previous_v, innovation_v,
    blocks_v, platforms_v, counts_v, lon_out, first, last, vertical_s, blocks_s, square_s, sems,
):
    pairs = (
        (spread, spread_v), (wind_e, wind_e_v), (wind_n, wind_n_v), (scale, scale_v), (blocks, blocks_s),
        (vertical, vertical_s), (previous_square, square_s), (control, control_v),
        (innovation, innovation_v), (previous, previous_v), (blocks, blocks_v), (platforms, platforms_v),
        (counts, counts_v),
    )
    copies = [pltpu.make_async_copy(a, b, sems.at[i]) for i, (a, b) in enumerate(pairs)]
    for copy in copies:
        copy.start()
    layers, rows, cols = control.shape
    slots, owners = blocks.shape
    for copy in copies[:5]:
        copy.wait()
    line = lax.broadcasted_iota(jnp.int32, (1, LANES), 1)
    numbers = jnp.full((1, LANES), -1.0, f32)
    for s in range(slots):
        for o in range(owners):
            numbers = jnp.where(line == s * owners + o, blocks_s[s, o].astype(f32), numbers)
    lane = lax.broadcasted_iota(jnp.int32, (rows, LANES), 1)
    packed = jnp.zeros((rows, LANES), f32)
    fields = (spread_v, wind_e_v, wind_n_v, scale_v)
    for i, field in enumerate(fields):
        for l in range(layers):
            packed = lon_item(packed, field[l], (1 + i) * layers + l, lane)
    lon_out[:rows, :] = packed
    lon_out[rows:, :] = jnp.broadcast_to(numbers, (8, LANES))
    for out, low in ((first, True), (last, False)):
        at = WIDTHS[0] * layers
        for field, width in zip(fields, WIDTHS[1:]):
            for l in range(layers):
                begin = 0 if low else rows - width
                out[at : at + width, :] = field[l, begin : begin + width, :]
                at += width
        for c in range(0, cols, LANES):
            out[at:, c : c + LANES] = jnp.broadcast_to(numbers, (out.shape[0] - at, LANES))
    for copy in copies[5:]:
        copy.wait()
    lev, levs = lax.axis_index("lev"), lax.axis_size("lev")
    for l in range(layers):
        for shift in range(levs):
            other = lax.rem(lev + levs - shift, levs)
            for m in range(layers):
                at = (l * levs + shift) * layers + m
                a, b = lev * layers + l, other * layers + m
                forth[at : at + 1, :] = jnp.full((1, LANES), vertical_s[a, b], f32)
                back[at : at + 1, :] = jnp.full((1, LANES), vertical_s[b, a], f32)
    square_v[...] = jnp.full((1, LANES), square_s[0], f32)


def lon_item(packed, field, item, lane):
    cols = field.shape[1]
    tile = jnp.where(lane < LANES // 2, field[:, :LANES], field[:, cols - LANES :])
    if item:
        tile = pltpu.roll(tile, 8 * item, 1)
    return jnp.where((lane + HALO - 8 * item) % LANES < 8, tile, packed)


def pack_kernel(n_other, *refs):
    forth, control, lon_part, first, last = refs[:5]
    others = refs[5 : 5 + n_other]
    blended, lon_out, lat_1, lat_2, diag_1, diag_2 = refs[5 + n_other :]
    layers, rows, cols = control.shape
    packed = lon_part[:rows, :]
    lane = lax.broadcasted_iota(jnp.int32, (rows, LANES), 1)
    firsts, lasts = [], []
    for l in range(layers):
        value = blend(forth, control, others, l)
        blended[l] = value
        packed = lon_item(packed, value, l, lane)
        firsts.append(value[:HALO, :])
        lasts.append(value[rows - HALO :, :])
    lon_out[:rows, :] = packed
    lon_out[rows:, :] = lon_part[rows:, :]
    even = lax.axis_index("lat") % 2 == 0
    for out, diag, use_last in ((lat_1, diag_1, even), (lat_2, diag_2, jnp.logical_not(even))):
        begin = HALO * layers
        flag = jnp.where(use_last, 1, 0)
        for l in range(layers):
            chosen = jnp.full((HALO, cols), flag, jnp.int32) == 1
            out[HALO * l : HALO * (l + 1), :] = jnp.where(chosen, lasts[l], firsts[l])
        chosen = jnp.full((first.shape[0] - begin, cols), flag, jnp.int32) == 1
        out[begin:, :] = jnp.where(chosen, last[begin:, :], first[begin:, :])
        diag[...] = edge_block(out[...])


def at_ends():
    lat = lax.axis_index("lat")
    return lat == 0, lat == lax.axis_size("lat") - 1


def unpack(own, lon_in, lat_1, lat_2, diag_1, diag_2, ext):
    layers, rows, cols = own[0].shape
    lane = lax.broadcasted_iota(jnp.int32, (rows, LANES), 1)
    keep = (lane < HALO) | (lane >= LANES - HALO)
    packed = lon_in[:rows, :]
    item = 0
    for field, out in zip(own, ext):
        for l in range(layers):
            out[l, :rows, :cols] = field[l]
            tile = pltpu.roll(packed, LANES - 8 * item, 1) if item else packed
            out[l, :rows, cols:] = jnp.where(keep, tile, 0.0)
            item += 1
    count = sum(WIDTHS) * layers
    for one, two, begin in ((lat_1, lat_2, 0), (diag_1, diag_2, cols)):
        width = one.shape[1]
        a, b = one[:count, :], two[:count, :]
        even = jnp.full(a.shape, lax.axis_index("lat") % 2, jnp.int32) == 0
        south_end, north_end = at_ends()
        top = jnp.full(a.shape, jnp.where(north_end, 1, 0), jnp.int32) == 0
        bottom = jnp.full(a.shape, jnp.where(south_end, 1, 0), jnp.int32) == 0
        if begin:
            lane_d = lax.broadcasted_iota(jnp.int32, a.shape, 1)
            inside = (lane_d < HALO) | (lane_d >= LANES - HALO)
            top = top & inside
            bottom = bottom & inside
        from_north = jnp.where(top, jnp.where(even, a, b), 0.0)
        from_south = jnp.where(bottom, jnp.where(even, b, a), 0.0)
        at = 0
        for out, l, w in [(e, l, w) for e, w in zip(ext, WIDTHS) for l in range(layers)]:
            if w < HALO:
                out[l, rows : rows + 8, begin : begin + width] = jnp.zeros((8, width), f32)
            out[l, rows : rows + w, begin : begin + width] = from_north[at : at + w, :]
            out[l, rows + 8 - w : rows + 8, begin : begin + width] = from_south[at : at + w, :]
            at += w


def inside_mask(ext_shape):
    south_end, north_end = at_ends()
    row = lax.broadcasted_iota(jnp.int32, ext_shape, 0)
    rows = ext_shape[0] - 8
    north_cut = jnp.where(north_end, rows, rows + 8)
    south_cut = jnp.where(south_end, rows + 4, rows + 8)
    cut = ((row >= north_cut) & (row < rows + 4)) | (row >= south_cut)
    return jnp.where(cut, 0.0, 1.0).astype(f32)


def forward_kernel(
    blocks, platforms, counts, mixed_in, spread_in, wind_e_in, wind_n_in, scale_in,
    lon_in, lat_1, lat_2, diag_1, diag_2, interp, innovation,
    sent, spread, scale, wind_e, wind_n,
    mixed, field, blocks_s, platforms_s, counts_s, sems,
):
    pairs = ((blocks, blocks_s), (platforms, platforms_s), (counts, counts_s))
    copies = [pltpu.make_async_copy(a, b, sems.at[i]) for i, (a, b) in enumerate(pairs)]
    for copy in copies:
        copy.start()
    own = (mixed_in, spread_in, wind_e_in, wind_n_in, scale_in)
    unpack(own, lon_in, lat_1, lat_2, diag_1, diag_2, (mixed, spread, wind_e, wind_n, scale))
    layers, ext_rows, ext_cols = mixed.shape
    rows, per = ext_rows - 8, ext_cols // LANES - 1
    mask = inside_mask((ext_rows, ext_cols))
    for l in range(layers):
        x = scale[l] * smooth(mixed[l], spread[l])
        u, v = 0.5 * wind_e[l], 0.5 * wind_n[l]
        for step in range(STEPS):
            if step:
                x = x * mask
            x = (
                (1.0 - 4.0 * diffusion) * x
                + (diffusion - u) * east(x)
                + (diffusion + u) * west(x)
                + (diffusion - v) * north(x)
                + (diffusion + v) * south(x)
            )
        for c in range(per):
            begin = (l * per + c) * ext_rows
            field[begin : begin + ext_rows, :] = x[:, c * LANES : (c + 1) * LANES]
    for copy in copies:
        copy.wait()
    count, width = innovation.shape
    slots, owners = blocks.shape
    row = lax.broadcasted_iota(jnp.int32, (count, width), 0)

    def body(b, total):
        block = blocks_s[b % slots, b // slots]
        at = (block // (rows * per) * per + block % per) * ext_rows + (block // per) % rows
        left = jnp.where(row == b, jnp.broadcast_to(field[pl.ds(at, 1), :], (count, width)), 0.0)
        return total + dot(left, interp[b], 1)

    departure = for_each(count, body, jnp.zeros((count, width), f32)) - innovation[...]
    half = sent.shape[1] // 2
    sent[...] = jnp.zeros(sent.shape, f32)
    for o in range(owners):
        for s in range(slots):
            live = jnp.full((1, width), counts_s[0, o], jnp.int32) > s
            b = o * slots + s
            sent[o, s : s + 1, :] = jnp.where(live, departure[b : b + 1, :], 0.0)
            sent[o, half + s : half + s + 1, :] = jnp.full((1, width), platforms_s[s, o].astype(f32), f32)


def weigh_kernel(slots, arrived, matrices, out, values, platform):
    tiles, height, width = arrived.shape
    for t in range(tiles):
        for s in range(slots):
            at = s * tiles + t
            values[at : at + 1, :] = arrived[t, s : s + 1, :]
            platform[at : at + 1, :] = arrived[t, height // 2 + s : height // 2 + s + 1, :]
    x, where = values[...], platform[...]
    total = jnp.zeros(x.shape, f32)
    for p in range(matrices.shape[0]):
        total = total + dot(jnp.where(where == float(p), x, 0.0), matrices[p], 1)
    out[...] = jnp.zeros(out.shape, f32)
    for t in range(tiles):
        for s in range(slots):
            at = s * tiles + t
            out[t, s : s + 1, :] = total[at : at + 1, :]


def transpose_kernel(slots, returned, interp, out):
    count, width = out.shape
    row = lax.broadcasted_iota(jnp.int32, (count, width), 0)

    def body(b, total):
        owner, slot = b // slots, b % slots
        weighted = returned[owner, pl.ds(slot, 1), :]
        left = jnp.where(
            row == slot * (count // slots) + owner, jnp.broadcast_to(weighted, (count, width)), 0.0
        )
        return total + dot(left, interp[b], 0)

    out[...] = for_each(count, body, jnp.zeros((count, width), f32))


def place_kernel(count, kinds, rows, layers, per, *refs):
    tiles, out = refs[:-1], refs[-1]
    line = lax.broadcasted_iota(jnp.int32, (1, LANES), 1)
    south_end, north_end = at_ends()
    odd = lax.axis_index("lat") % 2
    packs = -(-len(kinds) * count // LANES)
    targets = [jnp.full((1, LANES), -1.0, f32) for _ in range(packs)]
    for i, (tile, (phase, lon_step, begin)) in enumerate(zip(tiles, kinds)):
        block = tile[begin : begin + 1, :LANES]
        block_row = jnp.floor((block + 0.5) / per)
        col = block - block_row * per
        layer = jnp.floor((block_row + 0.5) / rows)
        row = block_row - layer * rows
        valid = block >= 0.0
        if phase:
            is_north = jnp.where(odd == phase - 1, 1, 0)
            usable = jnp.where(is_north == 1, jnp.where(north_end, 0, 1), jnp.where(south_end, 0, 1))
            is_north = jnp.full((1, LANES), is_north, jnp.int32) == 1
            usable = jnp.full((1, LANES), usable, jnp.int32) == 1
            valid = valid & usable
            valid = valid & ((is_north & (row < HALO)) | (jnp.logical_not(is_north) & (row >= rows - HALO)))
            row = jnp.where(is_north, row + rows, row + 8)
        if lon_step:
            at_first, at_last = col == 0.0, col == per - 1.0
            both = at_first | at_last
            if lon_step == 1:
                both = at_first
            if lon_step == -1:
                both = at_last
            valid = valid & both
            col = jnp.where(at_first, float(per), float(per + 1))
        place = jnp.where(valid, (layer * (per + 2) + col) * (rows + 8) + row, -1.0)
        pack, shift = divmod(i * count, LANES)
        if shift:
            place = pltpu.roll(place, shift, 1)
        mine = (line >= shift) & (line < shift + count)
        targets[pack] = jnp.where(mine, place, targets[pack])
    places = out.shape[0]
    index = lax.broadcasted_iota(jnp.int32, (places, LANES), 0)
    for pack, target in enumerate(targets):
        chosen = jnp.where(index == target.astype(jnp.int32), 1.0, 0.0).astype(bf16)
        out[:, pack * LANES : (pack + 1) * LANES] = chosen
        out[:, (packs + pack) * LANES : (packs + pack + 1) * LANES] = chosen


def adjoint_kernel(n_source, *refs):
    chosen = refs[0]
    sources = refs[1 : 1 + n_source]
    spread, scale, wind_e, wind_n = refs[1 + n_source : 5 + n_source]
    filtered, = refs[5 + n_source :]
    layers, ext_rows, ext_cols = spread.shape
    rows, cols = filtered.shape[1:]
    values = [s[...] for s in sources]
    spare = chosen.shape[1] // 2 - sum(v.shape[0] for v in values)
    if spare:
        values.append(jnp.zeros((spare, LANES), f32))
    parts = jnp.concatenate(split(jnp.concatenate(values, axis=0)), axis=0)
    forcing = lax.dot_general(chosen[...], parts, NN, preferred_element_type=f32)
    mask = inside_mask((ext_rows, ext_cols))
    lane = lax.broadcasted_iota(jnp.int32, (ext_rows, LANES), 1)
    per = cols // LANES
    for l in range(layers):
        begin = l * (per + 2) * ext_rows
        tiles = [forcing[begin + c * ext_rows : begin + (c + 1) * ext_rows, :] for c in range(per + 2)]
        y = jnp.concatenate(tiles[:per] + [jnp.where(lane < LANES // 2, tiles[per], tiles[per + 1])], axis=1)
        u, v = 0.5 * wind_e[l], 0.5 * wind_n[l]
        for step in range(STEPS):
            if step:
                y = y * mask
            y = (
                (1.0 - 4.0 * diffusion) * y
                + east((diffusion + u) * y)
                + west((diffusion - u) * y)
                + north((diffusion + v) * y)
                + south((diffusion - v) * y)
            )
        s = smooth(scale[l] * y, spread[l])
        filtered[l] = s[:rows, :cols]


def gradient_kernel(n_other, *refs):
    back, control, filtered = refs[:3]
    others = refs[3 : 3 + n_other]
    gradient, partial = refs[3 + n_other :]
    layers, rows, cols = control.shape
    total = jnp.zeros((8, LANES), f32)
    for m in range(layers):
        g = control[m] + blend(back, filtered, others, m)
        gradient[m] = g
        square = g * g
        for r in range(0, rows, 8):
            for c in range(0, cols, LANES):
                total = total + square[r : r + 8, c : c + LANES]
    total = jnp.sum(total, axis=0, keepdims=True)
    partial[...] = jnp.broadcast_to(total[None], partial.shape)


def direction_kernel(cell_count, gradient, sums, previous, previous_square, direction):
    total = jnp.sum(jnp.sum(sums[...], axis=0), axis=1, keepdims=True)
    factor = total / cell_count / previous_square[:, 0:1]
    for l in range(gradient.shape[0]):
        direction[l] = factor * previous[l] - gradient[l]


def local(
    control,
    vertical,
    spread,
    error_scale,
    wind_lon,
    wind_lat,
    obs_block,
    obs_platform,
    obs_count,
    interp,
    innovation,
    error_inverse,
    previous_direction,
    previous_square,
):
    n_lat, n_lon, n_lev = (lax.axis_size(a) for a in ("lat", "lon", "lev"))
    layers, rows, cols = control.shape
    ext_rows, ext_cols = rows + 8, cols + LANES
    owners = obs_count.shape[-1]
    slots = obs_block.shape[-1]
    width = interp.shape[-1]
    count = owners * slots
    blocks = obs_block.reshape(owners, slots).T
    platforms = obs_platform.reshape(owners, slots).T
    counts = obs_count.reshape(1, owners)
    weights = interp.reshape(count, width, width)
    limit = (8 << 20) + 3 * weights.size * 4
    per = cols // LANES
    lat_fields = sum(WIDTHS) * layers
    lat_rows = lat_fields // 8 * 8 + 8

    def from_levs(field):
        return [
            lax.ppermute(field, "lev", [(i, (i + k) % n_lev) for i in range(n_lev)]) for k in range(1, n_lev)
        ]

    def partner(a, phase):
        step = 1 if (a % 2 == 0) == (phase == 1) else -1
        return (a + step) % n_lat

    def exchange(field, phase, lon_step):
        pairs = []
        for a in range(n_lat):
            for b in range(n_lon):
                to = partner(a, phase) if phase else a
                pairs.append((a * n_lon + b, to * n_lon + (b + lon_step) % n_lon))
        return lax.ppermute(field, ("lat", "lon"), pairs)

    lon_steps = (2,) if n_lon == 2 else (1, -1)

    def from_lon(field, phase, step):
        return exchange(field, phase, 1 if step == 2 else -step)

    others = from_levs(control)
    field = held(layers, rows, cols)
    mix = held(layers * layers * n_lev, LANES)
    innovations = innovation.reshape(count, width)
    (
        forth, back, square_v, control_v, spread_v, wind_e_v, wind_n_v, scale_v, previous_v, innovation_v,
        blocks_v, platforms_v, counts_v, lon_part, first, last,
    ) = call(
        load_kernel,
        [mix, mix, held(1, LANES)] + [field] * 6 + [held(count, width)]
        + [held(*x.shape, dtype=jnp.int32) for x in (blocks, platforms, counts)]
        + [held(rows + 8, LANES), held(lat_rows, cols), held(lat_rows, cols)],
        [HBM] * 12,
        [
            pltpu.SMEM(vertical.shape, f32),
            pltpu.SMEM(blocks.shape, jnp.int32),
            pltpu.SMEM((1,), f32),
            pltpu.SemaphoreType.DMA((13,)),
        ],
        58 << 20,
    )(
        vertical, blocks, previous_square, control, spread, wind_lon, wind_lat, error_scale, previous_direction,
        innovations, platforms, counts,
    )
    blended, lon_out, lat_1, lat_2, diag_1, diag_2 = call(
        functools.partial(pack_kernel, len(others)),
        [field, held(rows + 8, LANES)] + [held(lat_rows, cols)] * 2 + [held(lat_rows, LANES)] * 2,
        [VMEM] * (5 + len(others)),
    )(forth, control_v, lon_part, first, last, *others)

    lane = jnp.arange(LANES, dtype=jnp.int32)
    lat_in = {phase: exchange(out, phase, 0) for phase, out in ((1, lat_1), (2, lat_2))}
    lon_raw = {step: from_lon(lon_out, 0, step) for step in lon_steps}
    diag_raw = {
        (phase, step): from_lon(out, phase, step)
        for phase, out in ((1, diag_1), (2, diag_2))
        for step in lon_steps
    }
    if n_lon == 2:
        lon_in = lon_raw[2]
        diag_in = {phase: diag_raw[phase, 2] for phase in (1, 2)}
    else:
        lon_in = jnp.where(lane % 8 < HALO, lon_raw[1], lon_raw[-1])
        diag_in = {
            phase: jnp.where(lane < LANES // 2, diag_raw[phase, 1], diag_raw[phase, -1]) for phase in (1, 2)
        }

    half = -(-slots // 4) * 4
    ext = held(layers, ext_rows, ext_cols)
    sent, ext_spread, ext_scale, ext_e, ext_n = call(
        forward_kernel,
        [shape(owners, 2 * half, width), ext, ext, ext, ext],
        [VMEM] * 15,
        [
            pltpu.VMEM((layers, ext_rows, ext_cols), f32),
            pltpu.VMEM((layers * ext_rows * per, LANES), f32),
            pltpu.SMEM(blocks.shape, jnp.int32),
            pltpu.SMEM(blocks.shape, jnp.int32),
            pltpu.SMEM(counts.shape, jnp.int32),
            pltpu.SemaphoreType.DMA((3,)),
        ],
        limit,
    )(
        blocks_v, platforms_v, counts_v, blended, spread_v, wind_e_v, wind_n_v, scale_v,
        lon_in, lat_in[1], lat_in[2], diag_in[1], diag_in[2], weights, innovation_v,
    )

    arrived = lax.all_to_all(sent, ("lat", "lon"), split_axis=0, concat_axis=0, tiled=True)
    matrices = error_inverse.reshape(error_inverse.shape[-3:])
    result = call(
        functools.partial(weigh_kernel, slots),
        shape(owners, 2 * half, width),
        [VMEM] * 2,
        [pltpu.VMEM((count, width), f32)] * 2,
    )(arrived, matrices)
    returned = lax.all_to_all(result, ("lat", "lon"), split_axis=0, concat_axis=0, tiled=True)
    adjoint_obs = call(
        functools.partial(transpose_kernel, slots), shape(count, width), [VMEM] * 2, (), limit
    )(returned, weights)

    sources, tiles, kinds = [adjoint_obs], [lon_out], [(0, 0, rows)]
    for step in lon_steps:
        sources.append(from_lon(adjoint_obs, 0, step))
        tiles.append(lon_raw[step])
        kinds.append((0, step, rows))
    for phase in (1, 2):
        sources.append(exchange(adjoint_obs, phase, 0))
        tiles.append(lat_in[phase])
        kinds.append((phase, 0, lat_fields))
        for step in lon_steps:
            sources.append(from_lon(adjoint_obs, phase, step))
            tiles.append(diag_raw[phase, step])
            kinds.append((phase, step, lat_fields))
    depth = -(-len(kinds) * count // LANES) * LANES
    chosen = call(
        functools.partial(place_kernel, count, kinds, rows, layers, per),
        held(layers * (per + 2) * ext_rows, 2 * depth, dtype=bf16),
        [VMEM] * len(tiles),
        (),
        limit,
    )(*tiles)
    filtered = call(
        functools.partial(adjoint_kernel, len(sources)),
        shape(layers, rows, cols),
        [VMEM] * (5 + len(sources)),
        (),
        limit,
    )(chosen, *sources, ext_spread, ext_scale, ext_e, ext_n)

    others = from_levs(filtered)
    group = n_lat * n_lon * n_lev
    gradient, partial = call(
        functools.partial(gradient_kernel, len(others)),
        [field, shape(group, 1, LANES)],
        [VMEM] * (3 + len(others)),
    )(back, control_v, filtered, *others)
    sums = lax.all_to_all(partial, ("lat", "lon", "lev"), split_axis=0, concat_axis=0, tiled=True)
    direction = call(
        functools.partial(direction_kernel, float(control.size * group)),
        shape(layers, rows, cols),
        [VMEM] * 4,
    )(gradient, sums, previous_v, square_v)
    return (gradient, direction)


def solution(mesh):
    field = P("lev", ("member", "lat"), "lon")
    shared = P("lev", "lat", "lon")
    placed = (
        field,
        P(),
        shared,
        shared,
        field,
        field,
        P("lev", "lat", "lon", None, None),
        P("lev", "lat", "lon", None, None),
        P("lev", "lat", "lon", None),
        P("lev", "lat", "lon", None, None, None, None),
        P("lev", ("member", "lat"), "lon", None, None, None),
        P("lat", "lon", None, None, None),
        field,
        P("member"),
    )
    return jax.shard_map(local, mesh=mesh, in_specs=placed, out_specs=(field, field), check_vma=False)
```

```python
import functools
import jax
import jax.numpy as jnp
from jax import lax
from jax.experimental import pallas as pl
from jax.experimental.pallas import tpu as pltpu
from jax.sharding import PartitionSpec as P

FILTER = 2
STEPS = 2
HALO = 4
WIDTHS = (4, 4, 4, 4, 2)
LANES = 128
smoothing = 0.1
diffusion = 0.15
f32 = jnp.float32
bf16 = jnp.bfloat16
VMEM = pl.BlockSpec(memory_space=pltpu.VMEM)
SMEM = pl.BlockSpec(memory_space=pltpu.SMEM)
HBM = pl.BlockSpec(memory_space=pltpu.HBM)
NN = (((1,), (0,)), ((), ()))


def call(kernel, out_shape, in_specs, scratch=(), limit=8 << 20, aliases=None):
    many = isinstance(out_shape, (list, tuple))
    return pl.pallas_call(
        kernel,
        out_shape=out_shape,
        in_specs=in_specs,
        out_specs=[VMEM] * len(out_shape) if many else VMEM,
        scratch_shapes=list(scratch),
        input_output_aliases=aliases or {},
        compiler_params=pltpu.CompilerParams(vmem_limit_bytes=limit),
        cost_estimate=pl.CostEstimate(flops=1 << 20, bytes_accessed=1 << 20, transcendentals=0),
    )


def held(*dims, dtype=f32):
    return pltpu.VMEM(dims, dtype)


def shape(*dims):
    return jax.ShapeDtypeStruct(dims, f32)


def split(value):
    high = value.astype(bf16)
    return high, (value - high.astype(f32)).astype(bf16)


def halves(value):
    high, low = split(value)
    return jnp.concatenate(
        [jnp.concatenate([high, high], axis=1), jnp.concatenate([low, jnp.zeros_like(low)], axis=1)], axis=0
    )


def dot(left, parts, axis):
    if axis:
        height = parts.shape[0] // 2
        parts = jnp.concatenate([parts[:height, :], parts[height:, :]], axis=1)
    result = lax.dot_general(halves(left), parts, (((1,), (axis,)), ((), ())), preferred_element_type=f32)
    return result[: left.shape[0]] + result[left.shape[0] :]


def for_each(count, body, start):
    if count <= 32:
        for i in range(count):
            start = body(i, start)
        return start
    return lax.fori_loop(0, count, body, start)


def north(x):
    return pltpu.roll(x, x.shape[0] - 1, 0)


def south(x):
    return pltpu.roll(x, 1, 0)


def east(x):
    return pltpu.roll(x, x.shape[1] - 1, 1)


def west(x):
    return pltpu.roll(x, 1, 1)


def smooth(s, spread):
    for repeat in range(FILTER):
        q = spread * s
        s = s + smoothing * spread * (north(q) + south(q) + east(q) + west(q) - 4.0 * q)
    return s


def edge_block(rows):
    lane = lax.broadcasted_iota(jnp.int32, (rows.shape[0], LANES), 1)
    return jnp.where(lane < LANES // 2, rows[:, :LANES], rows[:, rows.shape[1] - LANES :])


def blend(weights, own, others, layer):
    layers = own.shape[0]
    total = None
    for i, source in enumerate([own] + list(others)):
        for m in range(layers):
            at = layer * layers * (1 + len(others)) + i * layers + m
            term = weights[at : at + 1, 0:1] * source[m]
            total = term if total is None else total + term
    return total


def parts_of(block, rows, per):
    block_row = jnp.floor((block + 0.5) / per)
    layer = jnp.floor((block_row + 0.5) / rows)
    return layer, block_row - layer * rows, block - block_row * per


def load_kernel(
    vertical, blocks, control, spread, wind_e, wind_n, scale, previous, innovation,
    platforms, counts,
    forth, back, control_v, spread_v, wind_e_v, wind_n_v, scale_v, previous_v, innovation_v,
    places, platforms_v, counts_v, lon_out, first, last, vertical_s, blocks_s, sems,
):
    pairs = (
        (spread, spread_v), (wind_e, wind_e_v), (wind_n, wind_n_v), (scale, scale_v), (blocks, blocks_s),
        (vertical, vertical_s), (control, control_v),
        (innovation, innovation_v), (previous, previous_v), (platforms, platforms_v),
        (counts, counts_v),
    )
    copies = [pltpu.make_async_copy(a, b, sems.at[i]) for i, (a, b) in enumerate(pairs)]
    for copy in copies:
        copy.start()
    layers, rows, cols = control.shape
    slots, owners = blocks.shape
    for copy in copies[:5]:
        copy.wait()
    line = lax.broadcasted_iota(jnp.int32, (1, LANES), 1)
    numbers = jnp.full((1, LANES), -1.0, f32)
    for s in range(slots):
        for o in range(owners):
            numbers = jnp.where(line == s * owners + o, blocks_s[s, o].astype(f32), numbers)
    layer, row, col = parts_of(numbers, rows, cols // LANES)
    places[...] = ((layer * (cols // LANES) + col) * (rows + 8) + row).astype(jnp.int32)
    lane = lax.broadcasted_iota(jnp.int32, (rows, LANES), 1)
    packed = jnp.zeros((rows, LANES), f32)
    fields = (spread_v, wind_e_v, wind_n_v, scale_v)
    for i, field in enumerate(fields):
        for l in range(layers):
            packed = lon_item(packed, field[l], (1 + i) * layers + l, lane)
    lon_out[:rows, :] = packed
    lon_out[rows:, :] = jnp.broadcast_to(numbers, (8, LANES))
    for out, low in ((first, True), (last, False)):
        at = WIDTHS[0] * layers
        for field, width in zip(fields, WIDTHS[1:]):
            for l in range(layers):
                begin = 0 if low else rows - width
                out[at : at + width, :] = field[l, begin : begin + width, :]
                at += width
        for c in range(0, cols, LANES):
            out[at:, c : c + LANES] = jnp.broadcast_to(numbers, (out.shape[0] - at, LANES))
    for copy in copies[5:]:
        copy.wait()
    lev, levs = lax.axis_index("lev"), lax.axis_size("lev")
    for l in range(layers):
        for shift in range(levs):
            other = lax.rem(lev + levs - shift, levs)
            for m in range(layers):
                at = (l * levs + shift) * layers + m
                a, b = lev * layers + l, other * layers + m
                forth[at : at + 1, :] = jnp.full((1, LANES), vertical_s[a, b], f32)
                back[at : at + 1, :] = jnp.full((1, LANES), vertical_s[b, a], f32)


def lon_item(packed, field, item, lane):
    cols = field.shape[1]
    tile = jnp.where(lane < LANES // 2, field[:, :LANES], field[:, cols - LANES :])
    if item:
        tile = pltpu.roll(tile, 8 * item, 1)
    return jnp.where((lane + HALO - 8 * item) % LANES < 8, tile, packed)


def pack_kernel(n_other, *refs):
    forth, control, lon_part, first, last = refs[:5]
    others = refs[5 : 5 + n_other]
    blended, lon_out, lat_1, lat_2, diag_1, diag_2 = refs[5 + n_other :]
    layers, rows, cols = control.shape
    packed = lon_part[:rows, :]
    lane = lax.broadcasted_iota(jnp.int32, (rows, LANES), 1)
    firsts, lasts = [], []
    for l in range(layers):
        value = blend(forth, control, others, l)
        blended[l] = value
        packed = lon_item(packed, value, l, lane)
        firsts.append(value[:HALO, :])
        lasts.append(value[rows - HALO :, :])
    lon_out[:rows, :] = packed
    lon_out[rows:, :] = lon_part[rows:, :]
    even = lax.axis_index("lat") % 2 == 0
    for out, diag, use_last in ((lat_1, diag_1, even), (lat_2, diag_2, jnp.logical_not(even))):
        begin = HALO * layers
        flag = jnp.where(use_last, 1, 0)
        for l in range(layers):
            chosen = jnp.full((HALO, cols), flag, jnp.int32) == 1
            out[HALO * l : HALO * (l + 1), :] = jnp.where(chosen, lasts[l], firsts[l])
        chosen = jnp.full((first.shape[0] - begin, cols), flag, jnp.int32) == 1
        out[begin:, :] = jnp.where(chosen, last[begin:, :], first[begin:, :])
        diag[...] = edge_block(out[...])


def extend_kernel(*refs):
    half = len(refs) // 2
    for field, out in zip(refs[:half], refs[half:]):
        layers, rows, cols = field.shape
        for l in range(layers):
            out[l, :rows, :cols] = field[l]
            out[l, rows:, :] = jnp.zeros((8, cols + LANES), f32)


def parts_kernel(matrices, out):
    count, height = matrices.shape[:2]

    def body(i, carry):
        out[i, :height, :], out[i, height:, :] = split(matrices[i])
        return carry

    for_each(count, body, 0)


def at_ends():
    lat = lax.axis_index("lat")
    return lat == 0, lat == lax.axis_size("lat") - 1


def unpack(lon_in, lat_1, lat_2, diag_1, diag_2, ext):
    layers, rows, cols = ext[0].shape[0], ext[0].shape[1] - 8, ext[0].shape[2] - LANES
    lane = lax.broadcasted_iota(jnp.int32, (rows, LANES), 1)
    keep = (lane < HALO) | (lane >= LANES - HALO)
    packed = lon_in[:rows, :]
    item = 0
    for out in ext:
        for l in range(layers):
            tile = pltpu.roll(packed, LANES - 8 * item, 1) if item else packed
            out[l, :rows, cols:] = jnp.where(keep, tile, 0.0)
            item += 1
    count = sum(WIDTHS) * layers
    for one, two, begin in ((lat_1, lat_2, 0), (diag_1, diag_2, cols)):
        width = one.shape[1]
        a, b = one[:count, :], two[:count, :]
        even = jnp.full(a.shape, lax.axis_index("lat") % 2, jnp.int32) == 0
        south_end, north_end = at_ends()
        top = jnp.full(a.shape, jnp.where(north_end, 1, 0), jnp.int32) == 0
        bottom = jnp.full(a.shape, jnp.where(south_end, 1, 0), jnp.int32) == 0
        if begin:
            lane_d = lax.broadcasted_iota(jnp.int32, a.shape, 1)
            inside = (lane_d < HALO) | (lane_d >= LANES - HALO)
            top = top & inside
            bottom = bottom & inside
        from_north = jnp.where(top, jnp.where(even, a, b), 0.0)
        from_south = jnp.where(bottom, jnp.where(even, b, a), 0.0)
        at = 0
        for out, l, w in [(e, l, w) for e, w in zip(ext, WIDTHS) for l in range(layers)]:
            out[l, rows : rows + w, begin : begin + width] = from_north[at : at + w, :]
            out[l, rows + 8 - w : rows + 8, begin : begin + width] = from_south[at : at + w, :]
            at += w


def inside_mask(ext_shape):
    south_end, north_end = at_ends()
    row = lax.broadcasted_iota(jnp.int32, ext_shape, 0)
    rows = ext_shape[0] - 8
    north_cut = jnp.where(north_end, rows, rows + 8)
    south_cut = jnp.where(south_end, rows + 4, rows + 8)
    cut = ((row >= north_cut) & (row < rows + 4)) | (row >= south_cut)
    return jnp.where(cut, 0.0, 1.0).astype(f32)


def forward_kernel(
    places, platforms, counts, mixed_in, spread_in, wind_e_in, wind_n_in, scale_in,
    lon_in, lat_1, lat_2, diag_1, diag_2, interp, innovation,
    sent, mixed, spread, wind_e, wind_n, scale,
    field, places_s, platforms_s, counts_s, sems,
):
    pairs = ((places, places_s), (platforms, platforms_s), (counts, counts_s))
    copies = [pltpu.make_async_copy(a, b, sems.at[i]) for i, (a, b) in enumerate(pairs)]
    for copy in copies:
        copy.start()
    unpack(lon_in, lat_1, lat_2, diag_1, diag_2, (mixed, spread, wind_e, wind_n, scale))
    layers, ext_rows, ext_cols = mixed.shape
    per = ext_cols // LANES - 1
    mask = inside_mask((ext_rows, ext_cols))
    for l in range(layers):
        x = scale[l] * smooth(mixed[l], spread[l])
        u, v = 0.5 * wind_e[l], 0.5 * wind_n[l]
        for step in range(STEPS):
            if step:
                x = x * mask
            x = (
                (1.0 - 4.0 * diffusion) * x
                + (diffusion - u) * east(x)
                + (diffusion + u) * west(x)
                + (diffusion - v) * north(x)
                + (diffusion + v) * south(x)
            )
        for c in range(per):
            begin = (l * per + c) * ext_rows
            field[begin : begin + ext_rows, :] = x[:, c * LANES : (c + 1) * LANES]
    for copy in copies:
        copy.wait()
    count, width = innovation.shape
    slots, owners = platforms.shape
    row = lax.broadcasted_iota(jnp.int32, (count, width), 0)

    def body(b, total):
        at = places_s[0, (b % slots) * owners + b // slots]
        left = jnp.where(row == b, jnp.broadcast_to(field[pl.ds(at, 1), :], (count, width)), 0.0)
        return total + dot(left, interp[b], 1)

    departure = for_each(count, body, jnp.zeros((count, width), f32)) - innovation[...]
    half = sent.shape[1] // 2
    sent[...] = jnp.zeros(sent.shape, f32)
    for o in range(owners):
        for s in range(slots):
            live = jnp.full((1, width), counts_s[0, o], jnp.int32) > s
            b = o * slots + s
            sent[o, s : s + 1, :] = jnp.where(live, departure[b : b + 1, :], 0.0)
            sent[o, half + s : half + s + 1, :] = jnp.full((1, width), platforms_s[s, o].astype(f32), f32)


def weigh_kernel(slots, arrived, matrices, out, values, platform):
    tiles, height, width = arrived.shape
    for t in range(tiles):
        for s in range(slots):
            at = s * tiles + t
            values[at : at + 1, :] = arrived[t, s : s + 1, :]
            platform[at : at + 1, :] = arrived[t, height // 2 + s : height // 2 + s + 1, :]
    x, where = values[...], platform[...]
    total = jnp.zeros(x.shape, f32)
    for p in range(matrices.shape[0]):
        total = total + dot(jnp.where(where == float(p), x, 0.0), jnp.concatenate(split(matrices[p]), axis=0), 1)
    out[...] = jnp.zeros(out.shape, f32)
    for t in range(tiles):
        for s in range(slots):
            at = s * tiles + t
            out[t, s : s + 1, :] = total[at : at + 1, :]


def transpose_kernel(slots, returned, interp, out):
    count, width = out.shape
    row = lax.broadcasted_iota(jnp.int32, (count, width), 0)

    def body(b, total):
        owner, slot = b // slots, b % slots
        weighted = returned[owner, pl.ds(slot, 1), :]
        left = jnp.where(
            row == slot * (count // slots) + owner, jnp.broadcast_to(weighted, (count, width)), 0.0
        )
        return total + dot(left, interp[b], 0)

    out[...] = for_each(count, body, jnp.zeros((count, width), f32))


def place_kernel(count, kinds, rows, layers, per, *refs):
    tiles, square, out, square_out = refs[:-3], refs[-3], refs[-2], refs[-1]
    square_out[...] = jnp.full((1, LANES), square[0], f32)
    line = lax.broadcasted_iota(jnp.int32, (1, LANES), 1)
    south_end, north_end = at_ends()
    odd = lax.axis_index("lat") % 2
    packs = -(-len(kinds) * count // LANES)
    targets = [jnp.full((1, LANES), -1.0, f32) for _ in range(packs)]
    for i, (tile, (phase, lon_step, begin)) in enumerate(zip(tiles, kinds)):
        block = tile[begin : begin + 1, :LANES]
        layer, row, col = parts_of(block, rows, per)
        valid = block >= 0.0
        if phase:
            is_north = jnp.where(odd == phase - 1, 1, 0)
            usable = jnp.where(is_north == 1, jnp.where(north_end, 0, 1), jnp.where(south_end, 0, 1))
            is_north = jnp.full((1, LANES), is_north, jnp.int32) == 1
            usable = jnp.full((1, LANES), usable, jnp.int32) == 1
            valid = valid & usable
            valid = valid & ((is_north & (row < HALO)) | (jnp.logical_not(is_north) & (row >= rows - HALO)))
            row = jnp.where(is_north, row + rows, row + 8)
        if lon_step:
            at_first, at_last = col == 0.0, col == per - 1.0
            both = at_first | at_last
            if lon_step == 1:
                both = at_first
            if lon_step == -1:
                both = at_last
            valid = valid & both
            col = jnp.where(at_first, float(per), float(per + 1))
        place = jnp.where(valid, (layer * (per + 2) + col) * (rows + 8) + row, -1.0)
        pack, shift = divmod(i * count, LANES)
        if shift:
            place = pltpu.roll(place, shift, 1)
        mine = (line >= shift) & (line < shift + count)
        targets[pack] = jnp.where(mine, place, targets[pack])
    places = out.shape[0]
    index = lax.broadcasted_iota(jnp.int32, (places, LANES), 0)
    for pack, target in enumerate(targets):
        chosen = jnp.where(index == target.astype(jnp.int32), 1.0, 0.0).astype(bf16)
        out[:, pack * LANES : (pack + 1) * LANES] = chosen
        out[:, (packs + pack) * LANES : (packs + pack + 1) * LANES] = chosen


def adjoint_kernel(n_source, *refs):
    chosen = refs[0]
    sources = refs[1 : 1 + n_source]
    spread, scale, wind_e, wind_n = refs[1 + n_source : 5 + n_source]
    filtered, = refs[5 + n_source :]
    layers, ext_rows, ext_cols = spread.shape
    rows, cols = filtered.shape[1:]
    values = [s[...] for s in sources]
    spare = chosen.shape[1] // 2 - sum(v.shape[0] for v in values)
    if spare:
        values.append(jnp.zeros((spare, LANES), f32))
    parts = jnp.concatenate(split(jnp.concatenate(values, axis=0)), axis=0)
    forcing = lax.dot_general(chosen[...], parts, NN, preferred_element_type=f32)
    mask = inside_mask((ext_rows, ext_cols))
    lane = lax.broadcasted_iota(jnp.int32, (ext_rows, LANES), 1)
    per = cols // LANES
    for l in range(layers):
        begin = l * (per + 2) * ext_rows
        tiles = [forcing[begin + c * ext_rows : begin + (c + 1) * ext_rows, :] for c in range(per + 2)]
        y = jnp.concatenate(tiles[:per] + [jnp.where(lane < LANES // 2, tiles[per], tiles[per + 1])], axis=1)
        u, v = 0.5 * wind_e[l], 0.5 * wind_n[l]
        for step in range(STEPS):
            if step:
                y = y * mask
            y = (
                (1.0 - 4.0 * diffusion) * y
                + east((diffusion + u) * y)
                + west((diffusion - u) * y)
                + north((diffusion + v) * y)
                + south((diffusion - v) * y)
            )
        s = smooth(scale[l] * y, spread[l])
        filtered[l] = s[:rows, :cols]


def gradient_kernel(n_other, *refs):
    back, control, filtered = refs[:3]
    others = refs[3 : 3 + n_other]
    gradient, partial = refs[3 + n_other :]
    layers, rows, cols = control.shape
    total = jnp.zeros((8, LANES), f32)
    for m in range(layers):
        g = control[m] + blend(back, filtered, others, m)
        gradient[m] = g
        square = g * g
        for r in range(0, rows, 8):
            for c in range(0, cols, LANES):
                total = total + square[r : r + 8, c : c + LANES]
    total = jnp.sum(total, axis=0, keepdims=True)
    partial[...] = jnp.broadcast_to(total[None], partial.shape)


def direction_kernel(cell_count, gradient, sums, previous, previous_square, direction):
    total = jnp.sum(jnp.sum(sums[...], axis=0), axis=1, keepdims=True)
    factor = total / cell_count / previous_square[:, 0:1]
    for l in range(gradient.shape[0]):
        direction[l] = factor * previous[l] - gradient[l]


def local(
    control,
    vertical,
    spread,
    error_scale,
    wind_lon,
    wind_lat,
    obs_block,
    obs_platform,
    obs_count,
    interp,
    innovation,
    error_inverse,
    previous_direction,
    previous_square,
):
    n_lat, n_lon, n_lev = (lax.axis_size(a) for a in ("lat", "lon", "lev"))
    layers, rows, cols = control.shape
    ext_rows, ext_cols = rows + 8, cols + LANES
    owners = obs_count.shape[-1]
    slots = obs_block.shape[-1]
    width = interp.shape[-1]
    count = owners * slots
    blocks = obs_block.reshape(owners, slots).T
    platforms = obs_platform.reshape(owners, slots).T
    counts = obs_count.reshape(1, owners)
    weights = interp.reshape(count, width, width)
    limit = (8 << 20) + 3 * weights.size * 4
    per = cols // LANES
    lat_fields = sum(WIDTHS) * layers
    lat_rows = lat_fields // 8 * 8 + 8

    def from_levs(field):
        return [
            lax.ppermute(field, "lev", [(i, (i + k) % n_lev) for i in range(n_lev)]) for k in range(1, n_lev)
        ]

    def partner(a, phase):
        step = 1 if (a % 2 == 0) == (phase == 1) else -1
        return (a + step) % n_lat

    def exchange(field, phase, lon_step):
        pairs = []
        for a in range(n_lat):
            for b in range(n_lon):
                to = partner(a, phase) if phase else a
                pairs.append((a * n_lon + b, to * n_lon + (b + lon_step) % n_lon))
        return lax.ppermute(field, ("lat", "lon"), pairs)

    lon_steps = (2,) if n_lon == 2 else (1, -1)

    def from_lon(field, phase, step):
        return exchange(field, phase, 1 if step == 2 else -step)

    others = from_levs(control)
    field = held(layers, rows, cols)
    mix = held(layers * layers * n_lev, LANES)
    innovations = innovation.reshape(count, width)
    (
        forth, back, control_v, spread_v, wind_e_v, wind_n_v, scale_v, previous_v, innovation_v,
        places, platforms_v, counts_v, lon_part, first, last,
    ) = call(
        load_kernel,
        [mix, mix] + [field] * 6 + [held(count, width)]
        + [held(1, LANES, dtype=jnp.int32)]
        + [held(*x.shape, dtype=jnp.int32) for x in (platforms, counts)]
        + [held(rows + 8, LANES), held(lat_rows, cols), held(lat_rows, cols)],
        [HBM] * 11,
        [
            pltpu.SMEM(vertical.shape, f32),
            pltpu.SMEM(blocks.shape, jnp.int32),
            pltpu.SemaphoreType.DMA((11,)),
        ],
        58 << 20,
    )(
        vertical, blocks, control, spread, wind_lon, wind_lat, error_scale, previous_direction,
        innovations, platforms, counts,
    )
    blended, lon_out, lat_1, lat_2, diag_1, diag_2 = call(
        functools.partial(pack_kernel, len(others)),
        [field, held(rows + 8, LANES)] + [held(lat_rows, cols)] * 2 + [held(lat_rows, LANES)] * 2,
        [VMEM] * (5 + len(others)),
    )(forth, control_v, lon_part, first, last, *others)

    lane = jnp.arange(LANES, dtype=jnp.int32)
    lat_in = {phase: exchange(out, phase, 0) for phase, out in ((1, lat_1), (2, lat_2))}
    lon_raw = {step: from_lon(lon_out, 0, step) for step in lon_steps}
    diag_raw = {
        (phase, step): from_lon(out, phase, step)
        for phase, out in ((1, diag_1), (2, diag_2))
        for step in lon_steps
    }
    if n_lon == 2:
        lon_in = lon_raw[2]
        diag_in = {phase: diag_raw[phase, 2] for phase in (1, 2)}
    else:
        lon_in = jnp.where(lane % 8 < HALO, lon_raw[1], lon_raw[-1])
        diag_in = {
            phase: jnp.where(lane < LANES // 2, diag_raw[phase, 1], diag_raw[phase, -1]) for phase in (1, 2)
        }

    half = -(-slots // 4) * 4
    ext = held(layers, ext_rows, ext_cols)
    exts = call(extend_kernel, [ext] * 5, [VMEM] * 5)(blended, spread_v, wind_e_v, wind_n_v, scale_v)
    matrices = error_inverse.reshape(error_inverse.shape[-3:])
    weights = call(parts_kernel, held(count, 2 * width, width, dtype=bf16), [VMEM], (), limit)(weights)
    sent, _, ext_spread, ext_e, ext_n, ext_scale = call(
        forward_kernel,
        [held(owners, 2 * half, width)] + [ext] * 5,
        [VMEM] * 15,
        [
            pltpu.VMEM((layers * ext_rows * per, LANES), f32),
            pltpu.SMEM((1, LANES), jnp.int32),
            pltpu.SMEM(blocks.shape, jnp.int32),
            pltpu.SMEM(counts.shape, jnp.int32),
            pltpu.SemaphoreType.DMA((3,)),
        ],
        limit,
        {3 + i: 1 + i for i in range(5)},
    )(
        places, platforms_v, counts_v, *exts, lon_in, lat_in[1], lat_in[2], diag_in[1], diag_in[2], weights, innovation_v,
    )

    arrived = lax.all_to_all(sent, ("lat", "lon"), split_axis=0, concat_axis=0, tiled=True)
    result = call(
        functools.partial(weigh_kernel, slots),
        held(owners, 2 * half, width),
        [VMEM] * 2,
        [pltpu.VMEM((count, width), f32)] * 2,
    )(arrived, matrices)
    returned = lax.all_to_all(result, ("lat", "lon"), split_axis=0, concat_axis=0, tiled=True)
    adjoint_obs = call(
        functools.partial(transpose_kernel, slots), shape(count, width), [VMEM] * 2, (), limit
    )(returned, weights)

    sources, tiles, kinds = [adjoint_obs], [lon_out], [(0, 0, rows)]
    for step in lon_steps:
        sources.append(from_lon(adjoint_obs, 0, step))
        tiles.append(lon_raw[step])
        kinds.append((0, step, rows))
    for phase in (1, 2):
        sources.append(exchange(adjoint_obs, phase, 0))
        tiles.append(lat_in[phase])
        kinds.append((phase, 0, lat_fields))
        for step in lon_steps:
            sources.append(from_lon(adjoint_obs, phase, step))
            tiles.append(diag_raw[phase, step])
            kinds.append((phase, step, lat_fields))
    depth = -(-len(kinds) * count // LANES) * LANES
    chosen, square_v = call(
        functools.partial(place_kernel, count, kinds, rows, layers, per),
        [held(layers * (per + 2) * ext_rows, 2 * depth, dtype=bf16), held(1, LANES)],
        [VMEM] * len(tiles) + [SMEM],
        (),
        limit,
    )(*tiles, previous_square)
    filtered = call(
        functools.partial(adjoint_kernel, len(sources)),
        shape(layers, rows, cols),
        [VMEM] * (5 + len(sources)),
        (),
        limit,
    )(chosen, *sources, ext_spread, ext_scale, ext_e, ext_n)

    others = from_levs(filtered)
    group = n_lat * n_lon * n_lev
    gradient, partial = call(
        functools.partial(gradient_kernel, len(others)),
        [field, shape(group, 1, LANES)],
        [VMEM] * (3 + len(others)),
    )(back, control_v, filtered, *others)
    sums = lax.all_to_all(partial, ("lat", "lon", "lev"), split_axis=0, concat_axis=0, tiled=True)
    direction = call(
        functools.partial(direction_kernel, float(control.size * group)),
        shape(layers, rows, cols),
        [VMEM] * 4,
    )(gradient, sums, previous_v, square_v)
    return (gradient, direction)


def solution(mesh):
    field = P("lev", ("member", "lat"), "lon")
    shared = P("lev", "lat", "lon")
    placed = (
        field,
        P(),
        shared,
        shared,
        field,
        field,
        P("lev", "lat", "lon", None, None),
        P("lev", "lat", "lon", None, None),
        P("lev", "lat", "lon", None),
        P("lev", "lat", "lon", None, None, None, None),
        P("lev", ("member", "lat"), "lon", None, None, None),
        P("lat", "lon", None, None, None),
        field,
        P("member"),
    )
    return jax.shard_map(local, mesh=mesh, in_specs=placed, out_specs=(field, field), check_vma=False)
```

```python
import functools
import jax
import jax.numpy as jnp
from jax import lax
from jax.experimental import pallas as pl
from jax.experimental.pallas import tpu as pltpu
from jax.sharding import PartitionSpec as P

FILTER = 2
STEPS = 2
HALO = 4
WIDTHS = (4, 4, 4, 4, 2)
LANES = 128
smoothing = 0.1
diffusion = 0.15
f32 = jnp.float32
bf16 = jnp.bfloat16
VMEM = pl.BlockSpec(memory_space=pltpu.VMEM)
SMEM = pl.BlockSpec(memory_space=pltpu.SMEM)
HBM = pl.BlockSpec(memory_space=pltpu.HBM)
NN = (((1,), (0,)), ((), ()))


def call(kernel, out_shape, in_specs, scratch=(), limit=8 << 20, aliases=None):
    many = isinstance(out_shape, (list, tuple))
    return pl.pallas_call(
        kernel,
        out_shape=out_shape,
        in_specs=in_specs,
        out_specs=[VMEM] * len(out_shape) if many else VMEM,
        scratch_shapes=list(scratch),
        input_output_aliases=aliases or {},
        compiler_params=pltpu.CompilerParams(vmem_limit_bytes=limit),
        cost_estimate=pl.CostEstimate(flops=1 << 20, bytes_accessed=1 << 20, transcendentals=0),
    )


def held(*dims, dtype=f32):
    return pltpu.VMEM(dims, dtype)


def shape(*dims):
    return jax.ShapeDtypeStruct(dims, f32)


def split(value):
    high = value.astype(bf16)
    return high, (value - high.astype(f32)).astype(bf16)


def halves(value):
    high, low = split(value)
    return jnp.concatenate(
        [jnp.concatenate([high, high], axis=1), jnp.concatenate([low, jnp.zeros_like(low)], axis=1)], axis=0
    )


def dot(left, parts, axis):
    if axis:
        height = parts.shape[0] // 2
        parts = jnp.concatenate([parts[:height, :], parts[height:, :]], axis=1)
    result = lax.dot_general(halves(left), parts, (((1,), (axis,)), ((), ())), preferred_element_type=f32)
    return result[: left.shape[0]] + result[left.shape[0] :]


def for_each(count, body, start):
    if count <= 32:
        for i in range(count):
            start = body(i, start)
        return start
    return lax.fori_loop(0, count, body, start)


def north(x):
    return pltpu.roll(x, x.shape[0] - 1, 0)


def south(x):
    return pltpu.roll(x, 1, 0)


def east(x):
    return pltpu.roll(x, x.shape[1] - 1, 1)


def west(x):
    return pltpu.roll(x, 1, 1)


def smooth(s, spread):
    for repeat in range(FILTER):
        q = spread * s
        s = s + smoothing * spread * (north(q) + south(q) + east(q) + west(q) - 4.0 * q)
    return s


def edge_block(rows):
    lane = lax.broadcasted_iota(jnp.int32, (rows.shape[0], LANES), 1)
    return jnp.where(lane < LANES // 2, rows[:, :LANES], rows[:, rows.shape[1] - LANES :])


def blend(weights, own, others, layer):
    layers = own.shape[0]
    total = None
    for i, source in enumerate([own] + list(others)):
        for m in range(layers):
            at = layer * layers * (1 + len(others)) + i * layers + m
            term = weights[at : at + 1, 0:1] * source[m]
            total = term if total is None else total + term
    return total


def parts_of(block, rows, per):
    block_row = jnp.floor((block + 0.5) / per)
    layer = jnp.floor((block_row + 0.5) / rows)
    return layer, block_row - layer * rows, block - block_row * per


def load_kernel(
    vertical, blocks, control, spread, wind_e, wind_n, scale, previous, innovation,
    platforms, counts,
    forth, back, control_v, spread_v, wind_e_v, wind_n_v, scale_v, previous_v, innovation_v,
    places, platforms_v, counts_v, lon_out, first, last, vertical_s, blocks_s, sems,
):
    pairs = (
        (spread, spread_v), (wind_e, wind_e_v), (wind_n, wind_n_v), (scale, scale_v), (blocks, blocks_s),
        (vertical, vertical_s), (control, control_v),
        (innovation, innovation_v), (previous, previous_v), (platforms, platforms_v),
        (counts, counts_v),
    )
    copies = [pltpu.make_async_copy(a, b, sems.at[i]) for i, (a, b) in enumerate(pairs)]
    for copy in copies:
        copy.start()
    layers, rows, cols = control.shape
    slots, owners = blocks.shape
    for copy in copies[:5]:
        copy.wait()
    line = lax.broadcasted_iota(jnp.int32, (1, LANES), 1)
    numbers = jnp.full((1, LANES), -1.0, f32)
    for s in range(slots):
        for o in range(owners):
            numbers = jnp.where(line == s * owners + o, blocks_s[s, o].astype(f32), numbers)
    layer, row, col = parts_of(numbers, rows, cols // LANES)
    places[...] = ((layer * (cols // LANES) + col) * (rows + 8) + row).astype(jnp.int32)
    lane = lax.broadcasted_iota(jnp.int32, (rows, LANES), 1)
    packed = jnp.zeros((rows, LANES), f32)
    fields = (spread_v, wind_e_v, wind_n_v, scale_v)
    for i, field in enumerate(fields):
        for l in range(layers):
            packed = lon_item(packed, field[l], (1 + i) * layers + l, lane)
    lon_out[:rows, :] = packed
    lon_out[rows:, :] = jnp.broadcast_to(numbers, (8, LANES))
    for out, low in ((first, True), (last, False)):
        at = WIDTHS[0] * layers
        for field, width in zip(fields, WIDTHS[1:]):
            for l in range(layers):
                begin = 0 if low else rows - width
                out[at : at + width, :] = field[l, begin : begin + width, :]
                at += width
        for c in range(0, cols, LANES):
            out[at:, c : c + LANES] = jnp.broadcast_to(numbers, (out.shape[0] - at, LANES))
    for copy in copies[5:]:
        copy.wait()
    lev, levs = lax.axis_index("lev"), lax.axis_size("lev")
    for l in range(layers):
        for shift in range(levs):
            other = lax.rem(lev + levs - shift, levs)
            for m in range(layers):
                at = (l * levs + shift) * layers + m
                a, b = lev * layers + l, other * layers + m
                forth[at : at + 1, :] = jnp.full((1, LANES), vertical_s[a, b], f32)
                back[at : at + 1, :] = jnp.full((1, LANES), vertical_s[b, a], f32)


def lon_item(packed, field, item, lane):
    cols = field.shape[1]
    tile = jnp.where(lane < LANES // 2, field[:, :LANES], field[:, cols - LANES :])
    if item:
        tile = pltpu.roll(tile, 8 * item, 1)
    return jnp.where((lane + HALO - 8 * item) % LANES < 8, tile, packed)


def pack_kernel(n_other, *refs):
    forth, control, lon_part, first, last = refs[:5]
    others = refs[5 : 5 + n_other]
    blended, lon_out, lat_1, lat_2, diag_1, diag_2 = refs[5 + n_other :]
    layers, rows, cols = control.shape
    packed = lon_part[:rows, :]
    lane = lax.broadcasted_iota(jnp.int32, (rows, LANES), 1)
    firsts, lasts = [], []
    for l in range(layers):
        value = blend(forth, control, others, l)
        blended[l] = value
        packed = lon_item(packed, value, l, lane)
        firsts.append(value[:HALO, :])
        lasts.append(value[rows - HALO :, :])
    lon_out[:rows, :] = packed
    lon_out[rows:, :] = lon_part[rows:, :]
    even = lax.axis_index("lat") % 2 == 0
    for out, diag, use_last in ((lat_1, diag_1, even), (lat_2, diag_2, jnp.logical_not(even))):
        begin = HALO * layers
        flag = jnp.where(use_last, 1, 0)
        for l in range(layers):
            chosen = jnp.full((HALO, cols), flag, jnp.int32) == 1
            out[HALO * l : HALO * (l + 1), :] = jnp.where(chosen, lasts[l], firsts[l])
        chosen = jnp.full((first.shape[0] - begin, cols), flag, jnp.int32) == 1
        out[begin:, :] = jnp.where(chosen, last[begin:, :], first[begin:, :])
        diag[...] = edge_block(out[...])


def extend_kernel(*refs):
    square, refs = refs[0], refs[1:]
    half = len(refs) // 2
    refs[-1][...] = jnp.full((1, LANES), square[0], f32)
    for field, out in zip(refs[:half], refs[half:-1]):
        layers, rows, cols = field.shape
        for l in range(layers):
            out[l, :rows, :cols] = field[l]
            out[l, rows:, :] = jnp.zeros((8, cols + LANES), f32)


def parts_kernel(matrices, out):
    count, height = matrices.shape[:2]

    def body(i, carry):
        out[i, :height, :], out[i, height:, :] = split(matrices[i])
        return carry

    for_each(count, body, 0)


def at_ends():
    lat = lax.axis_index("lat")
    return lat == 0, lat == lax.axis_size("lat") - 1


def unpack(lon_in, lat_1, lat_2, diag_1, diag_2, ext):
    layers, rows, cols = ext[0].shape[0], ext[0].shape[1] - 8, ext[0].shape[2] - LANES
    lane = lax.broadcasted_iota(jnp.int32, (rows, LANES), 1)
    keep = (lane < HALO) | (lane >= LANES - HALO)
    packed = lon_in[:rows, :]
    item = 0
    for out in ext:
        for l in range(layers):
            tile = pltpu.roll(packed, LANES - 8 * item, 1) if item else packed
            out[l, :rows, cols:] = jnp.where(keep, tile, 0.0)
            item += 1
    count = sum(WIDTHS) * layers
    for one, two, begin in ((lat_1, lat_2, 0), (diag_1, diag_2, cols)):
        width = one.shape[1]
        a, b = one[:count, :], two[:count, :]
        even = jnp.full(a.shape, lax.axis_index("lat") % 2, jnp.int32) == 0
        south_end, north_end = at_ends()
        top = jnp.full(a.shape, jnp.where(north_end, 1, 0), jnp.int32) == 0
        bottom = jnp.full(a.shape, jnp.where(south_end, 1, 0), jnp.int32) == 0
        if begin:
            lane_d = lax.broadcasted_iota(jnp.int32, a.shape, 1)
            inside = (lane_d < HALO) | (lane_d >= LANES - HALO)
            top = top & inside
            bottom = bottom & inside
        from_north = jnp.where(top, jnp.where(even, a, b), 0.0)
        from_south = jnp.where(bottom, jnp.where(even, b, a), 0.0)
        at = 0
        for out, l, w in [(e, l, w) for e, w in zip(ext, WIDTHS) for l in range(layers)]:
            out[l, rows : rows + w, begin : begin + width] = from_north[at : at + w, :]
            out[l, rows + 8 - w : rows + 8, begin : begin + width] = from_south[at : at + w, :]
            at += w


def inside_mask(ext_shape):
    south_end, north_end = at_ends()
    row = lax.broadcasted_iota(jnp.int32, ext_shape, 0)
    rows = ext_shape[0] - 8
    north_cut = jnp.where(north_end, rows, rows + 8)
    south_cut = jnp.where(south_end, rows + 4, rows + 8)
    cut = ((row >= north_cut) & (row < rows + 4)) | (row >= south_cut)
    return jnp.where(cut, 0.0, 1.0).astype(f32)


def forward_kernel(
    places, platforms, counts, mixed_in, spread_in, wind_e_in, wind_n_in, scale_in,
    lon_in, lat_1, lat_2, diag_1, diag_2, interp, innovation,
    sent, mixed, spread, wind_e, wind_n, scale,
    field, places_s, platforms_s, counts_s, sems,
):
    pairs = ((places, places_s), (platforms, platforms_s), (counts, counts_s))
    copies = [pltpu.make_async_copy(a, b, sems.at[i]) for i, (a, b) in enumerate(pairs)]
    for copy in copies:
        copy.start()
    unpack(lon_in, lat_1, lat_2, diag_1, diag_2, (mixed, spread, wind_e, wind_n, scale))
    layers, ext_rows, ext_cols = mixed.shape
    per = ext_cols // LANES - 1
    mask = inside_mask((ext_rows, ext_cols))
    for l in range(layers):
        x = scale[l] * smooth(mixed[l], spread[l])
        u, v = 0.5 * wind_e[l], 0.5 * wind_n[l]
        for step in range(STEPS):
            if step:
                x = x * mask
            x = (
                (1.0 - 4.0 * diffusion) * x
                + (diffusion - u) * east(x)
                + (diffusion + u) * west(x)
                + (diffusion - v) * north(x)
                + (diffusion + v) * south(x)
            )
        for c in range(per):
            begin = (l * per + c) * ext_rows
            field[begin : begin + ext_rows, :] = x[:, c * LANES : (c + 1) * LANES]
    for copy in copies:
        copy.wait()
    count, width = innovation.shape
    slots, owners = platforms.shape
    row = lax.broadcasted_iota(jnp.int32, (count, width), 0)

    def body(b, total):
        at = places_s[0, (b % slots) * owners + b // slots]
        left = jnp.where(row == b, jnp.broadcast_to(field[pl.ds(at, 1), :], (count, width)), 0.0)
        return total + dot(left, interp[b], 1)

    departure = for_each(count, body, jnp.zeros((count, width), f32)) - innovation[...]
    half = sent.shape[1] // 2
    sent[...] = jnp.zeros(sent.shape, f32)
    for o in range(owners):
        for s in range(slots):
            live = jnp.full((1, width), counts_s[0, o], jnp.int32) > s
            b = o * slots + s
            sent[o, s : s + 1, :] = jnp.where(live, departure[b : b + 1, :], 0.0)
            sent[o, half + s : half + s + 1, :] = jnp.full((1, width), platforms_s[s, o].astype(f32), f32)


def weigh_kernel(slots, arrived, matrices, out, values, platform):
    tiles, height, width = arrived.shape
    for t in range(tiles):
        for s in range(slots):
            at = s * tiles + t
            values[at : at + 1, :] = arrived[t, s : s + 1, :]
            platform[at : at + 1, :] = arrived[t, height // 2 + s : height // 2 + s + 1, :]
    x, where = values[...], platform[...]
    total = jnp.zeros(x.shape, f32)
    for p in range(matrices.shape[0]):
        total = total + dot(jnp.where(where == float(p), x, 0.0), jnp.concatenate(split(matrices[p]), axis=0), 1)
    out[...] = jnp.zeros(out.shape, f32)
    for t in range(tiles):
        for s in range(slots):
            at = s * tiles + t
            out[t, s : s + 1, :] = total[at : at + 1, :]


def transpose_kernel(slots, returned, interp, out):
    count, width = out.shape
    row = lax.broadcasted_iota(jnp.int32, (count, width), 0)

    def body(b, total):
        owner, slot = b // slots, b % slots
        weighted = returned[owner, pl.ds(slot, 1), :]
        left = jnp.where(
            row == slot * (count // slots) + owner, jnp.broadcast_to(weighted, (count, width)), 0.0
        )
        return total + dot(left, interp[b], 0)

    out[...] = for_each(count, body, jnp.zeros((count, width), f32))


def place_kernel(count, kinds, rows, layers, per, *refs):
    tiles, out = refs[:-1], refs[-1]
    line = lax.broadcasted_iota(jnp.int32, (1, LANES), 1)
    south_end, north_end = at_ends()
    odd = lax.axis_index("lat") % 2
    packs = -(-len(kinds) * count // LANES)
    targets = [jnp.full((1, LANES), -1.0, f32) for _ in range(packs)]
    for i, (tile, (phase, lon_step, begin)) in enumerate(zip(tiles, kinds)):
        block = tile[begin : begin + 1, :LANES]
        layer, row, col = parts_of(block, rows, per)
        valid = block >= 0.0
        if phase:
            is_north = jnp.where(odd == phase - 1, 1, 0)
            usable = jnp.where(is_north == 1, jnp.where(north_end, 0, 1), jnp.where(south_end, 0, 1))
            is_north = jnp.full((1, LANES), is_north, jnp.int32) == 1
            usable = jnp.full((1, LANES), usable, jnp.int32) == 1
            valid = valid & usable
            valid = valid & ((is_north & (row < HALO)) | (jnp.logical_not(is_north) & (row >= rows - HALO)))
            row = jnp.where(is_north, row + rows, row + 8)
        if lon_step:
            at_first, at_last = col == 0.0, col == per - 1.0
            both = at_first | at_last
            if lon_step == 1:
                both = at_first
            if lon_step == -1:
                both = at_last
            valid = valid & both
            col = jnp.where(at_first, float(per), float(per + 1))
        place = jnp.where(valid, (layer * (per + 2) + col) * (rows + 8) + row, -1.0)
        pack, shift = divmod(i * count, LANES)
        if shift:
            place = pltpu.roll(place, shift, 1)
        mine = (line >= shift) & (line < shift + count)
        targets[pack] = jnp.where(mine, place, targets[pack])
    places = out.shape[0]
    index = lax.broadcasted_iota(jnp.int32, (places, LANES), 0)
    for pack, target in enumerate(targets):
        chosen = jnp.where(index == target.astype(jnp.int32), 1.0, 0.0).astype(bf16)
        out[:, pack * LANES : (pack + 1) * LANES] = chosen
        out[:, (packs + pack) * LANES : (packs + pack + 1) * LANES] = chosen


def adjoint_kernel(n_source, *refs):
    chosen = refs[0]
    sources = refs[1 : 1 + n_source]
    spread, scale, wind_e, wind_n = refs[1 + n_source : 5 + n_source]
    filtered, = refs[5 + n_source :]
    layers, ext_rows, ext_cols = spread.shape
    rows, cols = filtered.shape[1:]
    values = [s[...] for s in sources]
    spare = chosen.shape[1] // 2 - sum(v.shape[0] for v in values)
    if spare:
        values.append(jnp.zeros((spare, LANES), f32))
    parts = jnp.concatenate(split(jnp.concatenate(values, axis=0)), axis=0)
    forcing = lax.dot_general(chosen[...], parts, NN, preferred_element_type=f32)
    mask = inside_mask((ext_rows, ext_cols))
    lane = lax.broadcasted_iota(jnp.int32, (ext_rows, LANES), 1)
    per = cols // LANES
    for l in range(layers):
        begin = l * (per + 2) * ext_rows
        tiles = [forcing[begin + c * ext_rows : begin + (c + 1) * ext_rows, :] for c in range(per + 2)]
        y = jnp.concatenate(tiles[:per] + [jnp.where(lane < LANES // 2, tiles[per], tiles[per + 1])], axis=1)
        u, v = 0.5 * wind_e[l], 0.5 * wind_n[l]
        for step in range(STEPS):
            if step:
                y = y * mask
            y = (
                (1.0 - 4.0 * diffusion) * y
                + east((diffusion + u) * y)
                + west((diffusion - u) * y)
                + north((diffusion + v) * y)
                + south((diffusion - v) * y)
            )
        s = smooth(scale[l] * y, spread[l])
        filtered[l] = s[:rows, :cols]


def gradient_kernel(n_other, *refs):
    back, control, filtered = refs[:3]
    others = refs[3 : 3 + n_other]
    gradient, partial = refs[3 + n_other :]
    layers, rows, cols = control.shape
    total = jnp.zeros((8, LANES), f32)
    for m in range(layers):
        g = control[m] + blend(back, filtered, others, m)
        gradient[m] = g
        square = g * g
        for r in range(0, rows, 8):
            for c in range(0, cols, LANES):
                total = total + square[r : r + 8, c : c + LANES]
    total = jnp.sum(total, axis=0, keepdims=True)
    partial[...] = jnp.broadcast_to(total[None], partial.shape)


def direction_kernel(cell_count, gradient_in, sums, previous, previous_square, gradient, direction):
    total = jnp.sum(jnp.sum(sums[...], axis=0), axis=1, keepdims=True)
    factor = total / cell_count / previous_square[:, 0:1]
    for l in range(gradient.shape[0]):
        gradient[l] = gradient_in[l]
        direction[l] = factor * previous[l] - gradient_in[l]


def local(
    control,
    vertical,
    spread,
    error_scale,
    wind_lon,
    wind_lat,
    obs_block,
    obs_platform,
    obs_count,
    interp,
    innovation,
    error_inverse,
    previous_direction,
    previous_square,
):
    n_lat, n_lon, n_lev = (lax.axis_size(a) for a in ("lat", "lon", "lev"))
    layers, rows, cols = control.shape
    ext_rows, ext_cols = rows + 8, cols + LANES
    owners = obs_count.shape[-1]
    slots = obs_block.shape[-1]
    width = interp.shape[-1]
    count = owners * slots
    blocks = obs_block.reshape(owners, slots).T
    platforms = obs_platform.reshape(owners, slots).T
    counts = obs_count.reshape(1, owners)
    weights = interp.reshape(count, width, width)
    limit = (8 << 20) + 3 * weights.size * 4
    per = cols // LANES
    lat_fields = sum(WIDTHS) * layers
    lat_rows = lat_fields // 8 * 8 + 8

    def from_levs(field):
        return [
            lax.ppermute(field, "lev", [(i, (i + k) % n_lev) for i in range(n_lev)]) for k in range(1, n_lev)
        ]

    def partner(a, phase):
        to = a + (1 if (a % 2 == 0) == (phase == 1) else -1)
        return to if 0 <= to < n_lat else a

    def exchange(field, phase, lon_step):
        pairs = []
        for a in range(n_lat):
            for b in range(n_lon):
                to = partner(a, phase) if phase else a
                pairs.append((a * n_lon + b, to * n_lon + (b + lon_step) % n_lon))
        return lax.ppermute(field, ("lat", "lon"), pairs)

    lon_steps = (2,) if n_lon == 2 else (1, -1)

    def from_lon(field, phase, step):
        return exchange(field, phase, 1 if step == 2 else -step)

    others = from_levs(control)
    field = held(layers, rows, cols)
    mix = held(layers * layers * n_lev, LANES)
    innovations = innovation.reshape(count, width)
    (
        forth, back, control_v, spread_v, wind_e_v, wind_n_v, scale_v, previous_v, innovation_v,
        places, platforms_v, counts_v, lon_part, first, last,
    ) = call(
        load_kernel,
        [mix, mix] + [field] * 6 + [held(count, width)]
        + [held(1, LANES, dtype=jnp.int32)]
        + [held(*x.shape, dtype=jnp.int32) for x in (platforms, counts)]
        + [held(rows + 8, LANES), held(lat_rows, cols), held(lat_rows, cols)],
        [HBM] * 11,
        [
            pltpu.SMEM(vertical.shape, f32),
            pltpu.SMEM(blocks.shape, jnp.int32),
            pltpu.SemaphoreType.DMA((11,)),
        ],
        58 << 20,
    )(
        vertical, blocks, control, spread, wind_lon, wind_lat, error_scale, previous_direction,
        innovations, platforms, counts,
    )
    blended, lon_out, lat_1, lat_2, diag_1, diag_2 = call(
        functools.partial(pack_kernel, len(others)),
        [field, held(rows + 8, LANES)] + [held(lat_rows, cols)] * 2 + [held(lat_rows, LANES)] * 2,
        [VMEM] * (5 + len(others)),
    )(forth, control_v, lon_part, first, last, *others)

    lane = jnp.arange(LANES, dtype=jnp.int32)
    lat_in = {phase: exchange(out, phase, 0) for phase, out in ((1, lat_1), (2, lat_2))}
    lon_raw = {step: from_lon(lon_out, 0, step) for step in lon_steps}
    diag_raw = {
        (phase, step): from_lon(out, phase, step)
        for phase, out in ((1, diag_1), (2, diag_2))
        for step in lon_steps
    }
    if n_lon == 2:
        lon_in = lon_raw[2]
        diag_in = {phase: diag_raw[phase, 2] for phase in (1, 2)}
    else:
        lon_in = jnp.where(lane % 8 < HALO, lon_raw[1], lon_raw[-1])
        diag_in = {
            phase: jnp.where(lane < LANES // 2, diag_raw[phase, 1], diag_raw[phase, -1]) for phase in (1, 2)
        }

    half = -(-slots // 4) * 4
    ext = held(layers, ext_rows, ext_cols)
    *exts, square_v = call(extend_kernel, [ext] * 5 + [held(1, LANES)], [SMEM] + [VMEM] * 5)(
        previous_square, blended, spread_v, wind_e_v, wind_n_v, scale_v
    )
    matrices = error_inverse.reshape(error_inverse.shape[-3:])
    weights = call(parts_kernel, held(count, 2 * width, width, dtype=bf16), [VMEM], (), limit)(weights)
    sent, _, ext_spread, ext_e, ext_n, ext_scale = call(
        forward_kernel,
        [held(owners, 2 * half, width)] + [ext] * 5,
        [VMEM] * 15,
        [
            pltpu.VMEM((layers * ext_rows * per, LANES), f32),
            pltpu.SMEM((1, LANES), jnp.int32),
            pltpu.SMEM(blocks.shape, jnp.int32),
            pltpu.SMEM(counts.shape, jnp.int32),
            pltpu.SemaphoreType.DMA((3,)),
        ],
        limit,
        {3 + i: 1 + i for i in range(5)},
    )(
        places, platforms_v, counts_v, *exts, lon_in, lat_in[1], lat_in[2], diag_in[1], diag_in[2], weights, innovation_v,
    )

    arrived = lax.all_to_all(sent, ("lat", "lon"), split_axis=0, concat_axis=0, tiled=True)
    result = call(
        functools.partial(weigh_kernel, slots),
        held(owners, 2 * half, width),
        [VMEM] * 2,
        [pltpu.VMEM((count, width), f32)] * 2,
    )(arrived, matrices)
    returned = lax.all_to_all(result, ("lat", "lon"), split_axis=0, concat_axis=0, tiled=True)
    adjoint_obs = call(
        functools.partial(transpose_kernel, slots), held(count, width), [VMEM] * 2, (), limit
    )(returned, weights)

    sources, tiles, kinds = [adjoint_obs], [lon_out], [(0, 0, rows)]
    for step in lon_steps:
        sources.append(from_lon(adjoint_obs, 0, step))
        tiles.append(lon_raw[step])
        kinds.append((0, step, rows))
    for phase in (1, 2):
        sources.append(exchange(adjoint_obs, phase, 0))
        tiles.append(lat_in[phase])
        kinds.append((phase, 0, lat_fields))
        for step in lon_steps:
            sources.append(from_lon(adjoint_obs, phase, step))
            tiles.append(diag_raw[phase, step])
            kinds.append((phase, step, lat_fields))
    depth = -(-len(kinds) * count // LANES) * LANES
    chosen = call(
        functools.partial(place_kernel, count, kinds, rows, layers, per),
        held(layers * (per + 2) * ext_rows, 2 * depth, dtype=bf16),
        [VMEM] * len(tiles),
        (),
        limit,
    )(*tiles)
    filtered = call(
        functools.partial(adjoint_kernel, len(sources)),
        held(layers, rows, cols),
        [VMEM] * (5 + len(sources)),
        (),
        limit,
    )(chosen, *sources, ext_spread, ext_scale, ext_e, ext_n)

    others = from_levs(filtered)
    group = n_lat * n_lon * n_lev
    gradient, partial = call(
        functools.partial(gradient_kernel, len(others)),
        [field, held(group, 1, LANES)],
        [VMEM] * (3 + len(others)),
    )(back, control_v, filtered, *others)
    sums = lax.all_to_all(partial, ("lat", "lon", "lev"), split_axis=0, concat_axis=0, tiled=True)
    gradient, direction = call(
        functools.partial(direction_kernel, float(control.size * group)),
        [shape(layers, rows, cols)] * 2,
        [VMEM] * 4,
    )(gradient, sums, previous_v, square_v)
    return (gradient, direction)


def solution(mesh):
    field = P("lev", ("member", "lat"), "lon")
    shared = P("lev", "lat", "lon")
    placed = (
        field,
        P(),
        shared,
        shared,
        field,
        field,
        P("lev", "lat", "lon", None, None),
        P("lev", "lat", "lon", None, None),
        P("lev", "lat", "lon", None),
        P("lev", "lat", "lon", None, None, None, None),
        P("lev", ("member", "lat"), "lon", None, None, None),
        P("lat", "lon", None, None, None),
        field,
        P("member"),
    )
    return jax.shard_map(local, mesh=mesh, in_specs=placed, out_specs=(field, field), check_vma=False)
```

```python
import functools
import jax
import jax.numpy as jnp
from jax import lax
from jax.experimental import pallas as pl
from jax.experimental.pallas import tpu as pltpu
from jax.sharding import PartitionSpec as P

FILTER = 2
STEPS = 2
HALO = 4
WIDTHS = (4, 4, 4, 4, 2)
LANES = 128
smoothing = 0.1
diffusion = 0.15
f32 = jnp.float32
bf16 = jnp.bfloat16
VMEM = pl.BlockSpec(memory_space=pltpu.VMEM)
SMEM = pl.BlockSpec(memory_space=pltpu.SMEM)
HBM = pl.BlockSpec(memory_space=pltpu.HBM)
NN = (((1,), (0,)), ((), ()))


def call(kernel, out_shape, in_specs, scratch=(), limit=8 << 20, aliases=None):
    many = isinstance(out_shape, (list, tuple))
    return pl.pallas_call(
        kernel,
        out_shape=out_shape,
        in_specs=in_specs,
        out_specs=[VMEM] * len(out_shape) if many else VMEM,
        scratch_shapes=list(scratch),
        input_output_aliases=aliases or {},
        compiler_params=pltpu.CompilerParams(vmem_limit_bytes=limit),
        cost_estimate=pl.CostEstimate(flops=1 << 20, bytes_accessed=1 << 20, transcendentals=0),
    )


def held(*dims, dtype=f32):
    return pltpu.VMEM(dims, dtype)


def shape(*dims):
    return jax.ShapeDtypeStruct(dims, f32)


def split(value):
    high = value.astype(bf16)
    return high, (value - high.astype(f32)).astype(bf16)


def halves(value):
    high, low = split(value)
    return jnp.concatenate(
        [jnp.concatenate([high, high], axis=1), jnp.concatenate([low, jnp.zeros_like(low)], axis=1)], axis=0
    )


def dot(left, parts, axis):
    if axis:
        height = parts.shape[0] // 2
        parts = jnp.concatenate([parts[:height, :], parts[height:, :]], axis=1)
    result = lax.dot_general(halves(left), parts, (((1,), (axis,)), ((), ())), preferred_element_type=f32)
    return result[: left.shape[0]] + result[left.shape[0] :]


def for_each(count, body, start):
    if count <= 32:
        for i in range(count):
            start = body(i, start)
        return start
    return lax.fori_loop(0, count, body, start)


def north(x):
    return pltpu.roll(x, x.shape[0] - 1, 0)


def south(x):
    return pltpu.roll(x, 1, 0)


def east(x):
    return pltpu.roll(x, x.shape[1] - 1, 1)


def west(x):
    return pltpu.roll(x, 1, 1)


def smooth(s, spread):
    for repeat in range(FILTER):
        q = spread * s
        s = s + smoothing * spread * (north(q) + south(q) + east(q) + west(q) - 4.0 * q)
    return s


def edge_block(rows):
    lane = lax.broadcasted_iota(jnp.int32, (rows.shape[0], LANES), 1)
    return jnp.where(lane < LANES // 2, rows[:, :LANES], rows[:, rows.shape[1] - LANES :])


def blend(weights, own, others, layer):
    layers = own.shape[0]
    total = None
    for i, source in enumerate([own] + list(others)):
        for m in range(layers):
            at = layer * layers * (1 + len(others)) + i * layers + m
            term = weights[at : at + 1, 0:1] * source[m]
            total = term if total is None else total + term
    return total


def parts_of(block, rows, per):
    block_row = jnp.floor((block + 0.5) / per)
    layer = jnp.floor((block_row + 0.5) / rows)
    return layer, block_row - layer * rows, block - block_row * per


def load_kernel(
    vertical, blocks, control, spread, wind_e, wind_n, scale, previous, innovation,
    platforms, counts,
    forth, back, control_v, spread_v, wind_e_v, wind_n_v, scale_v, previous_v, innovation_v,
    places, platforms_v, counts_v, lon_out, first, last, vertical_s, blocks_s, sems,
):
    pairs = (
        (spread, spread_v), (wind_e, wind_e_v), (wind_n, wind_n_v), (scale, scale_v), (blocks, blocks_s),
        (vertical, vertical_s), (control, control_v),
        (innovation, innovation_v), (previous, previous_v), (platforms, platforms_v),
        (counts, counts_v),
    )
    copies = [pltpu.make_async_copy(a, b, sems.at[i]) for i, (a, b) in enumerate(pairs)]
    for copy in copies:
        copy.start()
    layers, rows, cols = control.shape
    slots, owners = blocks.shape
    for copy in copies[:5]:
        copy.wait()
    line = lax.broadcasted_iota(jnp.int32, (1, LANES), 1)
    numbers = jnp.full((1, LANES), -1.0, f32)
    for s in range(slots):
        for o in range(owners):
            numbers = jnp.where(line == s * owners + o, blocks_s[s, o].astype(f32), numbers)
    layer, row, col = parts_of(numbers, rows, cols // LANES)
    places[...] = ((layer * (cols // LANES) + col) * (rows + 8) + row).astype(jnp.int32)
    lane = lax.broadcasted_iota(jnp.int32, (rows, LANES), 1)
    packed = jnp.zeros((rows, LANES), f32)
    fields = (spread_v, wind_e_v, wind_n_v, scale_v)
    for i, field in enumerate(fields):
        for l in range(layers):
            packed = lon_item(packed, field[l], (1 + i) * layers + l, lane)
    lon_out[:rows, :] = packed
    lon_out[rows:, :] = jnp.broadcast_to(numbers, (8, LANES))
    for out, low in ((first, True), (last, False)):
        at = WIDTHS[0] * layers
        for field, width in zip(fields, WIDTHS[1:]):
            for l in range(layers):
                begin = 0 if low else rows - width
                out[at : at + width, :] = field[l, begin : begin + width, :]
                at += width
        for c in range(0, cols, LANES):
            out[at:, c : c + LANES] = jnp.broadcast_to(numbers, (out.shape[0] - at, LANES))
    for copy in copies[5:]:
        copy.wait()
    lev, levs = lax.axis_index("lev"), lax.axis_size("lev")
    for l in range(layers):
        for shift in range(levs):
            other = lax.rem(lev + levs - shift, levs)
            for m in range(layers):
                at = (l * levs + shift) * layers + m
                a, b = lev * layers + l, other * layers + m
                forth[at : at + 1, :] = jnp.full((1, LANES), vertical_s[a, b], f32)
                back[at : at + 1, :] = jnp.full((1, LANES), vertical_s[b, a], f32)


def lon_item(packed, field, item, lane):
    cols = field.shape[1]
    tile = jnp.where(lane < LANES // 2, field[:, :LANES], field[:, cols - LANES :])
    if item:
        tile = pltpu.roll(tile, 8 * item, 1)
    return jnp.where((lane + HALO - 8 * item) % LANES < 8, tile, packed)


def pack_kernel(n_other, *refs):
    forth, control, lon_part, first, last = refs[:5]
    others = refs[5 : 5 + n_other]
    blended, lon_out, lat_1, lat_2, diag_1, diag_2 = refs[5 + n_other :]
    layers, rows, cols = control.shape
    packed = lon_part[:rows, :]
    lane = lax.broadcasted_iota(jnp.int32, (rows, LANES), 1)
    firsts, lasts = [], []
    for l in range(layers):
        value = blend(forth, control, others, l)
        blended[l] = value
        packed = lon_item(packed, value, l, lane)
        firsts.append(value[:HALO, :])
        lasts.append(value[rows - HALO :, :])
    lon_out[:rows, :] = packed
    lon_out[rows:, :] = lon_part[rows:, :]
    even = lax.axis_index("lat") % 2 == 0
    for out, diag, use_last in ((lat_1, diag_1, even), (lat_2, diag_2, jnp.logical_not(even))):
        begin = HALO * layers
        flag = jnp.where(use_last, 1, 0)
        for l in range(layers):
            chosen = jnp.full((HALO, cols), flag, jnp.int32) == 1
            out[HALO * l : HALO * (l + 1), :] = jnp.where(chosen, lasts[l], firsts[l])
        chosen = jnp.full((first.shape[0] - begin, cols), flag, jnp.int32) == 1
        out[begin:, :] = jnp.where(chosen, last[begin:, :], first[begin:, :])
        diag[...] = edge_block(out[...])


def extend_kernel(*refs):
    square, refs = refs[0], refs[1:]
    half = len(refs) // 2
    refs[-1][...] = jnp.full((1, LANES), square[0], f32)
    for field, out in zip(refs[:half], refs[half:-1]):
        layers, rows, cols = field.shape
        for l in range(layers):
            out[l, :rows, :cols] = field[l]
            out[l, rows:, :] = jnp.zeros((8, cols + LANES), f32)


def parts_kernel(matrices, out):
    count, height = matrices.shape[:2]

    def body(i, carry):
        out[i, :height, :], out[i, height:, :] = split(matrices[i])
        return carry

    for_each(count, body, 0)


def at_ends():
    lat = lax.axis_index("lat")
    return lat == 0, lat == lax.axis_size("lat") - 1


def unpack(lon_in, lat_1, lat_2, diag_1, diag_2, ext):
    layers, rows, cols = ext[0].shape[0], ext[0].shape[1] - 8, ext[0].shape[2] - LANES
    lane = lax.broadcasted_iota(jnp.int32, (rows, LANES), 1)
    keep = (lane < HALO) | (lane >= LANES - HALO)
    packed = lon_in[:rows, :]
    item = 0
    for out in ext:
        for l in range(layers):
            tile = pltpu.roll(packed, LANES - 8 * item, 1) if item else packed
            out[l, :rows, cols:] = jnp.where(keep, tile, 0.0)
            item += 1
    count = sum(WIDTHS) * layers
    for one, two, begin in ((lat_1, lat_2, 0), (diag_1, diag_2, cols)):
        width = one.shape[1]
        a, b = one[:count, :], two[:count, :]
        even = jnp.full(a.shape, lax.axis_index("lat") % 2, jnp.int32) == 0
        south_end, north_end = at_ends()
        top = jnp.full(a.shape, jnp.where(north_end, 1, 0), jnp.int32) == 0
        bottom = jnp.full(a.shape, jnp.where(south_end, 1, 0), jnp.int32) == 0
        if begin:
            lane_d = lax.broadcasted_iota(jnp.int32, a.shape, 1)
            inside = (lane_d < HALO) | (lane_d >= LANES - HALO)
            top = top & inside
            bottom = bottom & inside
        from_north = jnp.where(top, jnp.where(even, a, b), 0.0)
        from_south = jnp.where(bottom, jnp.where(even, b, a), 0.0)
        at = 0
        for out, l, w in [(e, l, w) for e, w in zip(ext, WIDTHS) for l in range(layers)]:
            out[l, rows : rows + w, begin : begin + width] = from_north[at : at + w, :]
            out[l, rows + 8 - w : rows + 8, begin : begin + width] = from_south[at : at + w, :]
            at += w


def inside_mask(ext_shape):
    south_end, north_end = at_ends()
    row = lax.broadcasted_iota(jnp.int32, ext_shape, 0)
    rows = ext_shape[0] - 8
    north_cut = jnp.where(north_end, rows, rows + 8)
    south_cut = jnp.where(south_end, rows + 4, rows + 8)
    cut = ((row >= north_cut) & (row < rows + 4)) | (row >= south_cut)
    return jnp.where(cut, 0.0, 1.0).astype(f32)


def forward_kernel(
    places, platforms, counts, mixed_in, spread_in, wind_e_in, wind_n_in, scale_in,
    lon_in, lat_1, lat_2, diag_1, diag_2, interp, innovation,
    sent, mixed, spread, wind_e, wind_n, scale,
    field, places_s, platforms_s, counts_s, sems,
):
    pairs = ((places, places_s), (platforms, platforms_s), (counts, counts_s))
    copies = [pltpu.make_async_copy(a, b, sems.at[i]) for i, (a, b) in enumerate(pairs)]
    for copy in copies:
        copy.start()
    unpack(lon_in, lat_1, lat_2, diag_1, diag_2, (mixed, spread, wind_e, wind_n, scale))
    layers, ext_rows, ext_cols = mixed.shape
    per = ext_cols // LANES - 1
    mask = inside_mask((ext_rows, ext_cols))
    for l in range(layers):
        x = scale[l] * smooth(mixed[l], spread[l])
        u, v = 0.5 * wind_e[l], 0.5 * wind_n[l]
        for step in range(STEPS):
            if step:
                x = x * mask
            x = (
                (1.0 - 4.0 * diffusion) * x
                + (diffusion - u) * east(x)
                + (diffusion + u) * west(x)
                + (diffusion - v) * north(x)
                + (diffusion + v) * south(x)
            )
        for c in range(per):
            begin = (l * per + c) * ext_rows
            field[begin : begin + ext_rows, :] = x[:, c * LANES : (c + 1) * LANES]
    for copy in copies:
        copy.wait()
    count, width = innovation.shape
    slots, owners = platforms.shape
    row = lax.broadcasted_iota(jnp.int32, (count, width), 0)

    def body(b, total):
        at = places_s[0, (b % slots) * owners + b // slots]
        left = jnp.where(row == b, jnp.broadcast_to(field[pl.ds(at, 1), :], (count, width)), 0.0)
        return total + dot(left, interp[b], 1)

    departure = for_each(count, body, jnp.zeros((count, width), f32)) - innovation[...]
    half = sent.shape[1] // 2
    sent[...] = jnp.zeros(sent.shape, f32)
    for o in range(owners):
        for s in range(slots):
            live = jnp.full((1, width), counts_s[0, o], jnp.int32) > s
            b = o * slots + s
            sent[o, s : s + 1, :] = jnp.where(live, departure[b : b + 1, :], 0.0)
            sent[o, half + s : half + s + 1, :] = jnp.full((1, width), platforms_s[s, o].astype(f32), f32)


def weigh_kernel(slots, arrived, matrices, out, values, platform):
    tiles, height, width = arrived.shape
    for t in range(tiles):
        for s in range(slots):
            at = s * tiles + t
            values[at : at + 1, :] = arrived[t, s : s + 1, :]
            platform[at : at + 1, :] = arrived[t, height // 2 + s : height // 2 + s + 1, :]
    x, where = values[...], platform[...]
    total = jnp.zeros(x.shape, f32)
    for p in range(matrices.shape[0]):
        total = total + dot(jnp.where(where == float(p), x, 0.0), jnp.concatenate(split(matrices[p]), axis=0), 1)
    out[...] = jnp.zeros(out.shape, f32)
    for t in range(tiles):
        for s in range(slots):
            at = s * tiles + t
            out[t, s : s + 1, :] = total[at : at + 1, :]


def transpose_kernel(slots, returned, interp, out):
    count, width = out.shape
    row = lax.broadcasted_iota(jnp.int32, (count, width), 0)

    def body(b, total):
        owner, slot = b // slots, b % slots
        weighted = returned[owner, pl.ds(slot, 1), :]
        left = jnp.where(
            row == slot * (count // slots) + owner, jnp.broadcast_to(weighted, (count, width)), 0.0
        )
        return total + dot(left, interp[b], 0)

    out[...] = for_each(count, body, jnp.zeros((count, width), f32))


def place_kernel(count, kinds, rows, layers, per, *refs):
    tiles, out = refs[:-1], refs[-1]
    line = lax.broadcasted_iota(jnp.int32, (1, LANES), 1)
    south_end, north_end = at_ends()
    odd = lax.axis_index("lat") % 2
    packs = -(-len(kinds) * count // LANES)
    targets = [jnp.full((1, LANES), -1.0, f32) for _ in range(packs)]
    for i, (tile, (phase, lon_step, begin)) in enumerate(zip(tiles, kinds)):
        block = tile[begin : begin + 1, :LANES]
        layer, row, col = parts_of(block, rows, per)
        valid = block >= 0.0
        if phase:
            is_north = jnp.where(odd == phase - 1, 1, 0)
            usable = jnp.where(is_north == 1, jnp.where(north_end, 0, 1), jnp.where(south_end, 0, 1))
            is_north = jnp.full((1, LANES), is_north, jnp.int32) == 1
            usable = jnp.full((1, LANES), usable, jnp.int32) == 1
            valid = valid & usable
            valid = valid & ((is_north & (row < HALO)) | (jnp.logical_not(is_north) & (row >= rows - HALO)))
            row = jnp.where(is_north, row + rows, row + 8)
        if lon_step:
            at_first, at_last = col == 0.0, col == per - 1.0
            both = at_first | at_last
            if lon_step == 1:
                both = at_first
            if lon_step == -1:
                both = at_last
            valid = valid & both
            col = jnp.where(at_first, float(per), float(per + 1))
        place = jnp.where(valid, (layer * (per + 2) + col) * (rows + 8) + row, -1.0)
        pack, shift = divmod(i * count, LANES)
        if shift:
            place = pltpu.roll(place, shift, 1)
        mine = (line >= shift) & (line < shift + count)
        targets[pack] = jnp.where(mine, place, targets[pack])
    places = out.shape[0]
    index = lax.broadcasted_iota(jnp.int32, (places, LANES), 0)
    for pack, target in enumerate(targets):
        chosen = jnp.where(index == target.astype(jnp.int32), 1.0, 0.0).astype(bf16)
        out[:, pack * LANES : (pack + 1) * LANES] = chosen
        out[:, (packs + pack) * LANES : (packs + pack + 1) * LANES] = chosen


def adjoint_kernel(n_source, *refs):
    chosen = refs[0]
    sources = refs[1 : 1 + n_source]
    spread, scale, wind_e, wind_n = refs[1 + n_source : 5 + n_source]
    filtered, = refs[5 + n_source :]
    layers, ext_rows, ext_cols = spread.shape
    rows, cols = filtered.shape[1:]
    values = [s[...] for s in sources]
    spare = chosen.shape[1] // 2 - sum(v.shape[0] for v in values)
    if spare:
        values.append(jnp.zeros((spare, LANES), f32))
    parts = jnp.concatenate(split(jnp.concatenate(values, axis=0)), axis=0)
    forcing = lax.dot_general(chosen[...], parts, NN, preferred_element_type=f32)
    mask = inside_mask((ext_rows, ext_cols))
    lane = lax.broadcasted_iota(jnp.int32, (ext_rows, LANES), 1)
    per = cols // LANES
    for l in range(layers):
        begin = l * (per + 2) * ext_rows
        tiles = [forcing[begin + c * ext_rows : begin + (c + 1) * ext_rows, :] for c in range(per + 2)]
        y = jnp.concatenate(tiles[:per] + [jnp.where(lane < LANES // 2, tiles[per], tiles[per + 1])], axis=1)
        u, v = 0.5 * wind_e[l], 0.5 * wind_n[l]
        for step in range(STEPS):
            if step:
                y = y * mask
            y = (
                (1.0 - 4.0 * diffusion) * y
                + east((diffusion + u) * y)
                + west((diffusion - u) * y)
                + north((diffusion + v) * y)
                + south((diffusion - v) * y)
            )
        s = smooth(scale[l] * y, spread[l])
        filtered[l] = s[:rows, :cols]


def gradient_kernel(n_other, *refs):
    back, control, filtered = refs[:3]
    others = refs[3 : 3 + n_other]
    gradient, partial = refs[3 + n_other :]
    layers, rows, cols = control.shape
    total = jnp.zeros((8, LANES), f32)
    for m in range(layers):
        g = control[m] + blend(back, filtered, others, m)
        gradient[m] = g
        square = g * g
        for r in range(0, rows, 8):
            for c in range(0, cols, LANES):
                total = total + square[r : r + 8, c : c + LANES]
    total = jnp.sum(total, axis=0, keepdims=True)
    partial[...] = jnp.broadcast_to(total[None], partial.shape)


def direction_kernel(cell_count, gradient_in, sums, previous, previous_square, gradient, direction):
    total = jnp.sum(jnp.sum(sums[...], axis=0), axis=1, keepdims=True)
    factor = total / cell_count / previous_square[:, 0:1]
    for l in range(gradient.shape[0]):
        gradient[l] = gradient_in[l]
        direction[l] = factor * previous[l] - gradient_in[l]


def local(
    control,
    vertical,
    spread,
    error_scale,
    wind_lon,
    wind_lat,
    obs_block,
    obs_platform,
    obs_count,
    interp,
    innovation,
    error_inverse,
    previous_direction,
    previous_square,
):
    n_lat, n_lon, n_lev = (lax.axis_size(a) for a in ("lat", "lon", "lev"))
    layers, rows, cols = control.shape
    ext_rows, ext_cols = rows + 8, cols + LANES
    owners = obs_count.shape[-1]
    slots = obs_block.shape[-1]
    width = interp.shape[-1]
    count = owners * slots
    blocks = obs_block.reshape(owners, slots).T
    platforms = obs_platform.reshape(owners, slots).T
    counts = obs_count.reshape(1, owners)
    weights = interp.reshape(count, width, width)
    limit = (8 << 20) + 3 * weights.size * 4
    per = cols // LANES
    lat_fields = sum(WIDTHS) * layers
    lat_rows = lat_fields // 8 * 8 + 8

    def from_levs(field):
        return [
            lax.ppermute(field, "lev", [(i, (i + k) % n_lev) for i in range(n_lev)]) for k in range(1, n_lev)
        ]

    def partner(a, phase):
        to = a + (1 if (a % 2 == 0) == (phase == 1) else -1)
        return to if 0 <= to < n_lat else a

    def exchange(field, phase, lon_step):
        pairs = []
        for a in range(n_lat):
            for b in range(n_lon):
                to = partner(a, phase) if phase else a
                pairs.append((a * n_lon + b, to * n_lon + (b + lon_step) % n_lon))
        return lax.ppermute(field, ("lat", "lon"), pairs)

    lon_steps = (2,) if n_lon == 2 else (1, -1)

    def from_lon(field, phase, step):
        return exchange(field, phase, 1 if step == 2 else -step)

    others = from_levs(control)
    field = held(layers, rows, cols)
    mix = held(layers * layers * n_lev, LANES)
    innovations = innovation.reshape(count, width)
    (
        forth, back, control_v, spread_v, wind_e_v, wind_n_v, scale_v, previous_v, innovation_v,
        places, platforms_v, counts_v, lon_part, first, last,
    ) = call(
        load_kernel,
        [mix, mix] + [field] * 6 + [held(count, width)]
        + [held(1, LANES, dtype=jnp.int32)]
        + [held(*x.shape, dtype=jnp.int32) for x in (platforms, counts)]
        + [held(rows + 8, LANES), held(lat_rows, cols), held(lat_rows, cols)],
        [HBM] * 11,
        [
            pltpu.SMEM(vertical.shape, f32),
            pltpu.SMEM(blocks.shape, jnp.int32),
            pltpu.SemaphoreType.DMA((11,)),
        ],
        58 << 20,
    )(
        vertical, blocks, control, spread, wind_lon, wind_lat, error_scale, previous_direction,
        innovations, platforms, counts,
    )
    blended, lon_out, lat_1, lat_2, diag_1, diag_2 = call(
        functools.partial(pack_kernel, len(others)),
        [field, held(rows + 8, LANES)] + [held(lat_rows, cols)] * 2 + [held(lat_rows, LANES)] * 2,
        [VMEM] * (5 + len(others)),
    )(forth, control_v, lon_part, first, last, *others)

    lane = jnp.arange(LANES, dtype=jnp.int32)
    lat_in = {phase: exchange(out, phase, 0) for phase, out in ((1, lat_1), (2, lat_2))}
    lon_raw = {step: from_lon(lon_out, 0, step) for step in lon_steps}
    diag_raw = {
        (phase, step): from_lon(out, phase, step)
        for phase, out in ((1, diag_1), (2, diag_2))
        for step in lon_steps
    }
    if n_lon == 2:
        lon_in = lon_raw[2]
        diag_in = {phase: diag_raw[phase, 2] for phase in (1, 2)}
    else:
        lon_in = jnp.where(lane % 8 < HALO, lon_raw[1], lon_raw[-1])
        diag_in = {
            phase: jnp.where(lane < LANES // 2, diag_raw[phase, 1], diag_raw[phase, -1]) for phase in (1, 2)
        }

    half = -(-slots // 4) * 4
    ext = held(layers, ext_rows, ext_cols)
    *exts, square_v = call(extend_kernel, [ext] * 5 + [held(1, LANES)], [SMEM] + [VMEM] * 5)(
        previous_square, blended, spread_v, wind_e_v, wind_n_v, scale_v
    )
    matrices = error_inverse.reshape(error_inverse.shape[-3:])
    weights = call(parts_kernel, held(count, 2 * width, width, dtype=bf16), [VMEM], (), limit)(weights)
    sent, _, ext_spread, ext_e, ext_n, ext_scale = call(
        forward_kernel,
        [held(owners, 2 * half, width)] + [ext] * 5,
        [VMEM] * 15,
        [
            pltpu.VMEM((layers * ext_rows * per, LANES), f32),
            pltpu.SMEM((1, LANES), jnp.int32),
            pltpu.SMEM(blocks.shape, jnp.int32),
            pltpu.SMEM(counts.shape, jnp.int32),
            pltpu.SemaphoreType.DMA((3,)),
        ],
        limit,
        {3 + i: 1 + i for i in range(5)},
    )(
        places, platforms_v, counts_v, *exts, lon_in, lat_in[1], lat_in[2], diag_in[1], diag_in[2], weights, innovation_v,
    )

    arrived = lax.all_to_all(sent, ("lat", "lon"), split_axis=0, concat_axis=0, tiled=True)
    result = call(
        functools.partial(weigh_kernel, slots),
        held(owners, 2 * half, width),
        [VMEM] * 2,
        [pltpu.VMEM((count, width), f32)] * 2,
    )(arrived, matrices)
    returned = lax.all_to_all(result, ("lat", "lon"), split_axis=0, concat_axis=0, tiled=True)
    adjoint_obs = call(
        functools.partial(transpose_kernel, slots), held(count, width), [VMEM] * 2, (), limit
    )(returned, weights)

    sources, tiles, kinds = [adjoint_obs], [lon_out], [(0, 0, rows)]
    for step in lon_steps:
        sources.append(from_lon(adjoint_obs, 0, step))
        tiles.append(lon_raw[step])
        kinds.append((0, step, rows))
    row_of_tiles = jnp.concatenate(sources, axis=0)
    for phase in (1, 2):
        sources.append(exchange(row_of_tiles, phase, 0))
        tiles.append(lat_in[phase])
        kinds.append((phase, 0, lat_fields))
        for step in lon_steps:
            tiles.append(diag_raw[phase, step])
            kinds.append((phase, step, lat_fields))
    depth = -(-len(kinds) * count // LANES) * LANES
    chosen = call(
        functools.partial(place_kernel, count, kinds, rows, layers, per),
        held(layers * (per + 2) * ext_rows, 2 * depth, dtype=bf16),
        [VMEM] * len(tiles),
        (),
        limit,
    )(*tiles)
    filtered = call(
        functools.partial(adjoint_kernel, len(sources)),
        held(layers, rows, cols),
        [VMEM] * (5 + len(sources)),
        (),
        limit,
    )(chosen, *sources, ext_spread, ext_scale, ext_e, ext_n)

    others = from_levs(filtered)
    group = n_lat * n_lon * n_lev
    gradient, partial = call(
        functools.partial(gradient_kernel, len(others)),
        [field, held(group, 1, LANES)],
        [VMEM] * (3 + len(others)),
    )(back, control_v, filtered, *others)
    sums = lax.all_to_all(partial, ("lat", "lon", "lev"), split_axis=0, concat_axis=0, tiled=True)
    gradient, direction = call(
        functools.partial(direction_kernel, float(control.size * group)),
        [shape(layers, rows, cols)] * 2,
        [VMEM] * 4,
    )(gradient, sums, previous_v, square_v)
    return (gradient, direction)


def solution(mesh):
    field = P("lev", ("member", "lat"), "lon")
    shared = P("lev", "lat", "lon")
    placed = (
        field,
        P(),
        shared,
        shared,
        field,
        field,
        P("lev", "lat", "lon", None, None),
        P("lev", "lat", "lon", None, None),
        P("lev", "lat", "lon", None),
        P("lev", "lat", "lon", None, None, None, None),
        P("lev", ("member", "lat"), "lon", None, None, None),
        P("lat", "lon", None, None, None),
        field,
        P("member"),
    )
    return jax.shard_map(local, mesh=mesh, in_specs=placed, out_specs=(field, field), check_vma=False)
```

```python
import functools
import jax
import jax.numpy as jnp
from jax import lax
from jax.experimental import pallas as pl
from jax.experimental.pallas import tpu as pltpu
from jax.sharding import PartitionSpec as P

FILTER = 2
STEPS = 2
HALO = 4
WIDTHS = (4, 4, 4, 4, 2)
LANES = 128
smoothing = 0.1
diffusion = 0.15
f32 = jnp.float32
bf16 = jnp.bfloat16
VMEM = pl.BlockSpec(memory_space=pltpu.VMEM)
SMEM = pl.BlockSpec(memory_space=pltpu.SMEM)
HBM = pl.BlockSpec(memory_space=pltpu.HBM)
NN = (((1,), (0,)), ((), ()))


def call(kernel, out_shape, in_specs, scratch=(), limit=8 << 20, aliases=None):
    many = isinstance(out_shape, (list, tuple))
    return pl.pallas_call(
        kernel,
        out_shape=out_shape,
        in_specs=in_specs,
        out_specs=[VMEM] * len(out_shape) if many else VMEM,
        scratch_shapes=list(scratch),
        input_output_aliases=aliases or {},
        compiler_params=pltpu.CompilerParams(vmem_limit_bytes=limit),
        cost_estimate=pl.CostEstimate(flops=1 << 20, bytes_accessed=1 << 20, transcendentals=0),
    )


def held(*dims, dtype=f32):
    return pltpu.VMEM(dims, dtype)


def shape(*dims):
    return jax.ShapeDtypeStruct(dims, f32)


def split(value):
    high = value.astype(bf16)
    return high, (value - high.astype(f32)).astype(bf16)


def halves(value):
    high, low = split(value)
    return jnp.concatenate(
        [jnp.concatenate([high, high], axis=1), jnp.concatenate([low, jnp.zeros_like(low)], axis=1)], axis=0
    )


def dot(left, parts, axis):
    if axis:
        height = parts.shape[0] // 2
        parts = jnp.concatenate([parts[:height, :], parts[height:, :]], axis=1)
    result = lax.dot_general(halves(left), parts, (((1,), (axis,)), ((), ())), preferred_element_type=f32)
    return result[: left.shape[0]] + result[left.shape[0] :]


def for_each(count, body, start):
    if count <= 32:
        for i in range(count):
            start = body(i, start)
        return start
    return lax.fori_loop(0, count, body, start)


def north(x):
    return pltpu.roll(x, x.shape[0] - 1, 0)


def south(x):
    return pltpu.roll(x, 1, 0)


def east(x):
    return pltpu.roll(x, x.shape[1] - 1, 1)


def west(x):
    return pltpu.roll(x, 1, 1)


def smooth(s, spread):
    for repeat in range(FILTER):
        q = spread * s
        s = s + smoothing * spread * (north(q) + south(q) + east(q) + west(q) - 4.0 * q)
    return s


def edge_block(rows):
    lane = lax.broadcasted_iota(jnp.int32, (rows.shape[0], LANES), 1)
    return jnp.where(lane < LANES // 2, rows[:, :LANES], rows[:, rows.shape[1] - LANES :])


def blend(weights, own, others, layer):
    layers = own.shape[0]
    total = None
    for i, source in enumerate([own] + list(others)):
        for m in range(layers):
            at = layer * layers * (1 + len(others)) + i * layers + m
            term = weights[at : at + 1, 0:1] * source[m]
            total = term if total is None else total + term
    return total


def parts_of(block, rows, per):
    block_row = jnp.floor((block + 0.5) / per)
    layer = jnp.floor((block_row + 0.5) / rows)
    return layer, block_row - layer * rows, block - block_row * per


def load_kernel(
    vertical, blocks, control, spread, wind_e, wind_n, scale, previous, innovation,
    platforms, counts,
    forth, back, control_v, spread_v, wind_e_v, wind_n_v, scale_v, previous_v, innovation_v,
    places, platforms_v, counts_v, lon_out, first, last, vertical_s, blocks_s, sems,
):
    pairs = (
        (spread, spread_v), (wind_e, wind_e_v), (wind_n, wind_n_v), (scale, scale_v), (blocks, blocks_s),
        (vertical, vertical_s), (control, control_v),
        (innovation, innovation_v), (previous, previous_v), (platforms, platforms_v),
        (counts, counts_v),
    )
    copies = [pltpu.make_async_copy(a, b, sems.at[i]) for i, (a, b) in enumerate(pairs)]
    for copy in copies:
        copy.start()
    layers, rows, cols = control.shape
    slots, owners = blocks.shape
    for copy in copies[:5]:
        copy.wait()
    line = lax.broadcasted_iota(jnp.int32, (1, LANES), 1)
    numbers = jnp.full((1, LANES), -1.0, f32)
    for s in range(slots):
        for o in range(owners):
            numbers = jnp.where(line == s * owners + o, blocks_s[s, o].astype(f32), numbers)
    layer, row, col = parts_of(numbers, rows, cols // LANES)
    places[...] = ((layer * (cols // LANES) + col) * (rows + 8) + row).astype(jnp.int32)
    lane = lax.broadcasted_iota(jnp.int32, (rows, LANES), 1)
    packed = jnp.zeros((rows, LANES), f32)
    fields = (spread_v, wind_e_v, wind_n_v, scale_v)
    for i, field in enumerate(fields):
        for l in range(layers):
            packed = lon_item(packed, field[l], (1 + i) * layers + l, lane)
    lon_out[:rows, :] = packed
    lon_out[rows:, :] = jnp.broadcast_to(numbers, (8, LANES))
    for out, low in ((first, True), (last, False)):
        at = WIDTHS[0] * layers
        for field, width in zip(fields, WIDTHS[1:]):
            for l in range(layers):
                begin = 0 if low else rows - width
                out[at : at + width, :] = field[l, begin : begin + width, :]
                at += width
        for c in range(0, cols, LANES):
            out[at:, c : c + LANES] = jnp.broadcast_to(numbers, (out.shape[0] - at, LANES))
    for copy in copies[5:]:
        copy.wait()
    lev, levs = lax.axis_index("lev"), lax.axis_size("lev")
    for l in range(layers):
        for shift in range(levs):
            other = lax.rem(lev + levs - shift, levs)
            for m in range(layers):
                at = (l * levs + shift) * layers + m
                a, b = lev * layers + l, other * layers + m
                forth[at : at + 1, :] = jnp.full((1, LANES), vertical_s[a, b], f32)
                back[at : at + 1, :] = jnp.full((1, LANES), vertical_s[b, a], f32)


def lon_item(packed, field, item, lane):
    cols = field.shape[1]
    tile = jnp.where(lane < LANES // 2, field[:, :LANES], field[:, cols - LANES :])
    if item:
        tile = pltpu.roll(tile, 8 * item, 1)
    return jnp.where((lane + HALO - 8 * item) % LANES < 8, tile, packed)


def pack_kernel(n_other, *refs):
    forth, control, lon_part, first, last = refs[:5]
    others = refs[5 : 5 + n_other]
    blended, lon_out, lat_1, lat_2, diag_1, diag_2 = refs[5 + n_other :]
    layers, rows, cols = control.shape
    packed = lon_part[:rows, :]
    lane = lax.broadcasted_iota(jnp.int32, (rows, LANES), 1)
    firsts, lasts = [], []
    for l in range(layers):
        value = blend(forth, control, others, l)
        blended[l] = value
        packed = lon_item(packed, value, l, lane)
        firsts.append(value[:HALO, :])
        lasts.append(value[rows - HALO :, :])
    lon_out[:rows, :] = packed
    lon_out[rows:, :] = lon_part[rows:, :]
    even = lax.axis_index("lat") % 2 == 0
    for out, diag, use_last in ((lat_1, diag_1, even), (lat_2, diag_2, jnp.logical_not(even))):
        begin = HALO * layers
        flag = jnp.where(use_last, 1, 0)
        for l in range(layers):
            chosen = jnp.full((HALO, cols), flag, jnp.int32) == 1
            out[HALO * l : HALO * (l + 1), :] = jnp.where(chosen, lasts[l], firsts[l])
        chosen = jnp.full((first.shape[0] - begin, cols), flag, jnp.int32) == 1
        out[begin:, :] = jnp.where(chosen, last[begin:, :], first[begin:, :])
        diag[...] = edge_block(out[...])


def extend_kernel(*refs):
    square, refs = refs[0], refs[1:]
    half = len(refs) // 2
    refs[-1][...] = jnp.full((1, LANES), square[0], f32)
    for field, out in zip(refs[:half], refs[half:-1]):
        layers, rows, cols = field.shape
        for l in range(layers):
            out[l, :rows, :cols] = field[l]
            out[l, rows:, :] = jnp.zeros((8, cols + LANES), f32)


def parts_kernel(matrices, out):
    count, height = matrices.shape[:2]

    def body(i, carry):
        out[i, :height, :], out[i, height:, :] = split(matrices[i])
        return carry

    for_each(count, body, 0)


def at_ends():
    lat = lax.axis_index("lat")
    return lat == 0, lat == lax.axis_size("lat") - 1


def unpack(lon_in, lat_1, lat_2, diag_1, diag_2, ext):
    layers, rows, cols = ext[0].shape[0], ext[0].shape[1] - 8, ext[0].shape[2] - LANES
    lane = lax.broadcasted_iota(jnp.int32, (rows, LANES), 1)
    keep = (lane < HALO) | (lane >= LANES - HALO)
    packed = lon_in[:rows, :]
    item = 0
    for out in ext:
        for l in range(layers):
            tile = pltpu.roll(packed, LANES - 8 * item, 1) if item else packed
            out[l, :rows, cols:] = jnp.where(keep, tile, 0.0)
            item += 1
    count = sum(WIDTHS) * layers
    for one, two, begin in ((lat_1, lat_2, 0), (diag_1, diag_2, cols)):
        width = one.shape[1]
        a, b = one[:count, :], two[:count, :]
        even = jnp.full(a.shape, lax.axis_index("lat") % 2, jnp.int32) == 0
        south_end, north_end = at_ends()
        top = jnp.full(a.shape, jnp.where(north_end, 1, 0), jnp.int32) == 0
        bottom = jnp.full(a.shape, jnp.where(south_end, 1, 0), jnp.int32) == 0
        if begin:
            lane_d = lax.broadcasted_iota(jnp.int32, a.shape, 1)
            inside = (lane_d < HALO) | (lane_d >= LANES - HALO)
            top = top & inside
            bottom = bottom & inside
        from_north = jnp.where(top, jnp.where(even, a, b), 0.0)
        from_south = jnp.where(bottom, jnp.where(even, b, a), 0.0)
        at = 0
        for out, l, w in [(e, l, w) for e, w in zip(ext, WIDTHS) for l in range(layers)]:
            out[l, rows : rows + w, begin : begin + width] = from_north[at : at + w, :]
            out[l, rows + 8 - w : rows + 8, begin : begin + width] = from_south[at : at + w, :]
            at += w


def inside_mask(ext_shape):
    south_end, north_end = at_ends()
    row = lax.broadcasted_iota(jnp.int32, ext_shape, 0)
    rows = ext_shape[0] - 8
    north_cut = jnp.where(north_end, rows, rows + 8)
    south_cut = jnp.where(south_end, rows + 4, rows + 8)
    cut = ((row >= north_cut) & (row < rows + 4)) | (row >= south_cut)
    return jnp.where(cut, 0.0, 1.0).astype(f32)


def forward_kernel(
    places, platforms, counts, mixed_in, spread_in, wind_e_in, wind_n_in, scale_in,
    lon_in, lat_1, lat_2, diag_1, diag_2, interp, innovation,
    sent, mixed, spread, wind_e, wind_n, scale,
    field, places_s, platforms_s, counts_s, sems,
):
    pairs = ((places, places_s), (platforms, platforms_s), (counts, counts_s))
    copies = [pltpu.make_async_copy(a, b, sems.at[i]) for i, (a, b) in enumerate(pairs)]
    for copy in copies:
        copy.start()
    unpack(lon_in, lat_1, lat_2, diag_1, diag_2, (mixed, spread, wind_e, wind_n, scale))
    layers, ext_rows, ext_cols = mixed.shape
    per = ext_cols // LANES - 1
    mask = inside_mask((ext_rows, ext_cols))
    for l in range(layers):
        x = scale[l] * smooth(mixed[l], spread[l])
        u, v = 0.5 * wind_e[l], 0.5 * wind_n[l]
        for step in range(STEPS):
            if step:
                x = x * mask
            x = (
                (1.0 - 4.0 * diffusion) * x
                + (diffusion - u) * east(x)
                + (diffusion + u) * west(x)
                + (diffusion - v) * north(x)
                + (diffusion + v) * south(x)
            )
        for c in range(per):
            begin = (l * per + c) * ext_rows
            field[begin : begin + ext_rows, :] = x[:, c * LANES : (c + 1) * LANES]
    for copy in copies:
        copy.wait()
    count, width = innovation.shape
    slots, owners = platforms.shape
    row = lax.broadcasted_iota(jnp.int32, (count, width), 0)

    def body(b, total):
        at = places_s[0, (b % slots) * owners + b // slots]
        left = jnp.where(row == b, jnp.broadcast_to(field[pl.ds(at, 1), :], (count, width)), 0.0)
        return total + dot(left, interp[b], 1)

    departure = for_each(count, body, jnp.zeros((count, width), f32)) - innovation[...]
    for o in range(owners):
        for s in range(slots):
            live = jnp.full((1, width), counts_s[0, o], jnp.int32) > s
            b = o * slots + s
            sent[o, s : s + 1, :] = jnp.where(live, departure[b : b + 1, :], 0.0)
            sent[o, slots + s : slots + s + 1, :] = jnp.full((1, width), platforms_s[s, o].astype(f32), f32)


def weigh_kernel(slots, arrived, matrices, out, values, platform):
    tiles = arrived.shape[0]
    for t in range(tiles):
        for s in range(slots):
            at = s * tiles + t
            values[at : at + 1, :] = arrived[t, s : s + 1, :]
            platform[at : at + 1, :] = arrived[t, slots + s : slots + s + 1, :]
    x, where = values[...], platform[...]
    total = jnp.zeros(x.shape, f32)
    for p in range(matrices.shape[0]):
        total = total + dot(jnp.where(where == float(p), x, 0.0), jnp.concatenate(split(matrices[p]), axis=0), 1)
    for t in range(tiles):
        for s in range(slots):
            at = s * tiles + t
            out[t, s : s + 1, :] = total[at : at + 1, :]


def transpose_kernel(slots, returned, interp, out):
    count, width = out.shape
    row = lax.broadcasted_iota(jnp.int32, (count, width), 0)

    def body(b, total):
        owner, slot = b // slots, b % slots
        weighted = returned[owner, pl.ds(slot, 1), :]
        left = jnp.where(
            row == slot * (count // slots) + owner, jnp.broadcast_to(weighted, (count, width)), 0.0
        )
        return total + dot(left, interp[b], 0)

    out[...] = for_each(count, body, jnp.zeros((count, width), f32))


def place_kernel(count, kinds, rows, layers, per, *refs):
    tiles, out = refs[:-1], refs[-1]
    line = lax.broadcasted_iota(jnp.int32, (1, LANES), 1)
    south_end, north_end = at_ends()
    odd = lax.axis_index("lat") % 2
    packs = -(-len(kinds) * count // LANES)
    targets = [jnp.full((1, LANES), -1.0, f32) for _ in range(packs)]
    for i, (tile, (phase, lon_step, begin)) in enumerate(zip(tiles, kinds)):
        block = tile[begin : begin + 1, :LANES]
        layer, row, col = parts_of(block, rows, per)
        valid = block >= 0.0
        if phase:
            is_north = jnp.where(odd == phase - 1, 1, 0)
            usable = jnp.where(is_north == 1, jnp.where(north_end, 0, 1), jnp.where(south_end, 0, 1))
            is_north = jnp.full((1, LANES), is_north, jnp.int32) == 1
            usable = jnp.full((1, LANES), usable, jnp.int32) == 1
            valid = valid & usable
            valid = valid & ((is_north & (row < HALO)) | (jnp.logical_not(is_north) & (row >= rows - HALO)))
            row = jnp.where(is_north, row + rows, row + 8)
        if lon_step:
            at_first, at_last = col == 0.0, col == per - 1.0
            both = at_first | at_last
            if lon_step == 1:
                both = at_first
            if lon_step == -1:
                both = at_last
            valid = valid & both
            col = jnp.where(at_first, float(per), float(per + 1))
        place = jnp.where(valid, (layer * (per + 2) + col) * (rows + 8) + row, -1.0)
        pack, shift = divmod(i * count, LANES)
        if shift:
            place = pltpu.roll(place, shift, 1)
        mine = (line >= shift) & (line < shift + count)
        targets[pack] = jnp.where(mine, place, targets[pack])
    places = out.shape[0]
    index = lax.broadcasted_iota(jnp.int32, (places, LANES), 0)
    for pack, target in enumerate(targets):
        chosen = jnp.where(index == target.astype(jnp.int32), 1.0, 0.0).astype(bf16)
        out[:, pack * LANES : (pack + 1) * LANES] = chosen
        out[:, (packs + pack) * LANES : (packs + pack + 1) * LANES] = chosen


def adjoint_kernel(n_source, *refs):
    chosen = refs[0]
    sources = refs[1 : 1 + n_source]
    spread, scale, wind_e, wind_n = refs[1 + n_source : 5 + n_source]
    filtered, = refs[5 + n_source :]
    layers, ext_rows, ext_cols = spread.shape
    rows, cols = filtered.shape[1:]
    values = [s[...] for s in sources]
    spare = chosen.shape[1] // 2 - sum(v.shape[0] for v in values)
    if spare:
        values.append(jnp.zeros((spare, LANES), f32))
    parts = jnp.concatenate(split(jnp.concatenate(values, axis=0)), axis=0)
    forcing = lax.dot_general(chosen[...], parts, NN, preferred_element_type=f32)
    mask = inside_mask((ext_rows, ext_cols))
    lane = lax.broadcasted_iota(jnp.int32, (ext_rows, LANES), 1)
    per = cols // LANES
    for l in range(layers):
        begin = l * (per + 2) * ext_rows
        tiles = [forcing[begin + c * ext_rows : begin + (c + 1) * ext_rows, :] for c in range(per + 2)]
        y = jnp.concatenate(tiles[:per] + [jnp.where(lane < LANES // 2, tiles[per], tiles[per + 1])], axis=1)
        u, v = 0.5 * wind_e[l], 0.5 * wind_n[l]
        for step in range(STEPS):
            if step:
                y = y * mask
            y = (
                (1.0 - 4.0 * diffusion) * y
                + east((diffusion + u) * y)
                + west((diffusion - u) * y)
                + north((diffusion + v) * y)
                + south((diffusion - v) * y)
            )
        s = smooth(scale[l] * y, spread[l])
        filtered[l] = s[:rows, :cols]


def gradient_kernel(n_other, *refs):
    back, control, filtered = refs[:3]
    others = refs[3 : 3 + n_other]
    gradient, partial = refs[3 + n_other :]
    layers, rows, cols = control.shape
    total = jnp.zeros((8, LANES), f32)
    for m in range(layers):
        g = control[m] + blend(back, filtered, others, m)
        gradient[m] = g
        square = g * g
        for r in range(0, rows, 8):
            for c in range(0, cols, LANES):
                total = total + square[r : r + 8, c : c + LANES]
    total = jnp.sum(total, axis=0, keepdims=True)
    partial[...] = jnp.broadcast_to(total[None], partial.shape)


def direction_kernel(cell_count, gradient_in, sums, previous, previous_square, gradient, direction):
    total = jnp.sum(jnp.sum(sums[...], axis=0), axis=1, keepdims=True)
    factor = total / cell_count / previous_square[:, 0:1]
    for l in range(gradient.shape[0]):
        gradient[l] = gradient_in[l]
        direction[l] = factor * previous[l] - gradient_in[l]


def local(
    control,
    vertical,
    spread,
    error_scale,
    wind_lon,
    wind_lat,
    obs_block,
    obs_platform,
    obs_count,
    interp,
    innovation,
    error_inverse,
    previous_direction,
    previous_square,
):
    n_lat, n_lon, n_lev = (lax.axis_size(a) for a in ("lat", "lon", "lev"))
    layers, rows, cols = control.shape
    ext_rows, ext_cols = rows + 8, cols + LANES
    owners = obs_count.shape[-1]
    slots = obs_block.shape[-1]
    width = interp.shape[-1]
    count = owners * slots
    blocks = obs_block.reshape(owners, slots).T
    platforms = obs_platform.reshape(owners, slots).T
    counts = obs_count.reshape(1, owners)
    weights = interp.reshape(count, width, width)
    limit = (8 << 20) + 3 * weights.size * 4
    per = cols // LANES
    lat_fields = sum(WIDTHS) * layers
    lat_rows = lat_fields // 8 * 8 + 8

    def from_levs(field):
        return [
            lax.ppermute(field, "lev", [(i, (i + k) % n_lev) for i in range(n_lev)]) for k in range(1, n_lev)
        ]

    def partner(a, phase):
        to = a + (1 if (a % 2 == 0) == (phase == 1) else -1)
        return to if 0 <= to < n_lat else a

    def exchange(field, phase, lon_step):
        pairs = []
        for a in range(n_lat):
            for b in range(n_lon):
                to = partner(a, phase) if phase else a
                pairs.append((a * n_lon + b, to * n_lon + (b + lon_step) % n_lon))
        return lax.ppermute(field, ("lat", "lon"), pairs)

    lon_steps = (2,) if n_lon == 2 else (1, -1)

    def from_lon(field, phase, step):
        return exchange(field, phase, 1 if step == 2 else -step)

    others = from_levs(control)
    field = held(layers, rows, cols)
    mix = held(layers * layers * n_lev, LANES)
    innovations = innovation.reshape(count, width)
    (
        forth, back, control_v, spread_v, wind_e_v, wind_n_v, scale_v, previous_v, innovation_v,
        places, platforms_v, counts_v, lon_part, first, last,
    ) = call(
        load_kernel,
        [mix, mix] + [field] * 6 + [held(count, width)]
        + [held(1, LANES, dtype=jnp.int32)]
        + [held(*x.shape, dtype=jnp.int32) for x in (platforms, counts)]
        + [held(rows + 8, LANES), held(lat_rows, cols), held(lat_rows, cols)],
        [HBM] * 11,
        [
            pltpu.SMEM(vertical.shape, f32),
            pltpu.SMEM(blocks.shape, jnp.int32),
            pltpu.SemaphoreType.DMA((11,)),
        ],
        58 << 20,
    )(
        vertical, blocks, control, spread, wind_lon, wind_lat, error_scale, previous_direction,
        innovations, platforms, counts,
    )
    blended, lon_out, lat_1, lat_2, diag_1, diag_2 = call(
        functools.partial(pack_kernel, len(others)),
        [field, held(rows + 8, LANES)] + [held(lat_rows, cols)] * 2 + [held(lat_rows, LANES)] * 2,
        [VMEM] * (5 + len(others)),
    )(forth, control_v, lon_part, first, last, *others)

    lane = jnp.arange(LANES, dtype=jnp.int32)
    lat_in = {phase: exchange(out, phase, 0) for phase, out in ((1, lat_1), (2, lat_2))}
    lon_raw = {step: from_lon(lon_out, 0, step) for step in lon_steps}
    diag_raw = {
        (phase, step): from_lon(out, phase, step)
        for phase, out in ((1, diag_1), (2, diag_2))
        for step in lon_steps
    }
    if n_lon == 2:
        lon_in = lon_raw[2]
        diag_in = {phase: diag_raw[phase, 2] for phase in (1, 2)}
    else:
        lon_in = jnp.where(lane % 8 < HALO, lon_raw[1], lon_raw[-1])
        diag_in = {
            phase: jnp.where(lane < LANES // 2, diag_raw[phase, 1], diag_raw[phase, -1]) for phase in (1, 2)
        }

    ext = held(layers, ext_rows, ext_cols)
    *exts, square_v = call(extend_kernel, [ext] * 5 + [held(1, LANES)], [SMEM] + [VMEM] * 5)(
        previous_square, blended, spread_v, wind_e_v, wind_n_v, scale_v
    )
    matrices = error_inverse.reshape(error_inverse.shape[-3:])
    weights = call(parts_kernel, held(count, 2 * width, width, dtype=bf16), [VMEM], (), limit)(weights)
    sent, _, ext_spread, ext_e, ext_n, ext_scale = call(
        forward_kernel,
        [held(owners, 2 * slots, width)] + [ext] * 5,
        [VMEM] * 15,
        [
            pltpu.VMEM((layers * ext_rows * per, LANES), f32),
            pltpu.SMEM((1, LANES), jnp.int32),
            pltpu.SMEM(blocks.shape, jnp.int32),
            pltpu.SMEM(counts.shape, jnp.int32),
            pltpu.SemaphoreType.DMA((3,)),
        ],
        limit,
        {3 + i: 1 + i for i in range(5)},
    )(
        places, platforms_v, counts_v, *exts, lon_in, lat_in[1], lat_in[2], diag_in[1], diag_in[2], weights, innovation_v,
    )

    arrived = lax.all_to_all(sent, ("lat", "lon"), split_axis=0, concat_axis=0, tiled=True)
    result = call(
        functools.partial(weigh_kernel, slots),
        held(owners, slots, width),
        [VMEM] * 2,
        [pltpu.VMEM((count, width), f32)] * 2,
    )(arrived, matrices)
    returned = lax.all_to_all(result, ("lat", "lon"), split_axis=0, concat_axis=0, tiled=True)
    adjoint_obs = call(
        functools.partial(transpose_kernel, slots), held(count, width), [VMEM] * 2, (), limit
    )(returned, weights)

    sources, tiles, kinds = [adjoint_obs], [lon_out], [(0, 0, rows)]
    for step in lon_steps:
        sources.append(from_lon(adjoint_obs, 0, step))
        tiles.append(lon_raw[step])
        kinds.append((0, step, rows))
    row_of_tiles = jnp.concatenate(sources, axis=0)
    for phase in (1, 2):
        sources.append(exchange(row_of_tiles, phase, 0))
        tiles.append(lat_in[phase])
        kinds.append((phase, 0, lat_fields))
        for step in lon_steps:
            tiles.append(diag_raw[phase, step])
            kinds.append((phase, step, lat_fields))
    depth = -(-len(kinds) * count // LANES) * LANES
    chosen = call(
        functools.partial(place_kernel, count, kinds, rows, layers, per),
        held(layers * (per + 2) * ext_rows, 2 * depth, dtype=bf16),
        [VMEM] * len(tiles),
        (),
        limit,
    )(*tiles)
    filtered = call(
        functools.partial(adjoint_kernel, len(sources)),
        held(layers, rows, cols),
        [VMEM] * (5 + len(sources)),
        (),
        limit,
    )(chosen, *sources, ext_spread, ext_scale, ext_e, ext_n)

    others = from_levs(filtered)
    group = n_lat * n_lon * n_lev
    gradient, partial = call(
        functools.partial(gradient_kernel, len(others)),
        [field, held(group, 1, LANES)],
        [VMEM] * (3 + len(others)),
    )(back, control_v, filtered, *others)
    sums = lax.all_to_all(partial, ("lat", "lon", "lev"), split_axis=0, concat_axis=0, tiled=True)
    gradient, direction = call(
        functools.partial(direction_kernel, float(control.size * group)),
        [shape(layers, rows, cols)] * 2,
        [VMEM] * 4,
    )(gradient, sums, previous_v, square_v)
    return (gradient, direction)


def solution(mesh):
    field = P("lev", ("member", "lat"), "lon")
    shared = P("lev", "lat", "lon")
    placed = (
        field,
        P(),
        shared,
        shared,
        field,
        field,
        P("lev", "lat", "lon", None, None),
        P("lev", "lat", "lon", None, None),
        P("lev", "lat", "lon", None),
        P("lev", "lat", "lon", None, None, None, None),
        P("lev", ("member", "lat"), "lon", None, None, None),
        P("lat", "lon", None, None, None),
        field,
        P("member"),
    )
    return jax.shard_map(local, mesh=mesh, in_specs=placed, out_specs=(field, field), check_vma=False)
```

```python
import functools
import jax
import jax.numpy as jnp
from jax import lax
from jax.experimental import pallas as pl
from jax.experimental.pallas import tpu as pltpu
from jax.sharding import PartitionSpec as P

FILTER = 2
STEPS = 2
HALO = 4
WIDTHS = (4, 4, 4, 4, 2)
LANES = 128
smoothing = 0.1
diffusion = 0.15
f32 = jnp.float32
bf16 = jnp.bfloat16
VMEM = pl.BlockSpec(memory_space=pltpu.VMEM)
SMEM = pl.BlockSpec(memory_space=pltpu.SMEM)
HBM = pl.BlockSpec(memory_space=pltpu.HBM)
NN = (((1,), (0,)), ((), ()))


def call(kernel, out_shape, in_specs, scratch=(), limit=8 << 20, aliases=None):
    many = isinstance(out_shape, (list, tuple))
    return pl.pallas_call(
        kernel,
        out_shape=out_shape,
        in_specs=in_specs,
        out_specs=[VMEM] * len(out_shape) if many else VMEM,
        scratch_shapes=list(scratch),
        input_output_aliases=aliases or {},
        compiler_params=pltpu.CompilerParams(vmem_limit_bytes=limit),
        cost_estimate=pl.CostEstimate(flops=1 << 20, bytes_accessed=1 << 20, transcendentals=0),
    )


def held(*dims, dtype=f32):
    return pltpu.VMEM(dims, dtype)


def shape(*dims):
    return jax.ShapeDtypeStruct(dims, f32)


def split(value):
    high = value.astype(bf16)
    return high, (value - high.astype(f32)).astype(bf16)


def halves(value):
    high, low = split(value)
    return jnp.concatenate(
        [jnp.concatenate([high, high], axis=1), jnp.concatenate([low, jnp.zeros_like(low)], axis=1)], axis=0
    )


def dot(left, parts, axis):
    if axis:
        height = parts.shape[0] // 2
        parts = jnp.concatenate([parts[:height, :], parts[height:, :]], axis=1)
    result = lax.dot_general(halves(left), parts, (((1,), (axis,)), ((), ())), preferred_element_type=f32)
    return result[: left.shape[0]] + result[left.shape[0] :]


def for_each(count, body, start):
    if count <= 32:
        for i in range(count):
            start = body(i, start)
        return start
    return lax.fori_loop(0, count, body, start)


def north(x):
    return pltpu.roll(x, x.shape[0] - 1, 0)


def south(x):
    return pltpu.roll(x, 1, 0)


def east(x):
    return pltpu.roll(x, x.shape[1] - 1, 1)


def west(x):
    return pltpu.roll(x, 1, 1)


def smooth(s, spread):
    for repeat in range(FILTER):
        q = spread * s
        s = s + smoothing * spread * (north(q) + south(q) + east(q) + west(q) - 4.0 * q)
    return s


def edge_block(rows):
    lane = lax.broadcasted_iota(jnp.int32, (rows.shape[0], LANES), 1)
    return jnp.where(lane < LANES // 2, rows[:, :LANES], rows[:, rows.shape[1] - LANES :])


def blend(weights, own, others, layer):
    layers = own.shape[0]
    total = None
    for i, source in enumerate([own] + list(others)):
        for m in range(layers):
            at = layer * layers * (1 + len(others)) + i * layers + m
            term = weights[at : at + 1, 0:1] * source[m]
            total = term if total is None else total + term
    return total


def parts_of(block, rows, per):
    block_row = jnp.floor((block + 0.5) / per)
    layer = jnp.floor((block_row + 0.5) / rows)
    return layer, block_row - layer * rows, block - block_row * per


def load_kernel(
    vertical, blocks, control, spread, wind_e, wind_n, scale, previous, innovation,
    platforms, counts,
    forth, back, control_v, spread_v, wind_e_v, wind_n_v, scale_v, previous_v, innovation_v,
    places, platforms_v, counts_v, lon_out, first, last, vertical_s, blocks_s, sems,
):
    pairs = (
        (spread, spread_v), (wind_e, wind_e_v), (wind_n, wind_n_v), (scale, scale_v), (blocks, blocks_s),
        (vertical, vertical_s), (control, control_v),
        (innovation, innovation_v), (previous, previous_v), (platforms, platforms_v),
        (counts, counts_v),
    )
    copies = [pltpu.make_async_copy(a, b, sems.at[i]) for i, (a, b) in enumerate(pairs)]
    for copy in copies:
        copy.start()
    layers, rows, cols = control.shape
    slots, owners = blocks.shape
    for copy in copies[:5]:
        copy.wait()
    line = lax.broadcasted_iota(jnp.int32, (1, LANES), 1)
    numbers = jnp.full((1, LANES), -1.0, f32)
    for s in range(slots):
        for o in range(owners):
            numbers = jnp.where(line == s * owners + o, blocks_s[s, o].astype(f32), numbers)
    layer, row, col = parts_of(numbers, rows, cols // LANES)
    places[...] = ((layer * (cols // LANES) + col) * (rows + 8) + row).astype(jnp.int32)
    lane = lax.broadcasted_iota(jnp.int32, (rows, LANES), 1)
    packed = jnp.zeros((rows, LANES), f32)
    fields = (spread_v, wind_e_v, wind_n_v, scale_v)
    for i, field in enumerate(fields):
        for l in range(layers):
            packed = lon_item(packed, field[l], (1 + i) * layers + l, lane)
    lon_out[:rows, :] = packed
    lon_out[rows:, :] = jnp.broadcast_to(numbers, (8, LANES))
    for out, low in ((first, True), (last, False)):
        at = WIDTHS[0] * layers
        for field, width in zip(fields, WIDTHS[1:]):
            for l in range(layers):
                begin = 0 if low else rows - width
                out[at : at + width, :] = field[l, begin : begin + width, :]
                at += width
        for c in range(0, cols, LANES):
            out[at:, c : c + LANES] = jnp.broadcast_to(numbers, (out.shape[0] - at, LANES))
    for copy in copies[5:]:
        copy.wait()
    lev, levs = lax.axis_index("lev"), lax.axis_size("lev")
    for l in range(layers):
        for shift in range(levs):
            other = lax.rem(lev + levs - shift, levs)
            for m in range(layers):
                at = (l * levs + shift) * layers + m
                a, b = lev * layers + l, other * layers + m
                forth[at : at + 1, :] = jnp.full((1, LANES), vertical_s[a, b], f32)
                back[at : at + 1, :] = jnp.full((1, LANES), vertical_s[b, a], f32)


def lon_item(packed, field, item, lane):
    cols = field.shape[1]
    tile = jnp.where(lane < LANES // 2, field[:, :LANES], field[:, cols - LANES :])
    if item:
        tile = pltpu.roll(tile, 8 * item, 1)
    return jnp.where((lane + HALO - 8 * item) % LANES < 8, tile, packed)


def pack_kernel(n_other, *refs):
    forth, control, lon_part, first, last = refs[:5]
    others = refs[5 : 5 + n_other]
    blended, lon_out, lat_1, lat_2, diag_1, diag_2 = refs[5 + n_other :]
    layers, rows, cols = control.shape
    packed = lon_part[:rows, :]
    lane = lax.broadcasted_iota(jnp.int32, (rows, LANES), 1)
    firsts, lasts = [], []
    for l in range(layers):
        value = blend(forth, control, others, l)
        blended[l] = value
        packed = lon_item(packed, value, l, lane)
        firsts.append(value[:HALO, :])
        lasts.append(value[rows - HALO :, :])
    lon_out[:rows, :] = packed
    lon_out[rows:, :] = lon_part[rows:, :]
    even = lax.axis_index("lat") % 2 == 0
    for out, diag, use_last in ((lat_1, diag_1, even), (lat_2, diag_2, jnp.logical_not(even))):
        begin = HALO * layers
        flag = jnp.where(use_last, 1, 0)
        for l in range(layers):
            chosen = jnp.full((HALO, cols), flag, jnp.int32) == 1
            out[HALO * l : HALO * (l + 1), :] = jnp.where(chosen, lasts[l], firsts[l])
        chosen = jnp.full((first.shape[0] - begin, cols), flag, jnp.int32) == 1
        out[begin:, :] = jnp.where(chosen, last[begin:, :], first[begin:, :])
        diag[...] = edge_block(out[...])


def extend_kernel(*refs):
    square, refs = refs[0], refs[1:]
    half = len(refs) // 2
    refs[-1][...] = jnp.full((1, LANES), square[0], f32)
    for field, out in zip(refs[:half], refs[half:-1]):
        layers, rows, cols = field.shape
        for l in range(layers):
            out[l, :rows, :cols] = field[l]
            out[l, rows:, :] = jnp.zeros((8, cols + LANES), f32)


def parts_kernel(matrices, out):
    count, height = matrices.shape[:2]

    def body(i, carry):
        out[i, :height, :], out[i, height:, :] = split(matrices[i])
        return carry

    for_each(count, body, 0)


def at_ends():
    lat = lax.axis_index("lat")
    return lat == 0, lat == lax.axis_size("lat") - 1


def unpack(lon_in, lat_1, lat_2, diag_1, diag_2, ext):
    layers, rows, cols = ext[0].shape[0], ext[0].shape[1] - 8, ext[0].shape[2] - LANES
    lane = lax.broadcasted_iota(jnp.int32, (rows, LANES), 1)
    keep = (lane < HALO) | (lane >= LANES - HALO)
    packed = lon_in[:rows, :]
    item = 0
    for out in ext:
        for l in range(layers):
            tile = pltpu.roll(packed, LANES - 8 * item, 1) if item else packed
            out[l, :rows, cols:] = jnp.where(keep, tile, 0.0)
            item += 1
    count = sum(WIDTHS) * layers
    for one, two, begin in ((lat_1, lat_2, 0), (diag_1, diag_2, cols)):
        width = one.shape[1]
        a, b = one[:count, :], two[:count, :]
        even = jnp.full(a.shape, lax.axis_index("lat") % 2, jnp.int32) == 0
        south_end, north_end = at_ends()
        top = jnp.full(a.shape, jnp.where(north_end, 1, 0), jnp.int32) == 0
        bottom = jnp.full(a.shape, jnp.where(south_end, 1, 0), jnp.int32) == 0
        if begin:
            lane_d = lax.broadcasted_iota(jnp.int32, a.shape, 1)
            inside = (lane_d < HALO) | (lane_d >= LANES - HALO)
            top = top & inside
            bottom = bottom & inside
        from_north = jnp.where(top, jnp.where(even, a, b), 0.0)
        from_south = jnp.where(bottom, jnp.where(even, b, a), 0.0)
        at = 0
        for out, l, w in [(e, l, w) for e, w in zip(ext, WIDTHS) for l in range(layers)]:
            out[l, rows : rows + w, begin : begin + width] = from_north[at : at + w, :]
            out[l, rows + 8 - w : rows + 8, begin : begin + width] = from_south[at : at + w, :]
            at += w


def inside_mask(ext_shape):
    south_end, north_end = at_ends()
    row = lax.broadcasted_iota(jnp.int32, ext_shape, 0)
    rows = ext_shape[0] - 8
    north_cut = jnp.where(north_end, rows, rows + 8)
    south_cut = jnp.where(south_end, rows + 4, rows + 8)
    cut = ((row >= north_cut) & (row < rows + 4)) | (row >= south_cut)
    return jnp.where(cut, 0.0, 1.0).astype(f32)


def forward_kernel(
    places, platforms, counts, mixed_in, spread_in, wind_e_in, wind_n_in, scale_in,
    lon_in, lat_1, lat_2, diag_1, diag_2, interp, innovation,
    sent, mixed, spread, wind_e, wind_n, scale,
    field, places_s, platforms_s, counts_s, sems,
):
    pairs = ((places, places_s), (platforms, platforms_s), (counts, counts_s))
    copies = [pltpu.make_async_copy(a, b, sems.at[i]) for i, (a, b) in enumerate(pairs)]
    for copy in copies:
        copy.start()
    unpack(lon_in, lat_1, lat_2, diag_1, diag_2, (mixed, spread, wind_e, wind_n, scale))
    layers, ext_rows, ext_cols = mixed.shape
    per = ext_cols // LANES - 1
    mask = inside_mask((ext_rows, ext_cols))
    for l in range(layers):
        x = scale[l] * smooth(mixed[l], spread[l])
        u, v = 0.5 * wind_e[l], 0.5 * wind_n[l]
        for step in range(STEPS):
            if step:
                x = x * mask
            e, w, n, t = east(x), west(x), north(x), south(x)
            x = (1.0 - 4.0 * diffusion) * x + diffusion * ((e + w) + (n + t)) + (u * (w - e) + v * (t - n))
        for c in range(per):
            begin = (l * per + c) * ext_rows
            field[begin : begin + ext_rows, :] = x[:, c * LANES : (c + 1) * LANES]
    for copy in copies:
        copy.wait()
    count, width = innovation.shape
    slots, owners = platforms.shape
    row = lax.broadcasted_iota(jnp.int32, (count, width), 0)

    def body(b, total):
        at = places_s[0, (b % slots) * owners + b // slots]
        left = jnp.where(row == b, jnp.broadcast_to(field[pl.ds(at, 1), :], (count, width)), 0.0)
        return total + dot(left, interp[b], 1)

    departure = for_each(count, body, jnp.zeros((count, width), f32)) - innovation[...]
    for o in range(owners):
        for s in range(slots):
            live = jnp.full((1, width), counts_s[0, o], jnp.int32) > s
            b = o * slots + s
            sent[o, s : s + 1, :] = jnp.where(live, departure[b : b + 1, :], 0.0)
            sent[o, slots + s : slots + s + 1, :] = jnp.full((1, width), platforms_s[s, o].astype(f32), f32)


def weigh_kernel(slots, arrived, matrices, out, values, platform):
    tiles = arrived.shape[0]
    for t in range(tiles):
        for s in range(slots):
            at = s * tiles + t
            values[at : at + 1, :] = arrived[t, s : s + 1, :]
            platform[at : at + 1, :] = arrived[t, slots + s : slots + s + 1, :]
    x, where = values[...], platform[...]
    total = jnp.zeros(x.shape, f32)
    for p in range(matrices.shape[0]):
        total = total + dot(jnp.where(where == float(p), x, 0.0), jnp.concatenate(split(matrices[p]), axis=0), 1)
    for t in range(tiles):
        for s in range(slots):
            at = s * tiles + t
            out[t, s : s + 1, :] = total[at : at + 1, :]


def transpose_kernel(slots, returned, interp, out):
    count, width = out.shape
    row = lax.broadcasted_iota(jnp.int32, (count, width), 0)

    def body(b, total):
        owner, slot = b // slots, b % slots
        weighted = returned[owner, pl.ds(slot, 1), :]
        left = jnp.where(
            row == slot * (count // slots) + owner, jnp.broadcast_to(weighted, (count, width)), 0.0
        )
        return total + dot(left, interp[b], 0)

    out[...] = for_each(count, body, jnp.zeros((count, width), f32))


def place_kernel(count, kinds, rows, layers, per, *refs):
    tiles, out = refs[:-1], refs[-1]
    line = lax.broadcasted_iota(jnp.int32, (1, LANES), 1)
    south_end, north_end = at_ends()
    odd = lax.axis_index("lat") % 2
    packs = -(-len(kinds) * count // LANES)
    targets = [jnp.full((1, LANES), -1.0, f32) for _ in range(packs)]
    for i, (tile, (phase, lon_step, begin)) in enumerate(zip(tiles, kinds)):
        block = tile[begin : begin + 1, :LANES]
        layer, row, col = parts_of(block, rows, per)
        valid = block >= 0.0
        if phase:
            is_north = jnp.where(odd == phase - 1, 1, 0)
            usable = jnp.where(is_north == 1, jnp.where(north_end, 0, 1), jnp.where(south_end, 0, 1))
            is_north = jnp.full((1, LANES), is_north, jnp.int32) == 1
            usable = jnp.full((1, LANES), usable, jnp.int32) == 1
            valid = valid & usable
            valid = valid & ((is_north & (row < HALO)) | (jnp.logical_not(is_north) & (row >= rows - HALO)))
            row = jnp.where(is_north, row + rows, row + 8)
        if lon_step:
            at_first, at_last = col == 0.0, col == per - 1.0
            both = at_first | at_last
            if lon_step == 1:
                both = at_first
            if lon_step == -1:
                both = at_last
            valid = valid & both
            col = jnp.where(at_first, float(per), float(per + 1))
        place = jnp.where(valid, (layer * (per + 2) + col) * (rows + 8) + row, -1.0)
        pack, shift = divmod(i * count, LANES)
        if shift:
            place = pltpu.roll(place, shift, 1)
        mine = (line >= shift) & (line < shift + count)
        targets[pack] = jnp.where(mine, place, targets[pack])
    places = out.shape[0]
    index = lax.broadcasted_iota(jnp.int32, (places, LANES), 0)
    for pack, target in enumerate(targets):
        chosen = jnp.where(index == target.astype(jnp.int32), 1.0, 0.0).astype(bf16)
        out[:, pack * LANES : (pack + 1) * LANES] = chosen
        out[:, (packs + pack) * LANES : (packs + pack + 1) * LANES] = chosen


def adjoint_kernel(n_source, *refs):
    chosen = refs[0]
    sources = refs[1 : 1 + n_source]
    spread, scale, wind_e, wind_n = refs[1 + n_source : 5 + n_source]
    filtered, = refs[5 + n_source :]
    layers, ext_rows, ext_cols = spread.shape
    rows, cols = filtered.shape[1:]
    values = [s[...] for s in sources]
    spare = chosen.shape[1] // 2 - sum(v.shape[0] for v in values)
    if spare:
        values.append(jnp.zeros((spare, LANES), f32))
    parts = jnp.concatenate(split(jnp.concatenate(values, axis=0)), axis=0)
    forcing = lax.dot_general(chosen[...], parts, NN, preferred_element_type=f32)
    mask = inside_mask((ext_rows, ext_cols))
    lane = lax.broadcasted_iota(jnp.int32, (ext_rows, LANES), 1)
    per = cols // LANES
    for l in range(layers):
        begin = l * (per + 2) * ext_rows
        tiles = [forcing[begin + c * ext_rows : begin + (c + 1) * ext_rows, :] for c in range(per + 2)]
        y = jnp.concatenate(tiles[:per] + [jnp.where(lane < LANES // 2, tiles[per], tiles[per + 1])], axis=1)
        u, v = 0.5 * wind_e[l], 0.5 * wind_n[l]
        for step in range(STEPS):
            if step:
                y = y * mask
            y = (
                (1.0 - 4.0 * diffusion) * y
                + east((diffusion + u) * y)
                + west((diffusion - u) * y)
                + north((diffusion + v) * y)
                + south((diffusion - v) * y)
            )
        s = smooth(scale[l] * y, spread[l])
        filtered[l] = s[:rows, :cols]


def gradient_kernel(n_other, *refs):
    back, control, filtered = refs[:3]
    others = refs[3 : 3 + n_other]
    gradient, partial = refs[3 + n_other :]
    layers, rows, cols = control.shape
    total = jnp.zeros((8, LANES), f32)
    for m in range(layers):
        g = control[m] + blend(back, filtered, others, m)
        gradient[m] = g
        square = g * g
        for r in range(0, rows, 8):
            for c in range(0, cols, LANES):
                total = total + square[r : r + 8, c : c + LANES]
    total = jnp.sum(total, axis=0, keepdims=True)
    partial[...] = jnp.broadcast_to(total[None], partial.shape)


def direction_kernel(cell_count, gradient_in, sums, previous, previous_square, gradient, direction):
    total = jnp.sum(jnp.sum(sums[...], axis=0), axis=1, keepdims=True)
    factor = total / cell_count / previous_square[:, 0:1]
    for l in range(gradient.shape[0]):
        gradient[l] = gradient_in[l]
        direction[l] = factor * previous[l] - gradient_in[l]


def local(
    control,
    vertical,
    spread,
    error_scale,
    wind_lon,
    wind_lat,
    obs_block,
    obs_platform,
    obs_count,
    interp,
    innovation,
    error_inverse,
    previous_direction,
    previous_square,
):
    n_lat, n_lon, n_lev = (lax.axis_size(a) for a in ("lat", "lon", "lev"))
    layers, rows, cols = control.shape
    ext_rows, ext_cols = rows + 8, cols + LANES
    owners = obs_count.shape[-1]
    slots = obs_block.shape[-1]
    width = interp.shape[-1]
    count = owners * slots
    blocks = obs_block.reshape(owners, slots).T
    platforms = obs_platform.reshape(owners, slots).T
    counts = obs_count.reshape(1, owners)
    weights = interp.reshape(count, width, width)
    limit = (8 << 20) + 3 * weights.size * 4
    per = cols // LANES
    lat_fields = sum(WIDTHS) * layers
    lat_rows = lat_fields // 8 * 8 + 8

    def from_levs(field):
        return [
            lax.ppermute(field, "lev", [(i, (i + k) % n_lev) for i in range(n_lev)]) for k in range(1, n_lev)
        ]

    def partner(a, phase):
        to = a + (1 if (a % 2 == 0) == (phase == 1) else -1)
        return to if 0 <= to < n_lat else a

    def exchange(field, phase, lon_step):
        pairs = []
        for a in range(n_lat):
            for b in range(n_lon):
                to = partner(a, phase) if phase else a
                pairs.append((a * n_lon + b, to * n_lon + (b + lon_step) % n_lon))
        return lax.ppermute(field, ("lat", "lon"), pairs)

    lon_steps = (2,) if n_lon == 2 else (1, -1)

    def from_lon(field, phase, step):
        return exchange(field, phase, 1 if step == 2 else -step)

    others = from_levs(control)
    field = held(layers, rows, cols)
    mix = held(layers * layers * n_lev, LANES)
    innovations = innovation.reshape(count, width)
    (
        forth, back, control_v, spread_v, wind_e_v, wind_n_v, scale_v, previous_v, innovation_v,
        places, platforms_v, counts_v, lon_part, first, last,
    ) = call(
        load_kernel,
        [mix, mix] + [field] * 6 + [held(count, width)]
        + [held(1, LANES, dtype=jnp.int32)]
        + [held(*x.shape, dtype=jnp.int32) for x in (platforms, counts)]
        + [held(rows + 8, LANES), held(lat_rows, cols), held(lat_rows, cols)],
        [HBM] * 11,
        [
            pltpu.SMEM(vertical.shape, f32),
            pltpu.SMEM(blocks.shape, jnp.int32),
            pltpu.SemaphoreType.DMA((11,)),
        ],
        58 << 20,
    )(
        vertical, blocks, control, spread, wind_lon, wind_lat, error_scale, previous_direction,
        innovations, platforms, counts,
    )
    blended, lon_out, lat_1, lat_2, diag_1, diag_2 = call(
        functools.partial(pack_kernel, len(others)),
        [field, held(rows + 8, LANES)] + [held(lat_rows, cols)] * 2 + [held(lat_rows, LANES)] * 2,
        [VMEM] * (5 + len(others)),
    )(forth, control_v, lon_part, first, last, *others)

    lane = jnp.arange(LANES, dtype=jnp.int32)
    lat_in = {phase: exchange(out, phase, 0) for phase, out in ((1, lat_1), (2, lat_2))}
    lon_raw = {step: from_lon(lon_out, 0, step) for step in lon_steps}
    diag_raw = {
        (phase, step): from_lon(out, phase, step)
        for phase, out in ((1, diag_1), (2, diag_2))
        for step in lon_steps
    }
    if n_lon == 2:
        lon_in = lon_raw[2]
        diag_in = {phase: diag_raw[phase, 2] for phase in (1, 2)}
    else:
        lon_in = jnp.where(lane % 8 < HALO, lon_raw[1], lon_raw[-1])
        diag_in = {
            phase: jnp.where(lane < LANES // 2, diag_raw[phase, 1], diag_raw[phase, -1]) for phase in (1, 2)
        }

    ext = held(layers, ext_rows, ext_cols)
    *exts, square_v = call(extend_kernel, [ext] * 5 + [held(1, LANES)], [SMEM] + [VMEM] * 5)(
        previous_square, blended, spread_v, wind_e_v, wind_n_v, scale_v
    )
    matrices = error_inverse.reshape(error_inverse.shape[-3:])
    weights = call(parts_kernel, held(count, 2 * width, width, dtype=bf16), [VMEM], (), limit)(weights)
    sent, _, ext_spread, ext_e, ext_n, ext_scale = call(
        forward_kernel,
        [held(owners, 2 * slots, width)] + [ext] * 5,
        [VMEM] * 15,
        [
            pltpu.VMEM((layers * ext_rows * per, LANES), f32),
            pltpu.SMEM((1, LANES), jnp.int32),
            pltpu.SMEM(blocks.shape, jnp.int32),
            pltpu.SMEM(counts.shape, jnp.int32),
            pltpu.SemaphoreType.DMA((3,)),
        ],
        limit,
        {3 + i: 1 + i for i in range(5)},
    )(
        places, platforms_v, counts_v, *exts, lon_in, lat_in[1], lat_in[2], diag_in[1], diag_in[2], weights, innovation_v,
    )

    arrived = lax.all_to_all(sent, ("lat", "lon"), split_axis=0, concat_axis=0, tiled=True)
    result = call(
        functools.partial(weigh_kernel, slots),
        held(owners, slots, width),
        [VMEM] * 2,
        [pltpu.VMEM((count, width), f32)] * 2,
    )(arrived, matrices)
    returned = lax.all_to_all(result, ("lat", "lon"), split_axis=0, concat_axis=0, tiled=True)
    adjoint_obs = call(
        functools.partial(transpose_kernel, slots), held(count, width), [VMEM] * 2, (), limit
    )(returned, weights)

    sources, tiles, kinds = [adjoint_obs], [lon_out], [(0, 0, rows)]
    for step in lon_steps:
        sources.append(from_lon(adjoint_obs, 0, step))
        tiles.append(lon_raw[step])
        kinds.append((0, step, rows))
    row_of_tiles = jnp.concatenate(sources, axis=0)
    for phase in (1, 2):
        sources.append(exchange(row_of_tiles, phase, 0))
        tiles.append(lat_in[phase])
        kinds.append((phase, 0, lat_fields))
        for step in lon_steps:
            tiles.append(diag_raw[phase, step])
            kinds.append((phase, step, lat_fields))
    depth = -(-len(kinds) * count // LANES) * LANES
    chosen = call(
        functools.partial(place_kernel, count, kinds, rows, layers, per),
        held(layers * (per + 2) * ext_rows, 2 * depth, dtype=bf16),
        [VMEM] * len(tiles),
        (),
        limit,
    )(*tiles)
    filtered = call(
        functools.partial(adjoint_kernel, len(sources)),
        held(layers, rows, cols),
        [VMEM] * (5 + len(sources)),
        (),
        limit,
    )(chosen, *sources, ext_spread, ext_scale, ext_e, ext_n)

    others = from_levs(filtered)
    group = n_lat * n_lon * n_lev
    gradient, partial = call(
        functools.partial(gradient_kernel, len(others)),
        [field, held(group, 1, LANES)],
        [VMEM] * (3 + len(others)),
    )(back, control_v, filtered, *others)
    sums = lax.all_to_all(partial, ("lat", "lon", "lev"), split_axis=0, concat_axis=0, tiled=True)
    gradient, direction = call(
        functools.partial(direction_kernel, float(control.size * group)),
        [shape(layers, rows, cols)] * 2,
        [VMEM] * 4,
    )(gradient, sums, previous_v, square_v)
    return (gradient, direction)


def solution(mesh):
    field = P("lev", ("member", "lat"), "lon")
    shared = P("lev", "lat", "lon")
    placed = (
        field,
        P(),
        shared,
        shared,
        field,
        field,
        P("lev", "lat", "lon", None, None),
        P("lev", "lat", "lon", None, None),
        P("lev", "lat", "lon", None),
        P("lev", "lat", "lon", None, None, None, None),
        P("lev", ("member", "lat"), "lon", None, None, None),
        P("lat", "lon", None, None, None),
        field,
        P("member"),
    )
    return jax.shard_map(local, mesh=mesh, in_specs=placed, out_specs=(field, field), check_vma=False)
```
